128 devices in a mesh: fsdp: 16 (over z, x), ctx: 4 (over y_hi, core), tp: 2 (over y_lo).
Axes of the slice: x: 4, y: 4 (y_hi: 2, y_lo: 2; y = y_hi * 2 + y_lo), z: 4, core: 2. Of those that a mesh axis runs over, the one named last changes fastest.
Arguments:
- tokens: bfloat16 [16384, 2048], P(('fsdp', 'ctx')), may hold values from -6 to 6
- segments: int32 [16384], P(('fsdp', 'ctx')), may hold values from 0 to 2, as said below
- attn_gain: bfloat16 [2048], P('fsdp'), may hold values from 0.5 to 1.5
- q_weight: bfloat16 [2048, 2048], P('fsdp', 'tp'), may hold values from -0.125 to 0.125
- k_weight: bfloat16 [2048, 1024], P('fsdp', 'tp'), may hold values from -0.125 to 0.125
- v_weight: bfloat16 [2048, 1024], P('fsdp', 'tp'), may hold values from -0.125 to 0.125
- q_gain: bfloat16 [128], P('fsdp'), may hold values from 0.099609375 to 1.8984375
- k_gain: bfloat16 [128], P('fsdp'), may hold values from 0.099609375 to 1.8984375
- o_weight: bfloat16 [2048, 2048], P('tp', 'fsdp'), may hold values from -1.5 to 1.5
- mlp_gain: bfloat16 [2048], P('fsdp'), may hold values from 0.5 to 1.5
- gate_weight: bfloat16 [2048, 6144], P('fsdp', 'tp'), may hold values from -0.125 to 0.125
- up_weight: bfloat16 [2048, 6144], P('fsdp', 'tp'), may hold values from -0.125 to 0.125
- down_weight: bfloat16 [6144, 2048], P('tp', 'fsdp'), may hold values from -0.078125 to 0.078125
- cotangent: bfloat16 [16384, 2048], P(('fsdp', 'ctx')), may hold values from -6 to 6
Outputs:
- output: bfloat16 [16384, 2048], P(('fsdp', 'ctx'))
- grad_tokens: float32 [16384, 2048], P(('fsdp', 'ctx'))
- grad_attn_gain: float32 [2048], P('fsdp')
- grad_q_weight: float32 [2048, 2048], P('fsdp', 'tp')
- grad_k_weight: float32 [2048, 1024], P('fsdp', 'tp')
- grad_v_weight: float32 [2048, 1024], P('fsdp', 'tp')
- grad_q_gain: float32 [128], P('fsdp')
- grad_k_gain: float32 [128], P('fsdp')
- grad_o_weight: float32 [2048, 2048], P('tp', 'fsdp')
- grad_mlp_gain: float32 [2048], P('fsdp')
- grad_gate_weight: float32 [2048, 6144], P('fsdp', 'tp')
- grad_up_weight: float32 [2048, 6144], P('fsdp', 'tp')
- grad_down_weight: float32 [6144, 2048], P('tp', 'fsdp')
The draws below stay inside these ranges and needn't reach their ends.
Inputs may be any that keep to these rules, and one draw needn't show every extreme that they name: `segments`: within each sequence of 1024 tokens the ids are 0, 1, 2 in three unbroken documents in that order; the middle one has 800 tokens and starts at a token from 64 to 160.
All inputs are finite; a program needn't handle non-finite values.
Results may differ from the reference program's by a relative error of at most 0.028.
Values may be sent and summed in bfloat16 or wider, within the bound.
A program may use at most 192 MiB of HBM per device.

```python
import jax
import jax.numpy as jnp
from jax import lax

D = 2048
QH = 16
KH = 8
HD = 128
FF = 6144
LEN = 1024
SEQS = 16
TOKENS = 16384


def draw_segments(key, part):
    key = jax.random.fold_in(key, 7)
    longest = 25 * LEN // 32
    starts = jax.random.randint(key, (SEQS,), LEN // 16, 5 * LEN // 32 + 1)
    token_index = jnp.arange(LEN, dtype=jnp.int32)
    ids_first = (token_index[None, :] >= starts[:, None]).astype(jnp.int32)
    ids_second = (token_index[None, :] >= starts[:, None] + longest).astype(jnp.int32)
    return (ids_first + ids_second).reshape(SEQS * LEN)


def steps_of(stream_key, dims, cuts, low, high):
    level, own = 1.0, jax.random.fold_in(stream_key, 6)
    for dim, shards_of in cuts:
        heights = jnp.exp(jax.random.uniform(jax.random.fold_in(own, dim), (shards_of,), jnp.float32, low / len(cuts), high / len(cuts)))
        level = level * jnp.repeat(heights, dims[dim] // shards_of).reshape([-1 if axis == dim else 1 for axis in range(len(dims))])
    return level


def noise(stream_key, extent, width, bound, pieces=(), kind=jnp.bfloat16):
    values = width * jax.random.normal(stream_key, extent, jnp.float32)
    if pieces:
        values = values * steps_of(stream_key, extent, pieces, -0.22, 0.18)
    return jnp.clip(values, -bound, bound).astype(kind)


def setup_inputs(seed: int = 0) -> dict:
    key_of = jax.random.split(jax.random.key(seed), 15)
    return {
        "tokens": noise(key_of[0], (TOKENS, D), 1.0, 6.0, ((0, 64),)),
        "segments": draw_segments(jax.random.fold_in(key_of[14], 71), 0),
        "attn_gain": jnp.clip(1.0 + 0.1 * jax.random.normal(key_of[2], (D,), jnp.float32), 0.5, 1.5).astype(jnp.bfloat16),
        "q_weight": noise(key_of[3], (D, QH * HD), D ** -0.5, 0.125, ((0, 16), (1, 2))),
        "k_weight": noise(key_of[4], (D, KH * HD), D ** -0.5, 0.125, ((0, 16), (1, 2))),
        "v_weight": noise(key_of[5], (D, KH * HD), D ** -0.5, 0.125, ((0, 16), (1, 2))),
        "q_gain": jnp.clip(1.0 + 0.18 * jax.random.normal(key_of[6], (HD,), jnp.float32), 0.099609375, 1.8984375).astype(jnp.bfloat16),
        "k_gain": jnp.clip(1.0 + 0.18 * jax.random.normal(key_of[7], (HD,), jnp.float32), 0.099609375, 1.8984375).astype(jnp.bfloat16),
        "o_weight": noise(key_of[8], (QH * HD, D), (QH * HD * 8 // LEN) ** -0.5, 1.5, ((0, 2), (1, 16))),
        "mlp_gain": jnp.clip(1.0 + 0.1 * jax.random.normal(key_of[9], (D,), jnp.float32), 0.5, 1.5).astype(jnp.bfloat16),
        "gate_weight": noise(key_of[10], (D, FF), D ** -0.5, 0.125, ((0, 16), (1, 2))),
        "up_weight": noise(key_of[11], (D, FF), D ** -0.5, 0.125, ((0, 16), (1, 2))),
        "down_weight": noise(key_of[12], (FF, D), FF ** -0.5, 0.078125, ((0, 2), (1, 16))),
        "cotangent": noise(key_of[13], (TOKENS, D), 1.0, 6.0, ((0, 64),)),
    }


epsilon = 1e-06
rope_base = 1000000.0

@jax.custom_vjp
def low(v):
    return lax.optimization_barrier(v.astype(jnp.bfloat16)).astype(jnp.float32)

@jax.custom_vjp
def low_back(v):
    return v

def low_keep(v):
    return (low(v), None)

def low_pass(kept, grad):
    return (grad,)

def back_keep(v):
    return (v, None)

def back_low(kept, grad):
    return (low(grad),)
low.defvjp(low_keep, low_pass)
low_back.defvjp(back_keep, back_low)

def matmul(left_side, right_side):
    return jnp.dot(left_side, right_side, precision=lax.Precision.HIGHEST)

def unit_rows(values_in):
    return values_in * lax.rsqrt(lax.optimization_barrier(jnp.mean(values_in * values_in, -1, keepdims=True)) + epsilon)

def rotate(values_in, cosine_table, sine_table):
    half_width = values_in.shape[-1] // 2
    first_half = values_in[..., :half_width]
    second_half = values_in[..., half_width:]
    return jnp.concatenate([first_half * cosine_table - second_half * sine_table, second_half * cosine_table + first_half * sine_table], -1)

def sequence_layer(params, hidden, seq_ids):
    attn_gain, q_weight, k_weight, v_weight, q_gain, k_gain, o_weight, mlp_gain, gate_weight, up_weight, down_weight = params
    length = hidden.shape[0]
    token_index = jnp.arange(length, dtype=jnp.int32)
    earlier = lax.optimization_barrier(jnp.sum((seq_ids[None, :] < seq_ids[:, None]).astype(jnp.int32), axis=1))
    position = token_index - earlier
    frequency = jnp.power(rope_base, -2.0 * jnp.arange(HD // 2, dtype=jnp.float32) / HD)
    angles = position.astype(jnp.float32)[:, None] * frequency[None, :]
    cosine_table = jnp.cos(angles)[:, None, :]
    sine_table = jnp.sin(angles)[:, None, :]
    normed_one = low(unit_rows(hidden) * attn_gain)
    query_proj = low_back(matmul(normed_one, q_weight)).reshape(length, QH, HD)
    key_proj = low_back(matmul(normed_one, k_weight)).reshape(length, KH, HD)
    value_rows = low(low_back(matmul(normed_one, v_weight))).reshape(length, KH, HD)
    queries = low(rotate(unit_rows(query_proj) * q_gain, cosine_table, sine_table)).reshape(length, KH, QH // KH, HD)
    key_rows = low(rotate(unit_rows(key_proj) * k_gain, cosine_table, sine_table))
    scores = low_back(jnp.einsum('ignd,jgd->gnij', queries, key_rows, precision=lax.Precision.HIGHEST) * HD ** (-0.5))
    allowed = (token_index[None, :] <= token_index[:, None]) & (seq_ids[None, :] == seq_ids[:, None])
    masked = jnp.where(allowed, scores, -jnp.inf)
    row_max = lax.optimization_barrier(jnp.max(masked, -1, keepdims=True))
    exponent = jnp.exp(masked - row_max)
    probs = exponent / lax.optimization_barrier(jnp.sum(exponent, -1, keepdims=True))
    attended = jnp.einsum('gnij,jgd->ignd', low(probs), value_rows, precision=lax.Precision.HIGHEST).reshape(length, QH * HD)
    attended = low(low_back(attended))
    middle = hidden + low_back(matmul(attended, o_weight))
    normed_two = low(unit_rows(middle) * mlp_gain)
    gate_act = low_back(matmul(normed_two, gate_weight))
    up_act = low_back(matmul(normed_two, up_weight))
    product = low(jax.nn.silu(gate_act) * up_act)
    return middle + low_back(matmul(product, down_weight))

def reference(tokens, segments, attn_gain, q_weight, k_weight, v_weight, q_gain, k_gain, o_weight, mlp_gain, gate_weight, up_weight, down_weight, cotangent):
    params = (attn_gain.astype(jnp.float32), q_weight.astype(jnp.float32), k_weight.astype(jnp.float32), v_weight.astype(jnp.float32), q_gain.astype(jnp.float32), k_gain.astype(jnp.float32), o_weight.astype(jnp.float32), mlp_gain.astype(jnp.float32), gate_weight.astype(jnp.float32), up_weight.astype(jnp.float32), down_weight.astype(jnp.float32))
    seq_ids = segments.reshape(SEQS, LEN)
    step_layer = jax.checkpoint(sequence_layer)

    def forward(hidden_all, *weights):
        hidden_seq = hidden_all.reshape(SEQS, LEN, D)
        outputs = lax.map(lambda seq_pair: step_layer(weights, seq_pair[0], seq_pair[1]), (hidden_seq, seq_ids))
        return outputs.reshape(SEQS * LEN, D)
    result, pullback = jax.vjp(forward, tokens.astype(jnp.float32), *params)
    grads = pullback(cotangent.astype(jnp.float32))
    return (result.astype(jnp.bfloat16), grads[0], grads[1], grads[2], grads[3], grads[4], grads[5], grads[6], grads[7], grads[8], grads[9], grads[10], grads[11])
```

```python
import jax
import jax.numpy as jnp
from jax import lax
from jax.sharding import PartitionSpec as P

HD = 128
COLUMN = ("ctx", "tp")


epsilon = 1e-06
rope_base = 1000000.0


def scaled_rows(values_in):
    inverse = lax.rsqrt(jnp.mean(values_in * values_in, -1, keepdims=True) + epsilon)
    return (values_in * inverse, inverse)


def norm_back(grad_in, unit_in, inverse):
    return inverse * (grad_in - unit_in * jnp.mean(grad_in * unit_in, -1, keepdims=True))


def rotate(values_in, cosine_table, sine_table, direction):
    half_width = values_in.shape[-1] // 2
    first_half = values_in[..., :half_width]
    second_half = values_in[..., half_width:]
    return jnp.concatenate(
        [
            first_half * cosine_table - direction * second_half * sine_table,
            second_half * cosine_table + direction * first_half * sine_table,
        ],
        -1,
    )


def dot_nn(left, right):
    return jnp.dot(left, right, preferred_element_type=jnp.float32)


def dot_tn(left, right):
    return lax.dot_general(
        left, right, (((0,), (0,)), ((), ())), preferred_element_type=jnp.float32
    )


def dot_nt(left, right):
    return lax.dot_general(
        left, right, (((1,), (1,)), ((), ())), preferred_element_type=jnp.float32
    )


def low(values_in):
    return values_in.astype(jnp.bfloat16)


def full(values_in):
    return values_in.astype(jnp.float32)


def per_device(
    tokens,
    segments,
    attn_gain,
    q_weight,
    k_weight,
    v_weight,
    q_gain,
    k_gain,
    o_weight,
    mlp_gain,
    gate_weight,
    up_weight,
    down_weight,
    cotangent,
):
    part = lax.axis_index("ctx")
    parts = lax.axis_size("ctx")
    half = lax.axis_index("tp")
    halves = lax.axis_size("tp")
    rows_here = tokens.shape[0]
    seq_len = rows_here * parts
    own_rows = rows_here // halves
    score_scale = HD ** (-0.5)

    def quarter(weight, dim):
        size = weight.shape[dim] // parts
        return lax.dynamic_slice_in_dim(weight, part * size, size, dim)

    def own(array):
        return lax.dynamic_slice_in_dim(array, half * own_rows, own_rows, 0)

    attn_gain_f = full(attn_gain)[:, None]
    mlp_gain_f = full(mlp_gain)[:, None]
    wq, wk, wv = quarter(q_weight, 1), quarter(k_weight, 1), quarter(v_weight, 1)
    wg, wu = quarter(gate_weight, 1), quarter(up_weight, 1)
    wo_t = quarter(o_weight, 0).T
    wd_t = quarter(down_weight, 0).T
    w_qkv = jnp.concatenate([wq, wk, wv], 1)
    w_gu = jnp.concatenate([wg, wu], 1)
    send_a = jnp.concatenate([low(full(w_qkv) * attn_gain_f), wo_t], 1)
    send_b = low(full(w_gu) * mlp_gain_f)
    full_a = lax.all_gather(send_a, "fsdp", axis=0, tiled=True)
    full_b = lax.all_gather(send_b, "fsdp", axis=0, tiled=True)
    full_c = lax.all_gather(wd_t, "fsdp", axis=0, tiled=True)
    gains = lax.all_gather(jnp.stack([q_gain, k_gain]), "fsdp", axis=1, tiled=True)
    query_gain_f, key_gain_f = full(gains[0]), full(gains[1])
    nq, nkv, nff = wq.shape[1], wk.shape[1], wg.shape[1]
    full_qkv = full_a[:, : nq + 2 * nkv]
    full_o_t = full_a[:, nq + 2 * nkv :]

    seq_ids = lax.all_gather(segments, "ctx", axis=0, tiled=True)
    index = jnp.arange(seq_len, dtype=jnp.int32)
    count_0 = jnp.sum((seq_ids == 0).astype(jnp.int32))
    count_1 = jnp.sum((seq_ids == 1).astype(jnp.int32))
    position = index - jnp.where(
        seq_ids == 0, 0, jnp.where(seq_ids == 1, count_0, count_0 + count_1)
    )
    frequency = jnp.power(rope_base, -2.0 * jnp.arange(HD // 2, dtype=jnp.float32) / HD)
    angles = position.astype(jnp.float32)[:, None] * frequency[None, :]
    cosine = jnp.cos(angles)[:, None, :]
    sine = jnp.sin(angles)[:, None, :]
    allowed = (index[None, :] <= index[:, None]) & (seq_ids[None, :] == seq_ids[:, None])

    x_here = full(tokens)
    unit_one, inverse_one = scaled_rows(x_here)
    unit_all = lax.all_gather(low(unit_one), "ctx", axis=0, tiled=True)
    grad_out_all = lax.all_gather(cotangent, "ctx", axis=0, tiled=True)
    qkv = dot_nn(unit_all, full_qkv)
    query_proj = qkv[:, :nq].reshape(seq_len, nq // HD, HD)
    key_proj = qkv[:, nq : nq + nkv].reshape(seq_len, nkv // HD, HD)
    values = low(qkv[:, nq + nkv :]).reshape(seq_len, nkv // HD, HD)
    query_unit, query_inverse = scaled_rows(query_proj)
    key_unit, key_inverse = scaled_rows(key_proj)
    group = nq // nkv
    queries = low(rotate(query_unit * query_gain_f, cosine, sine, 1.0))
    keys = low(rotate(key_unit * key_gain_f, cosine, sine, 1.0))
    query_four = queries.reshape(seq_len, nkv // HD, group, HD)
    scores = (
        jnp.einsum("ignd,jgd->gnij", query_four, keys, preferred_element_type=jnp.float32)
        * score_scale
    )
    masked = jnp.where(allowed, scores, -jnp.inf)
    exponent = jnp.exp(masked - jnp.max(masked, -1, keepdims=True))
    probs = exponent / jnp.sum(exponent, -1, keepdims=True)
    attended = low(
        jnp.einsum("gnij,jgd->ignd", low(probs), values, preferred_element_type=jnp.float32)
    ).reshape(seq_len, nq)
    attn_part = low(dot_nt(attended, full_o_t))
    attn_out = lax.psum_scatter(attn_part, COLUMN, scatter_dimension=0, tiled=True)
    middle = own(x_here) + full(attn_out)
    unit_two, inverse_two = scaled_rows(middle)
    two_all = lax.all_gather(low(unit_two), COLUMN, axis=0, tiled=True)
    gate_up = dot_nn(two_all, full_b)
    gate_act, up_act = gate_up[:, :nff], gate_up[:, nff:]
    sigmoid_gate = jax.nn.sigmoid(gate_act)
    silu_gate = gate_act * sigmoid_gate
    product = low(silu_gate * up_act)
    down_part = low(dot_nt(product, full_c))
    mlp_out = lax.psum_scatter(down_part, COLUMN, scatter_dimension=0, tiled=True)
    result = lax.all_gather(low(middle + full(mlp_out)), "tp", axis=0, tiled=True)

    grad_product = dot_nn(grad_out_all, full_c)
    grad_down_t = low(dot_tn(grad_out_all, product))
    grad_gate = low(
        grad_product * up_act * sigmoid_gate * (1.0 + gate_act * (1.0 - sigmoid_gate))
    )
    grad_up = low(grad_product * silu_gate)
    grad_gu = jnp.concatenate([grad_gate, grad_up], 1)
    grad_two_part = low(dot_nt(grad_gu, full_b))
    grad_gu_w = low(dot_tn(two_all, grad_gu))
    grad_two = lax.psum_scatter(grad_two_part, COLUMN, scatter_dimension=0, tiled=True)
    grad_middle = full(own(cotangent)) + norm_back(full(grad_two), unit_two, inverse_two)
    grad_mid_all = lax.all_gather(low(grad_middle), COLUMN, axis=0, tiled=True)
    grad_o_t = low(dot_tn(grad_mid_all, attended))
    grad_attended = low(dot_nn(grad_mid_all, full_o_t))
    grad_four = grad_attended.reshape(seq_len, nkv // HD, group, HD)
    grad_probs = jnp.einsum(
        "ignd,jgd->gnij", grad_four, values, preferred_element_type=jnp.float32
    )
    row_dot = jnp.sum(probs * grad_probs, -1, keepdims=True)
    grad_scores = low(probs * (grad_probs - row_dot))
    grad_queries = (
        jnp.einsum("gnij,jgd->ignd", grad_scores, keys, preferred_element_type=jnp.float32)
        * score_scale
    )
    grad_keys = (
        jnp.einsum("gnij,ignd->jgd", grad_scores, query_four, preferred_element_type=jnp.float32)
        * score_scale
    )
    grad_values = jnp.einsum(
        "gnij,ignd->jgd", low(probs), grad_four, preferred_element_type=jnp.float32
    )
    query_back = rotate(grad_queries.reshape(seq_len, nq // HD, HD), cosine, sine, -1.0)
    grad_qg_part = jnp.sum(query_back * query_unit, (0, 1))
    grad_q_proj = low(norm_back(query_back * query_gain_f, query_unit, query_inverse))
    key_back = rotate(grad_keys, cosine, sine, -1.0)
    grad_kg_part = jnp.sum(key_back * key_unit, (0, 1))
    grad_k_proj = low(norm_back(key_back * key_gain_f, key_unit, key_inverse))
    grad_qkv = jnp.concatenate(
        [
            grad_q_proj.reshape(seq_len, nq),
            grad_k_proj.reshape(seq_len, nkv),
            low(grad_values).reshape(seq_len, nkv),
        ],
        1,
    )
    grad_one_part = low(dot_nt(grad_qkv, full_qkv))
    grad_qkv_w = low(dot_tn(unit_all, grad_qkv))
    grad_one = lax.psum_scatter(grad_one_part, COLUMN, scatter_dimension=0, tiled=True)
    grad_input = grad_middle + norm_back(full(grad_one), own(unit_one), own(inverse_one))
    grad_input = lax.all_gather(grad_input, "tp", axis=0, tiled=True)

    def scatter(grad):
        return lax.psum_scatter(grad, "fsdp", scatter_dimension=0, tiled=True)

    sum_d_t = scatter(grad_down_t)
    sum_gu = scatter(grad_gu_w)
    sum_o_t = scatter(grad_o_t)
    sum_qkv = scatter(grad_qkv_w)
    part_ag = jnp.sum(full(sum_qkv) * full(w_qkv), 1)
    part_mg = jnp.sum(full(sum_gu) * full(w_gu), 1)
    sum_gains = lax.psum(jnp.concatenate([part_ag, part_mg]), COLUMN)
    sum_qk = lax.psum(
        jnp.concatenate([grad_qg_part, grad_kg_part]), ("fsdp", "ctx", "tp")
    ).reshape(2, HD)
    sum_qk = lax.dynamic_slice_in_dim(
        sum_qk, lax.axis_index("fsdp") * q_gain.shape[0], q_gain.shape[0], 1
    )
    own_qkv = low(full(sum_qkv) * attn_gain_f)
    own_gu = low(full(sum_gu) * mlp_gain_f)
    owned = jnp.concatenate([own_qkv, sum_o_t, own_gu, sum_d_t], 1)
    owned = lax.all_gather(owned, "ctx", axis=0, tiled=False)
    rows_w = q_weight.shape[0]

    def columns(start, size):
        piece = owned[:, :, start : start + size]
        return full(jnp.swapaxes(piece, 0, 1).reshape(rows_w, parts * size))

    def rows(start, size):
        piece = owned[:, :, start : start + size]
        return full(jnp.swapaxes(piece, 1, 2).reshape(parts * size, rows_w))

    spots = [0]
    for size in (nq, nkv, nkv, nq, nff, nff, nff):
        spots.append(spots[-1] + size)
    return (
        result,
        grad_input,
        sum_gains[:rows_w],
        columns(spots[0], nq),
        columns(spots[1], nkv),
        columns(spots[2], nkv),
        sum_qk[0],
        sum_qk[1],
        rows(spots[3], nq),
        sum_gains[rows_w:],
        columns(spots[4], nff),
        columns(spots[5], nff),
        rows(spots[6], nff),
    )


def solution(mesh):
    weight = P("fsdp", "tp")
    turned = P("tp", "fsdp")
    acts = P(("fsdp", "ctx"), None)
    gain = P("fsdp")
    return jax.shard_map(
        per_device,
        mesh=mesh,
        in_specs=(
            acts,
            P(("fsdp", "ctx")),
            gain,
            weight,
            weight,
            weight,
            gain,
            gain,
            turned,
            gain,
            weight,
            weight,
            turned,
            acts,
        ),
        out_specs=(
            acts,
            acts,
            gain,
            weight,
            weight,
            weight,
            gain,
            gain,
            turned,
            gain,
            weight,
            weight,
            turned,
        ),
        check_vma=False,
    )
```

```python
import functools

import jax
import jax.numpy as jnp
from jax import lax
from jax.experimental import pallas as pl
from jax.experimental.pallas import tpu as pltpu
from jax.sharding import PartitionSpec as P

HD = 128
MESH = pl.DeviceIdType.MESH
HBM = pl.BlockSpec(memory_space=pl.ANY)
VMEM = pl.BlockSpec(memory_space=pltpu.VMEM)
LOW = jnp.bfloat16
WIDE = jnp.float32


epsilon = 1e-06
rope_base = 1000000.0


def scaled_rows(values_in):
    inverse = lax.rsqrt(jnp.mean(values_in * values_in, -1, keepdims=True) + epsilon)
    return (values_in * inverse, inverse)


def norm_back(grad_in, unit_in, inverse):
    return inverse * (grad_in - unit_in * jnp.mean(grad_in * unit_in, -1, keepdims=True))


def rotate(values_in, cosine_table, sine_table, direction):
    half_width = values_in.shape[-1] // 2
    first_half = values_in[..., :half_width]
    second_half = values_in[..., half_width:]
    return jnp.concatenate(
        [
            first_half * cosine_table - direction * second_half * sine_table,
            second_half * cosine_table + direction * first_half * sine_table,
        ],
        -1,
    )


def dot_nn(left, right):
    return jnp.dot(left, right, preferred_element_type=WIDE)


def dot_tn(left, right):
    return lax.dot_general(left, right, (((0,), (0,)), ((), ())), preferred_element_type=WIDE)


def dot_nt(left, right):
    return lax.dot_general(left, right, (((1,), (1,)), ((), ())), preferred_element_type=WIDE)


def low(values_in):
    return values_in.astype(LOW)


def full(values_in):
    return values_in.astype(WIDE)


def place():
    plane = lax.axis_index("fsdp")
    part = lax.axis_index("ctx")
    half = lax.axis_index("tp")
    return {
        "z": lax.div(plane, 4),
        "x": lax.rem(plane, 4),
        "y": lax.div(part, 2) * 2 + half,
        "core": lax.rem(part, 2),
    }


def device(where):
    return (
        where["z"] * 4 + where["x"],
        lax.div(where["y"], 2) * 2 + where["core"],
        lax.rem(where["y"], 2),
    )


def moved(here, axis, step):
    there = dict(here)
    if axis == "pair":
        there["y"] = here["y"] + 1 - 2 * lax.rem(here["y"], 2)
    elif axis == "core":
        there["core"] = 1 - here["core"]
    else:
        there[axis] = lax.rem(here[axis] + step, 4)
    return there


def block_of(y, core):
    return lax.div(y, 2) * 4 + core * 2 + lax.rem(y, 2)


class Links:
    def __init__(self, send_sems, recv_sems):
        self.here = place()
        self.send_sems, self.recv_sems = send_sems, recv_sems
        self.started = []

    def meet(self, peers):
        barrier = pltpu.get_barrier_semaphore()
        for axis, step in peers:
            pl.semaphore_signal(
                barrier,
                inc=1,
                device_id=device(moved(self.here, axis, step)),
                device_id_type=MESH,
            )
        pl.semaphore_wait(barrier, len(peers))

    def send(self, src, dst, axis, step=0):
        spot = len(self.started)
        copy = pltpu.make_async_remote_copy(
            src_ref=src,
            dst_ref=dst,
            send_sem=self.send_sems.at[spot],
            recv_sem=self.recv_sems.at[spot],
            device_id=device(moved(self.here, axis, step)),
            device_id_type=MESH,
        )
        copy.start()
        self.started.append(copy)
        return copy

    def drain(self):
        for copy in self.started:
            copy.wait_send()


PLANE = [("x", 1), ("x", 2), ("x", 3), ("z", 1), ("z", 2), ("z", 3)]
COLUMN = [("y", 1), ("y", 2), ("y", 3), ("core", 0)]


def together(jobs):
    jobs = list(jobs)
    while jobs:
        left = []
        for job in jobs:
            try:
                next(job)
                left.append(job)
            except StopIteration:
                pass
        jobs = left


def each(count, step, body):
    def one(i, carry):
        body(pl.ds(pl.multiple_of(i * step, step), step))
        return carry

    lax.fori_loop(0, count // step, one, 0)


def add_rows(into, first, second):
    lead, rows = into.shape[:-2], into.shape[-2]

    def add(spot):
        def body(window):
            spots = spot + (window,)
            into[spots] = low(full(first[spots]) + full(second[spots]))

        return body

    if not lead:
        each(rows, 16, add(()))
    else:
        for i in range(lead[0]):
            each(rows, 16, add((i,)))


def gather4(links, axis, own, block, arrived=None):
    me = links.here[axis]
    before, after, far = lax.rem(me + 3, 4), lax.rem(me + 1, 4), lax.rem(me + 2, 4)
    arrived = arrived or (lambda spot, side: None)
    up, down = {}, {}
    up[0] = links.send(own(0), block(me, 0), axis, 1)
    down[1] = links.send(own(1), block(me, 1), axis, 3)
    up[1] = links.send(own(1), block(me, 1), axis, 1)
    down[0] = links.send(own(0), block(me, 0), axis, 3)
    yield
    up[0].wait_recv()
    up_far = links.send(block(before, 0), block(before, 0), axis, 1)
    arrived(before, 0)
    down[1].wait_recv()
    down_far = links.send(block(after, 1), block(after, 1), axis, 3)
    arrived(after, 1)
    yield
    up[1].wait_recv()
    arrived(before, 1)
    down[0].wait_recv()
    arrived(after, 0)
    yield
    up_far.wait_recv()
    arrived(far, 0)
    down_far.wait_recv()
    arrived(far, 1)


def scatter4(links, axis, mine, near, far):
    me = links.here[axis]
    before, after, beyond = lax.rem(me + 3, 4), lax.rem(me + 1, 4), lax.rem(me + 2, 4)
    up_far = links.send(mine(beyond, 0), far[0], axis, 1)
    down_far = links.send(mine(beyond, 1), far[1], axis, 3)
    up_one = links.send(mine(after, 1), near[0](1), axis, 1)
    down_one = links.send(mine(before, 0), near[1](0), axis, 3)
    yield
    up_far.wait_recv()
    add_rows(far[0], far[0], mine(after, 0))
    up_two = links.send(far[0], near[0](0), axis, 1)
    down_far.wait_recv()
    add_rows(far[1], far[1], mine(before, 1))
    down_two = links.send(far[1], near[1](1), axis, 3)
    yield
    up_one.wait_recv()
    down_one.wait_recv()
    yield
    up_two.wait_recv()
    down_two.wait_recv()


def column_gather(links, own_ref, out):
    here = links.here
    rows = out.shape[1] // 2
    shared = []

    def own(h):
        return own_ref.at[pl.ds(h * rows, rows)]

    def block(p, h):
        return out.at[block_of(p, here["core"]), pl.ds(h * rows, rows)]

    def arrived(p, h):
        shared.append(links.send(block(p, h), block(p, h), "core"))

    ring = gather4(links, "y", own, block, arrived)
    next(ring)
    for h in range(2):
        shared.append(links.send(own(h), block(here["y"], h), "core"))
    yield
    for _ in ring:
        yield
    yield
    for copy in shared:
        copy.wait_recv()


def column_scatter(links, partial, passed, near, far, done):
    here = links.here
    rows = partial.shape[1] // 2
    core = here["core"]
    me = here["y"]
    order = [lax.rem(me + step, 4) for step in (2, 1, 3, 0)]
    over = [
        links.send(partial.at[block_of(p, 1 - core)], passed.at[p], "core") for p in order
    ]
    yield
    for copy, p in zip(over[:3], order[:3]):
        copy.wait_recv()
        add_rows(passed.at[p], passed.at[p], partial.at[block_of(p, core)])
    ring = scatter4(
        links,
        "y",
        lambda p, h: passed.at[p, pl.ds(h * rows, rows)],
        [lambda h, i=i: near.at[i, pl.ds(h * rows, rows)] for i in range(2)],
        [far.at[0], far.at[1]],
    )
    for _ in ring:
        yield
    over[3].wait_recv()
    own = partial.at[block_of(me, core)]
    mine = passed.at[me]

    def body(window):
        done(
            window,
            (full(own[window]) + full(mine[window]))
            + (full(near[0, window]) + full(near[1, window])),
        )

    each(2 * rows, 16, body)


def plane_gather(links, own_ref, out, local_sem):
    here = links.here
    z, x = here["z"], here["x"]
    width = own_ref.shape[1] // 2
    rows = own_ref.shape[0] // 2
    kept = pltpu.make_async_copy(own_ref, out.at[z, x], local_sem)
    kept.start()
    sides = [pl.ds(0, width), pl.ds(width, width)]

    def own(side):
        return lambda h: own_ref.at[pl.ds(h * rows, rows), side]

    first = [
        gather4(
            links, "x", own(sides[0]), lambda p, h: out.at[z, p, pl.ds(h * rows, rows), sides[0]]
        ),
        gather4(
            links, "z", own(sides[1]), lambda p, h: out.at[p, x, pl.ds(h * rows, rows), sides[1]]
        ),
    ]
    for _ in zip(*first):
        yield
    together(first)
    kept.wait()

    def by_z(p, h):
        return out.at[p, pl.ds(2 * h, 2), :, sides[0]]

    def by_x(p, h):
        return out.at[pl.ds(2 * h, 2), p, :, sides[1]]

    second = [
        gather4(links, "z", lambda h: by_z(z, h), by_z),
        gather4(links, "x", lambda h: by_x(x, h), by_x),
    ]
    for _ in zip(*second):
        yield
    together(second)


def plane_scratch(width):
    half = width // 2
    return [
        pltpu.VMEM((2, 2, 4, 128, half), LOW),
        pltpu.VMEM((2, 2, 2, 128, half), LOW),
        pltpu.VMEM((2, 4, 128, half), LOW),
        pltpu.VMEM((2, 2, 128, half), LOW),
        pltpu.VMEM((2, 2, 64, half), LOW),
    ]


def plane_scatter(links, grad, out, near, far, middle, near_two, far_two):
    here = links.here
    z, x = here["z"], here["x"]
    half = out.shape[1] // 2
    sides = [pl.ds(0, half), pl.ds(half, half)]
    first = [
        scatter4(
            links,
            "x",
            lambda p, h: grad.at[pl.ds(2 * h, 2), p, :, sides[0]],
            [lambda h, i=i: near.at[0, i, pl.ds(2 * h, 2)] for i in range(2)],
            [far.at[0, 0], far.at[0, 1]],
        ),
        scatter4(
            links,
            "z",
            lambda p, h: grad.at[p, pl.ds(2 * h, 2), :, sides[1]],
            [lambda h, i=i: near.at[1, i, pl.ds(2 * h, 2)] for i in range(2)],
            [far.at[1, 0], far.at[1, 1]],
        ),
    ]
    for _ in zip(*first):
        yield
    together(first)
    for s in range(2):
        for p in range(4):
            own = grad.at[p, x, :, sides[0]] if s == 0 else grad.at[z, p, :, sides[1]]

            def body(window, s=s, p=p, own=own):
                middle[s, p, window] = low(
                    full(own[window])
                    + (full(near[s, 0, p, window]) + full(near[s, 1, p, window]))
                )

            each(128, 16, body)
    second = [
        scatter4(
            links,
            axis,
            lambda p, h, s=s: middle.at[s, p, pl.ds(h * 64, 64)],
            [lambda h, s=s, i=i: near_two.at[s, i, pl.ds(h * 64, 64)] for i in range(2)],
            [far_two.at[s, 0], far_two.at[s, 1]],
        )
        for s, axis in enumerate(("z", "x"))
    ]
    for _ in zip(*second):
        yield
    together(second)
    for s, me in enumerate((z, x)):

        def body(window, s=s, me=me):
            out[window, sides[s]] = low(
                full(middle[s, me, window])
                + (full(near_two[s, 0, window]) + full(near_two[s, 1, window]))
            )

        each(128, 16, body)


def column_scratch():
    return [
        pltpu.VMEM((4, 128, 2048), LOW),
        pltpu.VMEM((2, 128, 2048), LOW),
        pltpu.VMEM((2, 64, 2048), LOW),
    ]


def small_plane(links, own, out):
    z, x = links.here["z"], links.here["x"]
    out[z, x] = own[...]
    copies = [links.send(own, out.at[z, x], "x", step) for step in (1, 2, 3)]
    yield
    for copy in copies:
        copy.wait_recv()
    copies = [links.send(out.at[z], out.at[z], "z", step) for step in (1, 2, 3)]
    yield
    for copy in copies:
        copy.wait_recv()


def small_column(links, own, out):
    core, y = links.here["core"], links.here["y"]
    out[core, y] = own[...]
    copies = [links.send(own, out.at[core, y], "y", step) for step in (1, 2, 3)]
    yield
    for copy in copies:
        copy.wait_recv()
    copy = links.send(out.at[core], out.at[core], "core")
    yield
    copy.wait_recv()


def call(kernel, name, number, copies, outs, out_specs, in_specs, scratch, vmem, operands):
    return pl.pallas_call(
        kernel,
        name=name,
        out_shape=outs,
        in_specs=in_specs,
        out_specs=out_specs,
        scratch_shapes=[pltpu.SemaphoreType.DMA((copies,)), pltpu.SemaphoreType.DMA((copies,))]
        + scratch,
        compiler_params=pltpu.CompilerParams(
            collective_id=number, has_side_effects=True, vmem_limit_bytes=vmem * 2**20
        ),
    )(*operands)


def shaped(shape, kind=LOW):
    return jax.ShapeDtypeStruct(shape, kind)


def front_kernel(
    own_a, unit_own, gains, seq, full_a, unit_all, gains_all, seq_all, send_sems, recv_sems, kept
):
    links = Links(send_sems, recv_sems)
    links.meet(PLANE + COLUMN)
    together(
        [
            small_plane(links, gains, gains_all),
            small_column(links, seq, seq_all),
            plane_gather(links, own_a, full_a, kept.at[0]),
            column_gather(links, unit_own, unit_all),
        ]
    )
    own = pltpu.make_async_copy(
        unit_own, unit_all.at[block_of(links.here["y"], links.here["core"])], kept.at[1]
    )
    own.start()
    own.wait()
    links.drain()


def turn_kernel(
    partial,
    x_own,
    own_b,
    own_c,
    dy_own,
    two_all,
    middle,
    full_b,
    full_c,
    dy_all,
    send_sems,
    recv_sems,
    kept,
    passed,
    near,
    far,
):
    links = Links(send_sems, recv_sems)
    links.meet(PLANE + COLUMN)
    spot = block_of(links.here["y"], links.here["core"])
    own_dy = pltpu.make_async_copy(dy_own, dy_all.at[spot], kept.at[2])
    own_dy.start()

    def done(window, total):
        value = full(x_own[window]) + total
        middle[window] = value
        two_all[spot, window] = low(scaled_rows(value)[0])

    def turn():
        yield from column_scatter(links, partial, passed, near, far, done)
        yield from column_gather(links, two_all.at[spot], two_all)
        yield from column_gather(links, dy_own, dy_all)

    def weights():
        yield from plane_gather(links, own_b, full_b, kept.at[0])
        yield from plane_gather(links, own_c, full_c, kept.at[1])

    together([turn(), weights()])
    own_dy.wait()
    links.drain()


def back_kernel(
    partial,
    down_part,
    grad_gu,
    grad_d,
    middle,
    dy_own,
    mid_all,
    grad_mid,
    result,
    sum_gu,
    sum_d,
    send_sems,
    recv_sems,
    passed,
    near,
    far,
    passed_two,
    near_two,
    far_two,
    *scratch,
):
    links = Links(send_sems, recv_sems)
    links.meet(PLANE + COLUMN)
    spot = block_of(links.here["y"], links.here["core"])

    def done(window, total):
        unit, inverse = scaled_rows(middle[window])
        value = full(dy_own[window]) + norm_back(total, unit, inverse)
        grad_mid[window] = value
        mid_all[spot, window] = low(value)

    def done_two(window, total):
        result[window] = low(middle[window] + total)

    def turn():
        yield from column_scatter(links, partial, passed, near, far, done)
        yield from column_gather(links, mid_all.at[spot], mid_all)
        yield from column_scatter(links, down_part, passed_two, near_two, far_two, done_two)

    together(
        [
            turn(),
            plane_scatter(links, grad_gu, sum_gu, *scratch[:5]),
            plane_scatter(links, grad_d, sum_d, *scratch[5:]),
        ]
    )
    links.drain()


def end_kernel(
    partial,
    grad_qkv,
    grad_o,
    sum_gu,
    sum_d,
    w_qkv,
    w_gu,
    gain_one,
    gain_two,
    grad_mid,
    x_own,
    result,
    small,
    grad_x,
    out_rows,
    all_qkv,
    all_o,
    all_gu,
    all_d,
    sums,
    send_sems,
    recv_sems,
    gains_all,
    column_all,
    row,
    turned,
    sum_qkv,
    passed,
    near,
    far,
    *scratch,
):
    links = Links(send_sems, recv_sems)
    links.meet(PLANE + COLUMN)
    here = links.here
    y, core = here["y"], here["core"]
    half = lax.rem(y, 2)
    part = lax.div(y, 2) * 2 + core
    other = lax.rem(y + 2, 4)
    part_other = lax.div(other, 2) * 2 + core

    def share(out):
        across = links.send(out.at[part], out.at[part], "y", 2)
        beside = links.send(out.at[part], out.at[part], "core")
        yield
        across.wait_recv()
        second = links.send(out.at[part_other], out.at[part_other], "core")
        yield
        beside.wait_recv()
        second.wait_recv()

    def exchange(ref):
        copy = links.send(ref.at[half], ref.at[half], "pair")
        yield
        copy.wait_recv()

    def scale_gu(window):
        all_gu[part, window] = low(full(sum_gu[window]) * gain_two[window])
        part_sum = jnp.sum(full(sum_gu[window]) * full(w_gu[window]), 1, keepdims=True)
        turned[1, window] = jnp.broadcast_to(part_sum, (16, 128))

    def scale_qkv(window):
        all_qkv[part, window] = low(full(sum_qkv[window]) * gain_one[window])
        part_sum = jnp.sum(full(sum_qkv[window]) * full(w_qkv[window]), 1, keepdims=True)
        turned[0, window] = jnp.broadcast_to(part_sum, (16, 128))

    def done(window, total):
        unit, inverse = scaled_rows(full(x_own[window]))
        grad_x[half, window] = low(grad_mid[window] + norm_back(total, unit, inverse))

    def rows_job():
        yield from column_scatter(links, partial, passed, near, far, done)
        yield from exchange(grad_x)

    def early():
        out_rows[half] = result[...]
        all_d[part] = sum_d[...]
        each(128, 16, scale_gu)
        yield
        yield from exchange(out_rows)
        yield from share(all_gu)
        yield from share(all_d)

    def late():
        yield from plane_scatter(links, grad_qkv, sum_qkv, *scratch[:5])
        each(128, 16, scale_qkv)
        row[0:2] = jnp.sum(gains_all[:, :, 0:2], (0, 1))
        row[2:3] = turned[0].T[0:1]
        row[3:4] = turned[1].T[0:1]
        row[4:8] = jnp.zeros((4, 128), WIDE)
        yield from share(all_qkv)
        yield from small_column(links, row, column_all)

    def late_o():
        yield from plane_scatter(links, grad_o, all_o.at[part], *scratch[5:])
        yield from share(all_o)

    together([late(), late_o(), rows_job(), early(), small_plane(links, small, gains_all)])
    sums[...] = jnp.sum(column_all[...], (0, 1))
    links.drain()


def per_device(
    tokens,
    segments,
    attn_gain,
    q_weight,
    k_weight,
    v_weight,
    q_gain,
    k_gain,
    o_weight,
    mlp_gain,
    gate_weight,
    up_weight,
    down_weight,
    cotangent,
):
    part = lax.axis_index("ctx")
    parts = lax.axis_size("ctx")
    half = lax.axis_index("tp")
    halves = lax.axis_size("tp")
    rows_here, width = tokens.shape
    seq_len = rows_here * parts
    own_rows = rows_here // halves
    blocks = parts * halves
    score_scale = HD ** (-0.5)

    def quarter(weight, dim):
        size = weight.shape[dim] // parts
        return lax.dynamic_slice_in_dim(weight, part * size, size, dim)

    def own(array):
        return lax.dynamic_slice_in_dim(array, half * own_rows, own_rows, 0)

    attn_gain_f = full(attn_gain)[:, None]
    mlp_gain_f = full(mlp_gain)[:, None]
    wq, wk, wv = quarter(q_weight, 1), quarter(k_weight, 1), quarter(v_weight, 1)
    wg, wu = quarter(gate_weight, 1), quarter(up_weight, 1)
    wo_t = quarter(o_weight, 0).T
    wd_t = quarter(down_weight, 0).T
    w_qkv = jnp.concatenate([wq, wk, wv], 1)
    w_gu = jnp.concatenate([wg, wu], 1)
    nq, nkv, nff = wq.shape[1], wk.shape[1], wg.shape[1]
    rows_w = q_weight.shape[0]
    na, nb, nc = 2 * nq + 2 * nkv, 2 * nff, nff
    send_a = jnp.concatenate([low(full(w_qkv) * attn_gain_f), wo_t], 1)
    send_b = low(full(w_gu) * mlp_gain_f)
    x_own = own(tokens)
    dy_own = own(cotangent)
    unit_own = low(scaled_rows(full(x_own))[0])
    few = q_gain.shape[0]
    gains_own = jnp.zeros((8, 128), WIDE).at[0, :few].set(full(q_gain)).at[1, :few].set(full(k_gain))
    seq_own = jnp.broadcast_to(own(segments)[None, :], (8, 128))

    full_a, unit_all, gains_all, seq_all = call(
        front_kernel,
        "front",
        0,
        64,
        (
            shaped((4, 4, rows_w, na)),
            shaped((blocks, own_rows, width)),
            shaped((4, 4, 8, 128), WIDE),
            shaped((2, 4, 8, 128), jnp.int32),
        ),
        [HBM, HBM, VMEM, VMEM],
        [HBM, HBM, VMEM, VMEM],
        [pltpu.SemaphoreType.DMA((2,))],
        40,
        (send_a, unit_own, gains_own, seq_own),
    )
    full_a = full_a.reshape(16 * rows_w, na)
    unit_all = unit_all.reshape(seq_len, width)
    query_gain_f = gains_all[:, :, 0, :few].reshape(HD)
    key_gain_f = gains_all[:, :, 1, :few].reshape(HD)
    seq_ids = jnp.swapaxes(seq_all[:, :, 0].reshape(2, 2, 2, 128), 0, 1).reshape(seq_len)
    full_qkv = full_a[:, : nq + 2 * nkv]
    full_o_t = full_a[:, nq + 2 * nkv :]

    index = jnp.arange(seq_len, dtype=jnp.int32)
    count_0 = jnp.sum((seq_ids == 0).astype(jnp.int32))
    count_1 = jnp.sum((seq_ids == 1).astype(jnp.int32))
    position = index - jnp.where(
        seq_ids == 0, 0, jnp.where(seq_ids == 1, count_0, count_0 + count_1)
    )
    frequency = jnp.power(rope_base, -2.0 * jnp.arange(HD // 2, dtype=WIDE) / HD)
    angles = position.astype(WIDE)[:, None] * frequency[None, :]
    cosine = jnp.cos(angles)[:, None, :]
    sine = jnp.sin(angles)[:, None, :]
    allowed = (index[None, :] <= index[:, None]) & (seq_ids[None, :] == seq_ids[:, None])

    qkv = dot_nn(unit_all, full_qkv)
    query_proj = qkv[:, :nq].reshape(seq_len, nq // HD, HD)
    key_proj = qkv[:, nq : nq + nkv].reshape(seq_len, nkv // HD, HD)
    values = low(qkv[:, nq + nkv :]).reshape(seq_len, nkv // HD, HD)
    query_unit, query_inverse = scaled_rows(query_proj)
    key_unit, key_inverse = scaled_rows(key_proj)
    group = nq // nkv
    queries = low(rotate(query_unit * query_gain_f, cosine, sine, 1.0))
    keys = low(rotate(key_unit * key_gain_f, cosine, sine, 1.0))
    query_four = queries.reshape(seq_len, nkv // HD, group, HD)
    scores = (
        jnp.einsum("ignd,jgd->gnij", query_four, keys, preferred_element_type=WIDE) * score_scale
    )
    masked = jnp.where(allowed, scores, -jnp.inf)
    exponent = jnp.exp(masked - jnp.max(masked, -1, keepdims=True))
    probs = exponent / jnp.sum(exponent, -1, keepdims=True)
    attended = low(
        jnp.einsum("gnij,jgd->ignd", low(probs), values, preferred_element_type=WIDE)
    ).reshape(seq_len, nq)
    attn_part = low(dot_nt(attended, full_o_t)).reshape(blocks, own_rows, width)

    two_all, middle, full_b, full_c, dy_all = call(
        turn_kernel,
        "turn",
        1,
        96,
        (
            shaped((blocks, own_rows, width)),
            shaped((own_rows, width), WIDE),
            shaped((4, 4, rows_w, nb)),
            shaped((4, 4, rows_w, nc)),
            shaped((blocks, own_rows, width)),
        ),
        [VMEM, VMEM, HBM, HBM, HBM],
        [VMEM, VMEM, HBM, HBM, HBM],
        [pltpu.SemaphoreType.DMA((3,))] + column_scratch(),
        40,
        (attn_part, x_own, send_b, wd_t, dy_own),
    )
    two_all = two_all.reshape(seq_len, width)
    dy_all = dy_all.reshape(seq_len, width)
    full_b = full_b.reshape(16 * rows_w, nb)
    full_c = full_c.reshape(16 * rows_w, nc)

    gate_up = dot_nn(two_all, full_b)
    gate_act, up_act = gate_up[:, :nff], gate_up[:, nff:]
    sigmoid_gate = jax.nn.sigmoid(gate_act)
    silu_gate = gate_act * sigmoid_gate
    product = low(silu_gate * up_act)
    down_part = low(dot_nt(product, full_c)).reshape(blocks, own_rows, width)
    grad_product = dot_nn(dy_all, full_c)
    grad_d = low(dot_tn(dy_all, product))
    grad_gate = low(
        grad_product * up_act * sigmoid_gate * (1.0 + gate_act * (1.0 - sigmoid_gate))
    )
    grad_up = low(grad_product * silu_gate)
    grad_gu = jnp.concatenate([grad_gate, grad_up], 1)
    grad_two_part = low(dot_nt(grad_gu, full_b)).reshape(blocks, own_rows, width)
    grad_gu_w = low(dot_tn(two_all, grad_gu))

    mid_all, grad_mid, result, sum_gu, sum_d = call(
        back_kernel,
        "back",
        2,
        112,
        (
            shaped((blocks, own_rows, width)),
            shaped((own_rows, width), WIDE),
            shaped((own_rows, width)),
            shaped((rows_w, nb)),
            shaped((rows_w, nc)),
        ),
        [VMEM] * 5,
        [VMEM] * 6,
        column_scratch() + column_scratch() + plane_scratch(nb) + plane_scratch(nc),
        60,
        (
            grad_two_part,
            down_part,
            grad_gu_w.reshape(4, 4, rows_w, nb),
            grad_d.reshape(4, 4, rows_w, nc),
            middle,
            dy_own,
        ),
    )
    mid_all = mid_all.reshape(seq_len, width)

    grad_o_t = low(dot_tn(mid_all, attended))
    grad_attended = low(dot_nn(mid_all, full_o_t))
    grad_four = grad_attended.reshape(seq_len, nkv // HD, group, HD)
    grad_probs = jnp.einsum("ignd,jgd->gnij", grad_four, values, preferred_element_type=WIDE)
    row_dot = jnp.sum(probs * grad_probs, -1, keepdims=True)
    grad_scores = low(probs * (grad_probs - row_dot))
    grad_queries = (
        jnp.einsum("gnij,jgd->ignd", grad_scores, keys, preferred_element_type=WIDE) * score_scale
    )
    grad_keys = (
        jnp.einsum("gnij,ignd->jgd", grad_scores, query_four, preferred_element_type=WIDE)
        * score_scale
    )
    grad_values = jnp.einsum("gnij,ignd->jgd", low(probs), grad_four, preferred_element_type=WIDE)
    query_back = rotate(grad_queries.reshape(seq_len, nq // HD, HD), cosine, sine, -1.0)
    grad_qg_part = jnp.sum(query_back * query_unit, (0, 1))
    grad_q_proj = low(norm_back(query_back * query_gain_f, query_unit, query_inverse))
    key_back = rotate(grad_keys, cosine, sine, -1.0)
    grad_kg_part = jnp.sum(key_back * key_unit, (0, 1))
    grad_k_proj = low(norm_back(key_back * key_gain_f, key_unit, key_inverse))
    grad_qkv = jnp.concatenate(
        [
            grad_q_proj.reshape(seq_len, nq),
            grad_k_proj.reshape(seq_len, nkv),
            low(grad_values).reshape(seq_len, nkv),
        ],
        1,
    )
    grad_one_part = low(dot_nt(grad_qkv, full_qkv)).reshape(blocks, own_rows, width)
    grad_qkv_w = low(dot_tn(unit_all, grad_qkv))
    small = jnp.zeros((8, 128), WIDE).at[0].set(grad_qg_part).at[1].set(grad_kg_part)

    grad_x, out_rows, all_qkv, all_o, all_gu, all_d, sums = call(
        end_kernel,
        "end",
        3,
        112,
        (
            shaped((halves, own_rows, width)),
            shaped((halves, own_rows, width)),
            shaped((parts, rows_w, nq + 2 * nkv)),
            shaped((parts, rows_w, nq)),
            shaped((parts, rows_w, nb)),
            shaped((parts, rows_w, nc)),
            shaped((8, 128), WIDE),
        ),
        [VMEM] * 7,
        [VMEM] * 13,
        [
            pltpu.VMEM((4, 4, 8, 128), WIDE),
            pltpu.VMEM((2, 4, 8, 128), WIDE),
            pltpu.VMEM((8, 128), WIDE),
            pltpu.VMEM((2, 128, 128), WIDE),
            pltpu.VMEM((rows_w, nq + 2 * nkv), LOW),
        ]
        + column_scratch()
        + plane_scratch(nq + 2 * nkv)
        + plane_scratch(nq),
        60,
        (
            grad_one_part,
            grad_qkv_w.reshape(4, 4, rows_w, nq + 2 * nkv),
            grad_o_t.reshape(4, 4, rows_w, nq),
            sum_gu,
            sum_d,
            w_qkv,
            w_gu,
            attn_gain_f,
            mlp_gain_f,
            grad_mid,
            x_own,
            result,
            small,
        ),
    )

    def columns(piece):
        return full(jnp.swapaxes(piece, 0, 1).reshape(rows_w, -1))

    def rows(piece):
        return full(jnp.swapaxes(piece, 1, 2).reshape(-1, rows_w))

    sum_qk = lax.dynamic_slice_in_dim(sums[:2], lax.axis_index("fsdp") * few, few, 1)
    return (
        out_rows.reshape(rows_here, width),
        full(grad_x).reshape(rows_here, width),
        sums[2],
        columns(all_qkv[:, :, :nq]),
        columns(all_qkv[:, :, nq : nq + nkv]),
        columns(all_qkv[:, :, nq + nkv :]),
        sum_qk[0],
        sum_qk[1],
        rows(all_o),
        sums[3],
        columns(all_gu[:, :, :nff]),
        columns(all_gu[:, :, nff:]),
        rows(all_d),
    )


def solution(mesh):
    weight = P("fsdp", "tp")
    turned = P("tp", "fsdp")
    acts = P(("fsdp", "ctx"), None)
    gain = P("fsdp")
    return jax.shard_map(
        per_device,
        mesh=mesh,
        in_specs=(
            acts,
            P(("fsdp", "ctx")),
            gain,
            weight,
            weight,
            weight,
            gain,
            gain,
            turned,
            gain,
            weight,
            weight,
            turned,
            acts,
        ),
        out_specs=(
            acts,
            acts,
            gain,
            weight,
            weight,
            weight,
            gain,
            gain,
            turned,
            gain,
            weight,
            weight,
            turned,
        ),
        check_vma=False,
    )
```

```python
import jax
import jax.numpy as jnp
from jax import lax
from jax.experimental import pallas as pl
from jax.experimental.pallas import tpu as pltpu
from jax.sharding import PartitionSpec as P

HD = 128
MESH = pl.DeviceIdType.MESH
HBM = pl.BlockSpec(memory_space=pl.ANY)
VMEM = pl.BlockSpec(memory_space=pltpu.VMEM)
LOW = jnp.bfloat16
WIDE = jnp.float32
SCALE = HD ** (-0.5)


epsilon = 1e-06
rope_base = 1000000.0


def inverse_of(values_in):
    return lax.rsqrt(jnp.mean(values_in * values_in, -1, keepdims=True) + epsilon)


def norm_back(grad_in, unit_in, inverse):
    return inverse * (grad_in - unit_in * jnp.mean(grad_in * unit_in, -1, keepdims=True))


def dot_nn(left, right):
    return jnp.dot(left, right, preferred_element_type=WIDE)


def dot_tn(left, right):
    return lax.dot_general(left, right, (((0,), (0,)), ((), ())), preferred_element_type=WIDE)


def dot_nt(left, right):
    return lax.dot_general(left, right, (((1,), (1,)), ((), ())), preferred_element_type=WIDE)


def low(values_in):
    return values_in.astype(LOW)


def full(values_in):
    return values_in.astype(WIDE)


def place():
    plane = lax.axis_index("fsdp")
    part = lax.axis_index("ctx")
    half = lax.axis_index("tp")
    return {
        "z": lax.div(plane, 4),
        "x": lax.rem(plane, 4),
        "y": lax.div(part, 2) * 2 + half,
        "core": lax.rem(part, 2),
    }


def device(where):
    return (
        where["z"] * 4 + where["x"],
        lax.div(where["y"], 2) * 2 + where["core"],
        lax.rem(where["y"], 2),
    )


def moved(here, axis, step):
    there = dict(here)
    if axis == "pair":
        there["y"] = here["y"] + 1 - 2 * lax.rem(here["y"], 2)
    elif axis == "cross":
        there["y"] = 3 - here["y"]
    elif axis == "core":
        there["core"] = 1 - here["core"]
    else:
        there[axis] = lax.rem(here[axis] + step, 4)
    return there


def block_of(y, core):
    return lax.div(y, 2) * 4 + core * 2 + lax.rem(y, 2)


class Group:
    def __init__(self, copies):
        self.copies = copies

    def wait_recv(self):
        for copy in self.copies:
            copy.wait_recv()


class Links:
    def __init__(self, send_sems, recv_sems):
        self.here = place()
        self.send_sems, self.recv_sems = send_sems, recv_sems
        self.started = []

    def meet(self, peers):
        barrier = pltpu.get_barrier_semaphore()
        for axis, step in peers:
            pl.semaphore_signal(
                barrier,
                inc=1,
                device_id=device(moved(self.here, axis, step)),
                device_id_type=MESH,
            )
        pl.semaphore_wait(barrier, len(peers))

    def send(self, src, dst, axis, step=0):
        if isinstance(src, list):
            return Group([self.send(a, b, axis, step) for a, b in zip(src, dst)])
        spot = len(self.started)
        assert spot < self.send_sems.shape[0]
        copy = pltpu.make_async_remote_copy(
            src_ref=src,
            dst_ref=dst,
            send_sem=self.send_sems.at[spot],
            recv_sem=self.recv_sems.at[spot],
            device_id=device(moved(self.here, axis, step)),
            device_id_type=MESH,
        )
        copy.start()
        self.started.append(copy)
        return copy

    def drain(self):
        for copy in self.started:
            copy.wait_send()


class Locals:
    def __init__(self, sems):
        self.sems = sems
        self.count = 0

    def start(self, src, dst):
        assert self.count < self.sems.shape[0]
        copy = pltpu.make_async_copy(src, dst, self.sems.at[self.count])
        self.count += 1
        copy.start()
        return copy


PLANE = [("x", 1), ("x", 2), ("x", 3), ("z", 1), ("z", 2), ("z", 3)]
COLUMN = [("y", 1), ("y", 2), ("y", 3), ("core", 0)]


def step_all(jobs):
    left = []
    for job in jobs:
        try:
            next(job)
            left.append(job)
        except StopIteration:
            pass
    return left


def together(jobs):
    jobs = list(jobs)
    while jobs:
        jobs = step_all(jobs)


def side_by_side(jobs):
    jobs = list(jobs)
    while jobs:
        jobs = step_all(jobs)
        if jobs:
            yield


def each(count, step, body):
    def one(i, carry):
        body(pl.ds(pl.multiple_of(i * step, step), step))
        return carry

    lax.fori_loop(0, count // step, one, 0)


def aligned(start, size):
    return pl.ds(pl.multiple_of(start, size), size)


def add_rows(into, first, second):
    if isinstance(into, list):
        for refs in zip(into, first, second):
            add_rows(*refs)
        return
    lead, rows = into.shape[:-2], into.shape[-2]

    def add(spot):
        def body(window):
            spots = spot + (window,)
            into[spots] = low(full(first[spots]) + full(second[spots]))

        return body

    if not lead:
        each(rows, 16, add(()))
    else:
        for i in range(lead[0]):
            each(rows, 16, add((i,)))


def gather4(links, axis, own, block, arrived=None):
    me = links.here[axis]
    before, after, far = lax.rem(me + 3, 4), lax.rem(me + 1, 4), lax.rem(me + 2, 4)
    arrived = arrived or (lambda spot, side: None)
    up, down = {}, {}
    up[0] = links.send(own(0), block(me, 0), axis, 1)
    down[1] = links.send(own(1), block(me, 1), axis, 3)
    up[1] = links.send(own(1), block(me, 1), axis, 1)
    down[0] = links.send(own(0), block(me, 0), axis, 3)
    yield
    up[0].wait_recv()
    up_far = links.send(block(before, 0), block(before, 0), axis, 1)
    arrived(before, 0)
    down[1].wait_recv()
    down_far = links.send(block(after, 1), block(after, 1), axis, 3)
    arrived(after, 1)
    yield
    up[1].wait_recv()
    arrived(before, 1)
    down[0].wait_recv()
    arrived(after, 0)
    yield
    up_far.wait_recv()
    arrived(far, 0)
    down_far.wait_recv()
    arrived(far, 1)


def straight4(links, axis, own, block):
    me = links.here[axis]
    copies = [
        links.send(own(h), block(me, h), axis, step) for step in (2, 1, 3) for h in range(2)
    ]
    yield
    for copy in copies:
        copy.wait_recv()


def scatter4(links, axis, mine, near, far):
    me = links.here[axis]
    before, after, beyond = lax.rem(me + 3, 4), lax.rem(me + 1, 4), lax.rem(me + 2, 4)
    up_far = links.send(mine(beyond, 0), far[0], axis, 1)
    down_far = links.send(mine(beyond, 1), far[1], axis, 3)
    up_one = links.send(mine(after, 1), near[0](1), axis, 1)
    down_one = links.send(mine(before, 0), near[1](0), axis, 3)
    yield
    up_far.wait_recv()
    add_rows(far[0], far[0], mine(after, 0))
    up_two = links.send(far[0], near[0](0), axis, 1)
    down_far.wait_recv()
    add_rows(far[1], far[1], mine(before, 1))
    down_two = links.send(far[1], near[1](1), axis, 3)
    yield
    up_one.wait_recv()
    down_one.wait_recv()
    yield
    up_two.wait_recv()
    down_two.wait_recv()


def column_gather(links, own_ref, out):
    here = links.here
    rows = out.shape[1] // 2
    shared = []

    def own(h):
        return own_ref.at[pl.ds(h * rows, rows)]

    def block(p, h):
        return out.at[block_of(p, here["core"]), pl.ds(h * rows, rows)]

    def arrived(p, h):
        shared.append(links.send(block(p, h), block(p, h), "core"))

    ring = gather4(links, "y", own, block, arrived)
    next(ring)
    for h in range(2):
        shared.append(links.send(own(h), block(here["y"], h), "core"))
    yield
    for _ in ring:
        yield
    yield
    for copy in shared:
        copy.wait_recv()


def column_fetch(links, own, out, pieces):
    here = links.here
    y, core = here["y"], here["core"]
    y_lo = lax.rem(y, 2)
    rows = out.shape[1] // pieces
    spots = [pl.ds(q * rows, rows) for q in range(pieces)]
    spot, twin = block_of(y, core), block_of(y + 1 - 2 * y_lo, core)
    first, second = block_of(3 - y, core), block_of(2 - y + 2 * y_lo, core)
    across = [links.send(own(y_lo, w), out.at[spot, w], "cross") for w in spots]
    shared = [
        links.send(own(y_lo, pl.ds(0, out.shape[1])), out.at[spot], "core"),
        links.send(own(1 - y_lo, pl.ds(0, out.shape[1])), out.at[twin], "core"),
    ]
    passed = []
    for copy, w in zip(across, spots):
        yield
        copy.wait_recv()
        passed.append(links.send(out.at[first, w], out.at[first, w], "pair"))
        shared.append(links.send(out.at[first, w], out.at[first, w], "core"))
    for copy, w in zip(passed, spots):
        yield
        copy.wait_recv()
        shared.append(links.send(out.at[second, w], out.at[second, w], "core"))
    yield
    for copy in shared:
        copy.wait_recv()


class ColumnSum:
    def __init__(self, links, partial, passed, near, far, done):
        self.links, self.partial, self.done = links, partial, done
        self.passed, self.near, self.far = passed, near, far
        self.copies = {}

    def over(self, y_hi):
        core = self.links.here["core"]
        for y in (2 * y_hi, 2 * y_hi + 1):
            self.copies[y] = self.links.send(
                self.partial.at[block_of(y, 1 - core)], self.passed.at[y], "core"
            )

    def ring(self):
        links, partial, passed, near, far = (
            self.links,
            self.partial,
            self.passed,
            self.near,
            self.far,
        )
        core, me = links.here["core"], links.here["y"]
        before, after, beyond = lax.rem(me + 3, 4), lax.rem(me + 1, 4), lax.rem(me + 2, 4)
        rows = partial.shape[1] // 2

        def mine(p, h):
            return passed.at[p, pl.ds(h * rows, rows)]

        def add(p, h):
            add_rows(mine(p, h), mine(p, h), partial.at[block_of(p, core), pl.ds(h * rows, rows)])

        for y in range(4):
            self.copies[y].wait_recv()
        add(beyond, 0)
        up_far = links.send(mine(beyond, 0), far.at[0], "y", 1)
        add(beyond, 1)
        down_far = links.send(mine(beyond, 1), far.at[1], "y", 3)
        add(after, 1)
        up_one = links.send(mine(after, 1), near.at[0, pl.ds(rows, rows)], "y", 1)
        add(before, 0)
        down_one = links.send(mine(before, 0), near.at[1, pl.ds(0, rows)], "y", 3)
        add(after, 0)
        add(before, 1)
        yield
        up_far.wait_recv()
        add_rows(far.at[0], far.at[0], mine(after, 0))
        up_two = links.send(far.at[0], near.at[0, pl.ds(0, rows)], "y", 1)
        down_far.wait_recv()
        add_rows(far.at[1], far.at[1], mine(before, 1))
        down_two = links.send(far.at[1], near.at[1, pl.ds(rows, rows)], "y", 3)
        for h in range(2):
            add(me, h)
        yield
        up_one.wait_recv()
        down_one.wait_recv()
        yield
        up_two.wait_recv()
        down_two.wait_recv()
        total = passed.at[me]

        def body(window):
            self.done(
                window, full(total[window]) + (full(near[0, window]) + full(near[1, window]))
            )

        each(2 * rows, 16, body)


def column_scratch(rows):
    return [
        pltpu.VMEM((4, rows, 2048), LOW),
        pltpu.VMEM((2, rows, 2048), LOW),
        pltpu.VMEM((2, rows // 2, 2048), LOW),
    ]


class ByRows:
    def __init__(self, ref):
        self.ref = ref
        self.sides = [pl.ds(s * ref.shape[3] // 2, ref.shape[3] // 2) for s in range(2)]

    def own(self, own_ref, h, s):
        rows = own_ref.shape[0] // 2
        return [own_ref.at[pl.ds(h * rows, rows), self.sides[s]]]

    def one(self, z, x, h, s):
        rows = self.ref.shape[2] // 2
        return [self.ref.at[z, x, pl.ds(h * rows, rows), self.sides[s]]]

    def of_z(self, z, h, s):
        return [self.ref.at[z, pl.ds(2 * h, 2), :, self.sides[s]]]

    def of_x(self, x, h, s):
        return [self.ref.at[pl.ds(2 * h, 2), x, :, self.sides[s]]]


class ByColumns:
    def __init__(self, ref):
        self.ref = ref
        self.rows = ref.shape[0] // 2

    def own(self, own_ref, h, s):
        rows = self.rows // 2
        return [own_ref.at[pl.ds(s * self.rows + h * rows, rows)]]

    def one(self, z, x, h, s):
        rows = self.rows // 2
        return [self.ref.at[pl.ds(s * self.rows + h * rows, rows), aligned((z * 4 + x) * 128, 128)]]

    def of_z(self, z, h, s):
        return [self.ref.at[pl.ds(s * self.rows, self.rows), aligned(z * 512 + h * 256, 256)]]

    def of_x(self, x, h, s):
        return [
            self.ref.at[pl.ds(s * self.rows, self.rows), aligned((2 * h + k) * 512 + x * 128, 128)]
            for k in range(2)
        ]


def plane_first(links, blocks, own_ref, how):
    z, x = links.here["z"], links.here["x"]
    return side_by_side(
        [
            how(
                links,
                "x",
                lambda h: blocks.own(own_ref, h, 0),
                lambda p, h: blocks.one(z, p, h, 0),
            ),
            how(
                links,
                "z",
                lambda h: blocks.own(own_ref, h, 1),
                lambda p, h: blocks.one(p, x, h, 1),
            ),
        ]
    )


def plane_second(links, blocks, how):
    z, x = links.here["z"], links.here["x"]
    return side_by_side(
        [
            how(
                links, "z", lambda h: blocks.of_z(z, h, 0), lambda p, h: blocks.of_z(p, h, 0)
            ),
            how(
                links, "x", lambda h: blocks.of_x(x, h, 1), lambda p, h: blocks.of_x(p, h, 1)
            ),
        ]
    )


def plane_scratch(rows, width):
    return [
        pltpu.VMEM((2, 2, 4, rows, width), LOW),
        pltpu.VMEM((2, 2, 2, rows, width), LOW),
        pltpu.VMEM((2, 4, rows, width), LOW),
        pltpu.VMEM((2, 2, rows, width), LOW),
        pltpu.VMEM((2, 2, rows // 2, width), LOW),
    ]


def plane_scatter(links, grad, out, near, far, middle, near_two, far_two):
    z, x = links.here["z"], links.here["x"]
    by_rows = len(grad.shape) == 4
    rows, half = middle.shape[2:]

    def block(i, j, s):
        if by_rows:
            return grad.at[i, j, :, pl.ds(s * half, half)]
        return grad.at[pl.ds(s * rows, rows), aligned((i * 4 + j) * 128, 128)]

    def window_of(ref, s):
        if by_rows:
            return ref.at[:, pl.ds(s * half, half)]
        return ref.at[pl.ds(s * rows, rows)]

    def mine(s):
        if s == 0:
            return lambda p, h: [block(2 * h + k, p, 0) for k in range(2)]
        return lambda p, h: [block(p, 2 * h + k, 1) for k in range(2)]

    yield from side_by_side(
        [
            scatter4(
                links,
                axis,
                mine(s),
                [
                    lambda h, s=s, i=i: [near.at[s, i, 2 * h + k] for k in range(2)]
                    for i in range(2)
                ],
                [[far.at[s, i, k] for k in range(2)] for i in range(2)],
            )
            for s, axis in enumerate(("x", "z"))
        ]
    )
    for s in range(2):
        for p in range(4):
            own = block(p, x, 0) if s == 0 else block(z, p, 1)

            def body(window, s=s, p=p, own=own):
                middle[s, p, window] = low(
                    full(own[window])
                    + (full(near[s, 0, p, window]) + full(near[s, 1, p, window]))
                )

            each(rows, 16, body)
    part = rows // 2
    yield from side_by_side(
        [
            scatter4(
                links,
                axis,
                lambda p, h, s=s: middle.at[s, p, pl.ds(h * part, part)],
                [lambda h, s=s, i=i: near_two.at[s, i, pl.ds(h * part, part)] for i in range(2)],
                [far_two.at[s, 0], far_two.at[s, 1]],
            )
            for s, axis in enumerate(("z", "x"))
        ]
    )
    for s, me in enumerate((z, x)):
        into = window_of(out, s)

        def body(window, s=s, me=me, into=into):
            into[window] = low(
                full(middle[s, me, window])
                + (full(near_two[s, 0, window]) + full(near_two[s, 1, window]))
            )

        each(rows, 16, body)


def small_plane(links, own, out):
    z, x = links.here["z"], links.here["x"]
    out[z, x] = own[...]
    copies = [links.send(own, out.at[z, x], "x", step) for step in (1, 2, 3)]
    yield
    for copy in copies:
        copy.wait_recv()
    copies = [links.send(out.at[z], out.at[z], "z", step) for step in (1, 2, 3)]
    yield
    for copy in copies:
        copy.wait_recv()


def small_column(links, own, out):
    core, y = links.here["core"], links.here["y"]
    out[core, y] = own[...]
    copies = [links.send(own, out.at[core, y], "y", step) for step in (1, 2, 3)]
    yield
    for copy in copies:
        copy.wait_recv()
    copy = links.send(out.at[core], out.at[core], "core")
    yield
    copy.wait_recv()


def call(kernel, name, number, copies, kept, outs, out_specs, in_specs, scratch, vmem, operands):
    return pl.pallas_call(
        kernel,
        name=name,
        out_shape=outs,
        in_specs=in_specs,
        out_specs=out_specs,
        scratch_shapes=[
            pltpu.SemaphoreType.DMA((copies,)),
            pltpu.SemaphoreType.DMA((copies,)),
            pltpu.SemaphoreType.DMA((kept,)),
        ]
        + scratch,
        compiler_params=pltpu.CompilerParams(
            collective_id=number, has_side_effects=True, vmem_limit_bytes=vmem * 2**20
        ),
    )(*operands)


def shaped(shape, kind=LOW):
    return jax.ShapeDtypeStruct(shape, kind)


def turn_rows(values, cosine, sine):
    return values * cosine + pltpu.roll(values, HD // 2, 1) * sine


def forward_kernel(
    q_weight,
    k_weight,
    v_weight,
    o_weight,
    gate_weight,
    up_weight,
    down_weight,
    tokens,
    cotangent,
    gain_one,
    gain_two,
    gains,
    seq,
    waves,
    full_qkv_out,
    full_o_out,
    full_gu,
    full_d,
    unit_out,
    two_all,
    dy_all,
    middle,
    attended,
    queries,
    keys,
    values,
    proj,
    table,
    gains_all,
    starts,
    send_sems,
    recv_sems,
    kept,
    raw_qkv,
    own_qkv,
    own_o,
    raw_gu,
    own_gu,
    x_both,
    dy_both,
    down_own,
    full_qkv,
    full_o,
    unit_all,
    seq_all,
    partial,
    two_own,
    *column,
):
    links = Links(send_sems, recv_sems)
    local = Locals(kept)
    here = links.here
    z, x, y, core = here["z"], here["x"], here["y"], here["core"]
    half = lax.rem(y, 2)
    part = lax.div(y, 2) * 2 + core
    spot = block_of(y, core)
    plane = z * 4 + x
    own_rows = x_both.shape[0] // 2
    nq, nkv = own_o.shape[0], keys.shape[1]
    nff = raw_gu.shape[1] // 2

    load_x = local.start(tokens, x_both)
    load_qkv = [
        local.start(q_weight.at[:, aligned(part * nq, nq)], raw_qkv.at[:, pl.ds(0, nq)]),
        local.start(k_weight.at[:, aligned(part * nkv, nkv)], raw_qkv.at[:, pl.ds(nq, nkv)]),
        local.start(v_weight.at[:, aligned(part * nkv, nkv)], raw_qkv.at[:, pl.ds(nq + nkv, nkv)]),
    ]
    load_o = local.start(o_weight.at[aligned(part * nq, nq)], own_o)
    load_gu = [
        local.start(gate_weight.at[:, aligned(part * nff, nff)], raw_gu.at[:, pl.ds(0, nff)]),
        local.start(up_weight.at[:, aligned(part * nff, nff)], raw_gu.at[:, pl.ds(nff, nff)]),
    ]
    load_late = [
        local.start(down_weight.at[aligned(part * nff, nff)], down_own),
        local.start(cotangent, dy_both),
    ]
    links.meet(PLANE + COLUMN)
    load_x.wait()

    base = part * 2

    def norm_one(window):
        rows = pl.ds(pl.multiple_of(half * own_rows + window.start, 16), 16)
        value = full(x_both[rows])
        unit_all[spot, window] = low(value * inverse_of(value))

    each(own_rows, 16, norm_one)
    column_one = column_gather(links, unit_all.at[spot], unit_all)
    small = [small_column(links, seq, seq_all), small_plane(links, gains, gains_all)]
    step_all([column_one] + small)
    for copy in load_qkv:
        copy.wait()

    def scale_qkv(window):
        own_qkv[window] = low(full(raw_qkv[window]) * gain_one[window])
        full_qkv[z, x, window] = own_qkv[window]

    each(own_rows, 16, scale_qkv)
    blocks_qkv, blocks_o = ByRows(full_qkv), ByColumns(full_o)
    blocks_gu, blocks_d = ByRows(full_gu), ByColumns(full_d)
    first_qkv = plane_first(links, blocks_qkv, own_qkv, straight4)
    step_all([first_qkv])
    load_o.wait()
    first_o = plane_first(links, blocks_o, own_o, straight4)
    keep_o = local.start(own_o, full_o.at[:, aligned(plane * 128, 128)])
    for copy in load_gu + load_late:
        copy.wait()

    def scale_gu(window):
        own_gu[window] = low(full(raw_gu[window]) * gain_two[window])

    each(own_rows, 16, scale_gu)
    step_all([first_o])
    first_late = [
        plane_first(links, blocks_gu, own_gu, straight4),
        plane_first(links, blocks_d, down_own, straight4),
    ]
    step_all(first_late)
    keep_gu = local.start(own_gu, full_gu.at[z, x])
    keep_d = local.start(down_own, full_d.at[:, aligned(plane * 128, 128)])
    late = [
        local.start(dy_both.at[pl.ds(i * own_rows, own_rows)], dy_all.at[base + i])
        for i in range(2)
    ]
    together([first_qkv])
    second_qkv = plane_second(links, blocks_qkv, gather4)
    step_all([second_qkv, column_one] + small)
    together(small)

    ids = full(seq_all[...])
    count_0 = jnp.sum((ids < 0.5).astype(WIDE), (0, 1))
    count_01 = jnp.sum((ids < 1.5).astype(WIDE), (0, 1))
    start_1 = jnp.sum(count_0[0:1], 1, keepdims=True)
    start_2 = jnp.sum(count_01[0:1], 1, keepdims=True)
    starts[0:4] = jnp.broadcast_to(start_1, (4, HD))
    starts[4:8] = jnp.broadcast_to(start_2, (4, HD))

    def start_of(index):
        return jnp.where(index < start_1, 0.0, jnp.where(index < start_2, start_1, start_2))

    def tables(i, carry):
        window = aligned(i * 64, 64)
        index = full(lax.broadcasted_iota(jnp.int32, (64, HD), 0) + i * 64)
        angle = (index - start_of(index)) * waves[0:1]
        table[0, window] = jnp.cos(angle)
        table[1, window] = jnp.sin(angle) * waves[1:2]
        return carry

    lax.fori_loop(0, 6, tables, 0)
    step_all([column_one, second_qkv])
    together([first_o])
    keep_o.wait()
    second_o = plane_second(links, blocks_o, gather4)
    step_all([second_o])
    lax.fori_loop(6, 12, tables, 0)
    step_all([column_one, second_qkv])
    lax.fori_loop(12, 16, tables, 0)
    together([second_qkv, column_one])
    step_all([second_o])
    together(first_late)
    keep_gu.wait()
    keep_d.wait()
    second_late = [
        plane_second(links, blocks_gu, gather4),
        plane_second(links, blocks_d, gather4),
    ]
    step_all(second_late)
    column_dy = column_fetch(
        links,
        lambda i, w: dy_both.at[
            pl.ds(pl.multiple_of(i * own_rows + w.start, w.size), w.size)
        ],
        dy_all,
        4,
    )
    step_all([column_dy])
    late += [
        local.start(full_qkv, full_qkv_out),
        local.start(unit_all, unit_out),
    ]

    gain_rows = jnp.sum(gains_all[...], (0, 1))
    q_gain, k_gain = gain_rows[0:1], gain_rows[1:2]

    def project(i, carry):
        window = aligned(i * 256, 256)
        unit = unit_all[pl.ds(2 * i, 2)].reshape(256, unit_all.shape[2])
        weights = full_qkv[...].reshape(16 * own_rows, nq + 2 * nkv)
        out = dot_nn(unit, weights)
        cosine, sine = table[0, window], table[1, window]
        for head in range(3):
            value = out[:, head * HD : (head + 1) * HD]
            proj[head, window] = value
            gain = q_gain if head < 2 else k_gain
            rotated = low(turn_rows(value * inverse_of(value) * gain, cosine, sine))
            if head < 2:
                queries[head, window] = rotated
            else:
                keys[window] = rotated
        values[window] = low(out[:, 3 * HD :])
        return carry

    lax.fori_loop(0, 4, project, 0)
    together([second_o])
    late.append(local.start(full_o, full_o_out))
    step_all([column_dy])

    def turn_done(window, total):
        rows = pl.ds(pl.multiple_of(half * own_rows + window.start, 16), 16)
        value = full(x_both[rows]) + total
        middle[window] = value
        two_own[window] = low(value * inverse_of(value))

    summed = ColumnSum(links, partial, *column, turn_done)
    for i in range(4):
        window = pl.ds(i * 256, 256)
        seen = 256 * (i + 1)
        query = jnp.concatenate([queries[0, window], queries[1, window]], 0)
        scores = dot_nt(query, keys[0:seen]) * SCALE
        row = lax.broadcasted_iota(jnp.int32, (256, 1), 0) + i * 256
        row = full(jnp.concatenate([row, row], 0))
        column_index = full(lax.broadcasted_iota(jnp.int32, (512, seen), 1))
        seen_here = (column_index <= row) & (column_index >= start_of(row))
        scores = jnp.where(seen_here, scores, -jnp.inf)
        power = jnp.exp(scores - jnp.max(scores, -1, keepdims=True))
        probs = power * (1.0 / jnp.sum(power, -1, keepdims=True))
        mixed = low(dot_nn(low(probs), values[0:seen]))
        both = jnp.concatenate([mixed[:256], mixed[256:]], 1)
        attended[window] = both
        partial[2 * i : 2 * i + 2] = low(dot_nn(both, full_o[...])).reshape(
            2, own_rows, partial.shape[2]
        )
        if i % 2:
            summed.over(i // 2)
        if i > 0:
            step_all([column_dy])
    ring = summed.ring()
    for _ in range(3):
        step_all([ring])
    step_all(second_late)
    together([ring])
    late.append(local.start(two_own, two_all.at[spot]))
    column_two = column_gather(links, two_own, two_all)
    step_all([column_two])
    step_all([column_two])
    together([column_two, column_dy])
    together(second_late)
    for copy in late:
        copy.wait()
    links.drain()


def middle_kernel(
    full_gu,
    full_d,
    two_all,
    dy_all,
    middle,
    mid_all,
    down_part,
    grad_gu_w,
    grad_mid,
    sum_d,
    send_sems,
    recv_sems,
    kept,
    gu,
    down,
    two,
    dy,
    product,
    grad_gu,
    partial,
    partial_down,
    grad_w,
    grad_d,
    dy_own,
    mid_own,
    *scratch,
):
    column_a, column_b, plane = scratch[:3], scratch[3:6], scratch[6:]
    links = Links(send_sems, recv_sems)
    local = Locals(kept)
    here = links.here
    spot = block_of(here["y"], here["core"])
    rows = partial.shape[1] // 2
    width = partial.shape[2]
    nff = product.shape[1]
    windows = [pl.ds(h * rows, rows) for h in range(2)]

    load_gu = local.start(full_gu, gu)
    load_two = [local.start(two_all.at[:, windows[h]], two.at[h]) for h in range(2)]
    load_d = local.start(full_d, down)
    load_dy = [local.start(dy_all.at[:, windows[h]], dy.at[h]) for h in range(2)]
    load_own = local.start(dy_all.at[spot], dy_own)
    links.meet([("x", 1), ("x", 3), ("z", 1), ("z", 3), ("y", 1), ("y", 3), ("core", 0)])

    def chunk(h, k):
        weights = gu[...].reshape(width, 2 * nff)
        at = pl.ds((2 * h + k) * 4 * rows, 4 * rows)
        acts = dot_nn(two[h, 4 * k : 4 * k + 4].reshape(4 * rows, width), weights)
        gate, up = acts[:, :nff], acts[:, nff:]
        sigmoid = 1.0 / (1.0 + jnp.exp(-gate))
        silu = gate * sigmoid
        product[at] = low(silu * up)
        grad = dot_nt(dy[h, 4 * k : 4 * k + 4].reshape(4 * rows, width), down[...])
        grad_gu[at, 0:nff] = low(grad * up * (sigmoid * (1.0 + gate * (1.0 - sigmoid))))
        grad_gu[at, nff:] = low(grad * silu)
        part = low(dot_nt(grad_gu[at], weights))
        partial[4 * k : 4 * k + 4, windows[h]] = part.reshape(4, rows, width)

    def done(h):
        def body(window, total):
            at = pl.ds(pl.multiple_of(h * rows + window.start, 16), 16)
            value = middle[at]
            inverse = inverse_of(value)
            value = full(dy_own[at]) + norm_back(total, value * inverse, inverse)
            grad_mid[at] = value
            mid_own[at] = low(value)

        return body

    sums = [
        ColumnSum(links, partial.at[:, windows[h]], *(column_a, column_b)[h], done(h))
        for h in range(2)
    ]
    rings = [one.ring() for one in sums]
    gathers = [
        column_gather(links, mid_own.at[windows[h]], mid_all.at[:, windows[h]]) for h in range(2)
    ]
    load_gu.wait()
    load_two[0].wait()
    load_d.wait()
    load_dy[0].wait()
    load_own.wait()
    for k in range(2):
        chunk(0, k)
        sums[0].over(k)
    step_all([rings[0]])
    load_two[1].wait()
    load_dy[1].wait()
    chunk(1, 0)
    sums[1].over(0)
    step_all([rings[0]])
    chunk(1, 1)
    sums[1].over(1)
    together([rings[0]])
    step_all([gathers[0]])
    step_all([gathers[0]])
    step_all([rings[1]])

    def down_grad(i, carry):
        at = aligned(i * 256, 256)
        grad_d[at] = low(dot_tn(product[:, at], dy[...].reshape(16 * rows, width)))
        return carry

    lax.fori_loop(0, nff // 256, down_grad, 0)
    scatter = plane_scatter(links, grad_d, sum_d, *plane)
    step_all([scatter])
    step_all([gathers[0], rings[1]])

    def gate_up_grad(i, carry):
        at = aligned(i * 512, 512)
        out = dot_tn(two[:, :, :, at].reshape(16 * rows, 512), grad_gu[...])
        grad_w[i] = low(out).reshape(4, 128, 2 * nff)
        return carry

    lax.fori_loop(0, 2, gate_up_grad, 0)
    step_all([gathers[0], rings[1], scatter])
    lax.fori_loop(2, 4, gate_up_grad, 0)
    keep_w = local.start(grad_w, grad_gu_w)
    together([gathers[0], rings[1]])
    step_all([gathers[1]])
    step_all([gathers[1], scatter])
    keep_mid = local.start(mid_own, mid_all.at[spot])

    def down_forward(i, carry):
        h, k = lax.div(i, 2), lax.rem(i, 2)
        out = low(dot_nn(product[aligned(i * 4 * rows, 4 * rows)], down[...]))
        partial_down[pl.ds(4 * k, 4), aligned(h * rows, rows)] = out.reshape(4, rows, width)
        return carry

    lax.fori_loop(0, 4, down_forward, 0)
    keep_down = local.start(partial_down, down_part)
    together([gathers[1], scatter])
    for copy in (keep_w, keep_mid, keep_down):
        copy.wait()
    links.drain()


def end_kernel(
    q_weight,
    k_weight,
    v_weight,
    gate_weight,
    up_weight,
    tokens,
    full_qkv,
    full_o,
    unit_all,
    mid_all,
    down_part,
    grad_gu_w,
    attended,
    queries,
    keys,
    values,
    proj,
    table,
    gains_all,
    starts,
    gain_one,
    gain_two,
    grad_mid,
    middle,
    sum_d,
    grad_x,
    out_rows,
    all_qkv,
    all_o,
    all_gu,
    all_d,
    sums_out,
    send_sems,
    recv_sems,
    kept,
    weights,
    weight_o,
    unit,
    mid,
    part_down,
    grad_gu,
    grad_o,
    grad_qkv_w,
    raw_qkv,
    raw_gu,
    x_own,
    grad_att,
    dk,
    dv,
    grad_qkv,
    sum_gu,
    sum_qkv,
    own_o,
    own_gu,
    own_qkv,
    small,
    small_all,
    row,
    row_all,
    turned,
    x_pair,
    row_pair,
    *scratch,
):
    column_a, column_b = scratch[:3], scratch[3:6]
    plane_gu, plane_o, plane_qkv = scratch[6:11], scratch[11:16], scratch[16:]
    links = Links(send_sems, recv_sems)
    local = Locals(kept)
    here = links.here
    y, core = here["y"], here["core"]
    half = lax.rem(y, 2)
    part = lax.div(y, 2) * 2 + core
    part_other = lax.div(lax.rem(y + 2, 4), 2) * 2 + core
    rows, width = x_own.shape
    nq, nkv = own_o.shape[0], keys.shape[1]
    nff = sum_gu.shape[1] // 2

    load_mid = local.start(mid_all, mid)
    load_o = local.start(full_o, weight_o)
    load_down = local.start(down_part, part_down)
    load_gu = local.start(grad_gu_w, grad_gu)
    loads = [
        local.start(full_qkv, weights),
        local.start(unit_all, unit),
        local.start(tokens.at[aligned(half * rows, rows)], x_own),
        local.start(q_weight.at[:, aligned(part * nq, nq)], raw_qkv.at[:, pl.ds(0, nq)]),
        local.start(k_weight.at[:, aligned(part * nkv, nkv)], raw_qkv.at[:, pl.ds(nq, nkv)]),
        local.start(v_weight.at[:, aligned(part * nkv, nkv)], raw_qkv.at[:, pl.ds(nq + nkv, nkv)]),
        local.start(gate_weight.at[:, aligned(part * nff, nff)], raw_gu.at[:, pl.ds(0, nff)]),
        local.start(up_weight.at[:, aligned(part * nff, nff)], raw_gu.at[:, pl.ds(nff, nff)]),
    ]
    links.meet(PLANE + COLUMN)

    def share(own, out):
        across = links.send(own, out.at[part], "y", 2)
        beside = links.send(own, out.at[part], "core")
        keep = local.start(own, out.at[part])
        yield
        across.wait_recv()
        second = links.send(out.at[part_other], out.at[part_other], "core")
        yield
        beside.wait_recv()
        second.wait_recv()
        keep.wait()

    def exchange(own, out):
        copy = links.send(own, out.at[half], "pair")
        keep = local.start(own, out.at[half])
        yield
        copy.wait_recv()
        keep.wait()

    def done_down(window, total):
        row_pair[window] = low(middle[window] + total)

    def done_one(window, total):
        value = full(x_own[window])
        inverse = inverse_of(value)
        x_pair[window] = low(grad_mid[window] + norm_back(total, value * inverse, inverse))

    load_down.wait()
    sum_down = ColumnSum(links, part_down, *column_a, done_down)
    sum_down.over(0)
    sum_down.over(1)
    load_gu.wait()
    scatter_gu = plane_scatter(links, grad_gu, sum_gu, *plane_gu)
    step_all([scatter_gu])
    load_mid.wait()
    load_o.wait()

    def attended_grad(i, carry):
        window = aligned(i * 256, 256)
        out = low(dot_nt(mid[pl.ds(2 * i, 2)].reshape(256, width), weight_o[...]))
        grad_att[0, window] = out[:, :HD]
        grad_att[1, window] = out[:, HD:]
        return carry

    lax.fori_loop(0, 4, attended_grad, 0)
    ring_down = sum_down.ring()
    step_all([ring_down])
    grad_o[...] = low(dot_tn(attended[...], mid[...].reshape(8 * rows, width)))
    scatter_o = plane_scatter(links, grad_o, own_o, *plane_o)
    step_all([scatter_o])

    gain_rows = jnp.sum(gains_all[...], (0, 1))
    q_gain, k_gain = gain_rows[0:1], gain_rows[1:2]
    start_1, start_2 = starts[0:1, 0:1], starts[4:5, 0:1]
    dk[...] = jnp.zeros_like(dk)
    dv[...] = jnp.zeros_like(dv)
    small[...] = jnp.zeros_like(small)

    def project_back(grad, head, window, gain):
        cosine, sine = table[0, window], table[1, window]
        back = grad * cosine - pltpu.roll(grad, HD // 2, 1) * sine
        value = proj[head, window]
        inverse = inverse_of(value)
        scaled = value * inverse
        spot = 0 if head < 2 else 1
        small[spot : spot + 1] += jnp.sum(back * scaled, 0, keepdims=True)
        return low(norm_back(back * gain, scaled, inverse))

    for i in range(4):
        window = pl.ds(i * 256, 256)
        seen = 256 * (i + 1)
        query = jnp.concatenate([queries[0, window], queries[1, window]], 0)
        grad = jnp.concatenate([grad_att[0, window], grad_att[1, window]], 0)
        key, value = keys[0:seen], values[0:seen]
        scores = dot_nt(key, query) * SCALE
        column = lax.broadcasted_iota(jnp.int32, (1, 256), 1) + i * 256
        column = full(jnp.concatenate([column, column], 1))
        start = jnp.where(
            column < start_1, 0.0, jnp.where(column < start_2, start_1, start_2)
        )
        index = full(lax.broadcasted_iota(jnp.int32, (seen, 512), 0))
        scores = jnp.where((index <= column) & (index >= start), scores, -jnp.inf)
        power = jnp.exp(scores - jnp.max(scores, 0, keepdims=True))
        probs = power * (1.0 / jnp.sum(power, 0, keepdims=True))
        grad_probs = dot_nt(value, grad)
        inner = jnp.sum(probs * grad_probs, 0, keepdims=True)
        grad_scores = low(probs * (grad_probs - inner))
        dv[0:seen] += dot_nn(low(probs), grad)
        dk[0:seen] += dot_nn(grad_scores, query)
        dq = dot_tn(key, grad_scores).T * SCALE
        for head in range(2):
            grad_qkv[window, head * HD : (head + 1) * HD] = project_back(
                dq[head * 256 : (head + 1) * 256], head, window, q_gain
            )
        if i < 3:
            step_all([ring_down])

    def keys_back(i, carry):
        window = aligned(i * 256, 256)
        grad_qkv[window, nq : nq + nkv] = project_back(dk[window] * SCALE, 2, window, k_gain)
        grad_qkv[window, nq + nkv :] = low(dv[window])
        return carry

    lax.fori_loop(0, 4, keys_back, 0)
    small_job = small_plane(links, small, small_all)
    step_all([small_job])
    for copy in loads:
        copy.wait()

    def unit_grad(i, carry):
        out = low(
            dot_nt(
                grad_qkv[aligned(i * 256, 256)], weights[...].reshape(width, nq + 2 * nkv)
            )
        )
        mid[pl.ds(2 * i, 2)] = out.reshape(2, rows, width)
        return carry

    sum_one = ColumnSum(links, mid, *column_b, done_one)
    lax.fori_loop(0, 2, unit_grad, 0)
    sum_one.over(0)
    lax.fori_loop(2, 4, unit_grad, 0)
    sum_one.over(1)
    ring_one = sum_one.ring()
    step_all([ring_one, ring_down])
    together([ring_down])
    step_all([small_job, scatter_o])

    def weight_grad(i, carry):
        at = aligned(i * 512, 512)
        out = dot_tn(unit[:, :, at].reshape(8 * rows, 512), grad_qkv[...])
        grad_qkv_w[i] = low(out).reshape(4, rows, nq + 2 * nkv)
        return carry

    lax.fori_loop(0, 4, weight_grad, 0)
    scatter_qkv = plane_scatter(links, grad_qkv_w, sum_qkv, *plane_qkv)
    step_all([scatter_qkv, scatter_gu])
    share_d = share(sum_d, all_d)
    step_all([share_d])
    step_all([ring_one, scatter_o])
    pair_rows = exchange(row_pair, out_rows)
    step_all([pair_rows])
    together([scatter_o, small_job])
    share_o = share(own_o, all_o)
    step_all([share_o, scatter_qkv, scatter_gu])
    step_all([ring_one, share_d])
    together([ring_one])
    pair_x = exchange(x_pair, grad_x)
    step_all([pair_x])
    together([scatter_gu, scatter_qkv])

    def scale(into, total, raw, gain, spot):
        def body(window):
            into[window] = low(full(total[window]) * gain[window])
            part_sum = jnp.sum(full(total[window]) * full(raw[window]), 1, keepdims=True)
            turned[spot, window] = jnp.broadcast_to(part_sum, (16, HD))

        each(rows, 16, body)

    scale(own_gu, sum_gu, raw_gu, gain_two, 1)
    share_gu = share(own_gu, all_gu)
    step_all([share_gu])
    scale(own_qkv, sum_qkv, raw_qkv, gain_one, 0)
    share_qkv = share(own_qkv, all_qkv)
    step_all([share_qkv])
    row[0:2] = jnp.sum(small_all[:, :, 0:2], (0, 1))
    row[2:3] = turned[0].T[0:1]
    row[3:4] = turned[1].T[0:1]
    row[4:8] = jnp.zeros((4, HD), WIDE)
    row_job = small_column(links, row, row_all)
    together([row_job, share_gu, share_qkv, share_o, share_d, pair_rows, pair_x])
    sums_out[...] = jnp.sum(row_all[...], (0, 1))
    links.drain()


def per_device(
    tokens,
    segments,
    attn_gain,
    q_weight,
    k_weight,
    v_weight,
    q_gain,
    k_gain,
    o_weight,
    mlp_gain,
    gate_weight,
    up_weight,
    down_weight,
    cotangent,
):
    parts, halves = lax.axis_size("ctx"), lax.axis_size("tp")
    half = lax.axis_index("tp")
    rows_here, width = tokens.shape
    seq_len = rows_here * parts
    own_rows = rows_here // halves
    blocks = parts * halves

    def own(array):
        return lax.dynamic_slice_in_dim(array, half * own_rows, own_rows, 0)

    attn_gain_f = jnp.broadcast_to(full(attn_gain)[:, None], (attn_gain.shape[0], 1))
    mlp_gain_f = jnp.broadcast_to(full(mlp_gain)[:, None], (mlp_gain.shape[0], 1))
    rows_w = q_weight.shape[0]
    nq, nkv, nff = q_weight.shape[1] // parts, k_weight.shape[1] // parts, gate_weight.shape[1] // parts
    na, nb = nq + 2 * nkv, 2 * nff
    few = q_gain.shape[0]
    gains = lax.dynamic_update_slice(
        jnp.zeros((8, HD), WIDE),
        full(jnp.stack([q_gain, k_gain])),
        (0, lax.axis_index("fsdp") * few),
    )
    seq = jnp.broadcast_to(own(segments)[None, :], (8, own_rows))
    frequency = jnp.power(rope_base, -2.0 * jnp.arange(HD // 2, dtype=WIDE) / HD)
    ones = jnp.ones((HD // 2,), WIDE)
    waves = jnp.zeros((8, HD), WIDE).at[0].set(jnp.tile(frequency, 2))
    waves = waves.at[1].set(jnp.concatenate([-ones, ones]))

    (
        full_qkv,
        full_o,
        full_gu,
        full_d,
        unit_all,
        two_all,
        dy_all,
        middle,
        attended,
        queries,
        keys,
        values,
        proj,
        table,
        gains_all,
        starts,
    ) = call(
        forward_kernel,
        "forward",
        0,
        176,
        24,
        (
            shaped((4, 4, rows_w, na)),
            shaped((nq, width)),
            shaped((4, 4, rows_w, nb)),
            shaped((nff, width)),
            shaped((blocks, own_rows, width)),
            shaped((blocks, own_rows, width)),
            shaped((blocks, own_rows, width)),
            shaped((own_rows, width), WIDE),
            shaped((seq_len, nq)),
            shaped((2, seq_len, HD)),
            shaped((seq_len, HD)),
            shaped((seq_len, HD)),
            shaped((3, seq_len, HD), WIDE),
            shaped((2, seq_len, HD), WIDE),
            shaped((4, 4, 8, HD), WIDE),
            shaped((8, HD), WIDE),
        ),
        [HBM] * 7 + [VMEM] * 9,
        [HBM] * 9 + [VMEM] * 5,
        [
            pltpu.VMEM((rows_w, na), LOW),
            pltpu.VMEM((rows_w, na), LOW),
            pltpu.VMEM((nq, rows_w), LOW),
            pltpu.VMEM((rows_w, nb), LOW),
            pltpu.VMEM((rows_w, nb), LOW),
            pltpu.VMEM((rows_here, width), LOW),
            pltpu.VMEM((rows_here, width), LOW),
            pltpu.VMEM((nff, rows_w), LOW),
            pltpu.VMEM((4, 4, rows_w, na), LOW),
            pltpu.VMEM((nq, width), LOW),
            pltpu.VMEM((blocks, own_rows, width), LOW),
            pltpu.VMEM((2, 4, 8, own_rows), jnp.int32),
            pltpu.VMEM((blocks, own_rows, width), LOW),
            pltpu.VMEM((own_rows, width), LOW),
        ]
        + column_scratch(own_rows),
        58,
        (
            q_weight,
            k_weight,
            v_weight,
            o_weight,
            gate_weight,
            up_weight,
            down_weight,
            tokens,
            cotangent,
            attn_gain_f,
            mlp_gain_f,
            gains,
            seq,
            waves,
        ),
    )

    mid_all, down_part, grad_gu_w, grad_mid, sum_d = call(
        middle_kernel,
        "middle",
        1,
        112,
        16,
        (
            shaped((blocks, own_rows, width)),
            shaped((blocks, own_rows, width)),
            shaped((4, 4, rows_w, nb)),
            shaped((own_rows, width), WIDE),
            shaped((nff, rows_w)),
        ),
        [HBM] * 3 + [VMEM] * 2,
        [HBM] * 4 + [VMEM],
        [
            pltpu.VMEM((4, 4, rows_w, nb), LOW),
            pltpu.VMEM((nff, width), LOW),
            pltpu.VMEM((2, blocks, own_rows // 2, width), LOW),
            pltpu.VMEM((2, blocks, own_rows // 2, width), LOW),
            pltpu.VMEM((seq_len, nff), LOW),
            pltpu.VMEM((seq_len, nb), LOW),
            pltpu.VMEM((blocks, own_rows, width), LOW),
            pltpu.VMEM((blocks, own_rows, width), LOW),
            pltpu.VMEM((4, 4, rows_w, nb), LOW),
            pltpu.VMEM((nff, width), LOW),
            pltpu.VMEM((own_rows, width), LOW),
            pltpu.VMEM((own_rows, width), LOW),
        ]
        + column_scratch(own_rows // 2)
        + column_scratch(own_rows // 2)
        + plane_scratch(nff // 2, rows_w),
        62,
        (full_gu, full_d, two_all, dy_all, middle),
    )

    grad_x, out_rows, all_qkv, all_o, all_gu, all_d, sums = call(
        end_kernel,
        "end",
        2,
        160,
        40,
        (
            shaped((halves, own_rows, width)),
            shaped((halves, own_rows, width)),
            shaped((parts, rows_w, na)),
            shaped((parts, nq, rows_w)),
            shaped((parts, rows_w, nb)),
            shaped((parts, nff, rows_w)),
            shaped((8, HD), WIDE),
        ),
        [HBM] * 6 + [VMEM],
        [HBM] * 12 + [VMEM] * 13,
        [
            pltpu.VMEM((4, 4, rows_w, na), LOW),
            pltpu.VMEM((nq, width), LOW),
            pltpu.VMEM((blocks, own_rows, width), LOW),
            pltpu.VMEM((blocks, own_rows, width), LOW),
            pltpu.VMEM((blocks, own_rows, width), LOW),
            pltpu.VMEM((4, 4, rows_w, nb), LOW),
            pltpu.VMEM((nq, width), LOW),
            pltpu.VMEM((4, 4, rows_w, na), LOW),
            pltpu.VMEM((rows_w, na), LOW),
            pltpu.VMEM((rows_w, nb), LOW),
            pltpu.VMEM((own_rows, width), LOW),
            pltpu.VMEM((2, seq_len, HD), LOW),
            pltpu.VMEM((seq_len, HD), WIDE),
            pltpu.VMEM((seq_len, HD), WIDE),
            pltpu.VMEM((seq_len, na), LOW),
            pltpu.VMEM((rows_w, nb), LOW),
            pltpu.VMEM((rows_w, na), LOW),
            pltpu.VMEM((nq, rows_w), LOW),
            pltpu.VMEM((rows_w, nb), LOW),
            pltpu.VMEM((rows_w, na), LOW),
            pltpu.VMEM((8, HD), WIDE),
            pltpu.VMEM((4, 4, 8, HD), WIDE),
            pltpu.VMEM((8, HD), WIDE),
            pltpu.VMEM((2, 4, 8, HD), WIDE),
            pltpu.VMEM((2, rows_w, HD), WIDE),
            pltpu.VMEM((own_rows, width), LOW),
            pltpu.VMEM((own_rows, width), LOW),
        ]
        + column_scratch(own_rows)
        + column_scratch(own_rows)
        + plane_scratch(rows_w, nb // 2)
        + plane_scratch(nq // 2, rows_w)
        + plane_scratch(rows_w, na // 2),
        62,
        (
            q_weight,
            k_weight,
            v_weight,
            gate_weight,
            up_weight,
            tokens,
            full_qkv,
            full_o,
            unit_all,
            mid_all,
            down_part,
            grad_gu_w,
            attended,
            queries,
            keys,
            values,
            proj,
            table,
            gains_all,
            starts,
            attn_gain_f,
            mlp_gain_f,
            grad_mid,
            middle,
            sum_d,
        ),
    )

    def columns(piece):
        return full(jnp.swapaxes(piece, 0, 1).reshape(rows_w, -1))

    sum_qk = lax.dynamic_slice_in_dim(sums[:2], lax.axis_index("fsdp") * few, few, 1)
    return (
        out_rows.reshape(rows_here, width),
        full(grad_x).reshape(rows_here, width),
        sums[2],
        columns(all_qkv[:, :, :nq]),
        columns(all_qkv[:, :, nq : nq + nkv]),
        columns(all_qkv[:, :, nq + nkv :]),
        sum_qk[0],
        sum_qk[1],
        full(all_o).reshape(-1, rows_w),
        sums[3],
        columns(all_gu[:, :, :nff]),
        columns(all_gu[:, :, nff:]),
        full(all_d).reshape(-1, rows_w),
    )


def solution(mesh):
    weight = P("fsdp", "tp")
    turned = P("tp", "fsdp")
    acts = P(("fsdp", "ctx"), None)
    gain = P("fsdp")
    return jax.shard_map(
        per_device,
        mesh=mesh,
        in_specs=(
            acts,
            P(("fsdp", "ctx")),
            gain,
            weight,
            weight,
            weight,
            gain,
            gain,
            turned,
            gain,
            weight,
            weight,
            turned,
            acts,
        ),
        out_specs=(
            acts,
            acts,
            gain,
            weight,
            weight,
            weight,
            gain,
            gain,
            turned,
            gain,
            weight,
            weight,
            turned,
        ),
        check_vma=False,
    )
```

```python
import jax
import jax.numpy as jnp
from jax import lax
from jax.experimental import pallas as pl
from jax.experimental.pallas import tpu as pltpu
from jax.sharding import PartitionSpec as P

HD = 128
MESH = pl.DeviceIdType.MESH
HBM = pl.BlockSpec(memory_space=pl.ANY)
VMEM = pl.BlockSpec(memory_space=pltpu.VMEM)
LOW = jnp.bfloat16
WIDE = jnp.float32
SCALE = HD ** (-0.5)


epsilon = 1e-06
rope_base = 1000000.0


def inverse_of(values_in):
    return lax.rsqrt(jnp.mean(values_in * values_in, -1, keepdims=True) + epsilon)


def norm_back(grad_in, unit_in, inverse):
    return inverse * (grad_in - unit_in * jnp.mean(grad_in * unit_in, -1, keepdims=True))


def dot_nn(left, right):
    return jnp.dot(left, right, preferred_element_type=WIDE)


def dot_tn(left, right):
    return lax.dot_general(left, right, (((0,), (0,)), ((), ())), preferred_element_type=WIDE)


def dot_nt(left, right):
    return lax.dot_general(left, right, (((1,), (1,)), ((), ())), preferred_element_type=WIDE)


def low(values_in):
    return values_in.astype(LOW)


def full(values_in):
    return values_in.astype(WIDE)


def place():
    plane = lax.axis_index("fsdp")
    part = lax.axis_index("ctx")
    half = lax.axis_index("tp")
    return {
        "z": lax.div(plane, 4),
        "x": lax.rem(plane, 4),
        "y": lax.div(part, 2) * 2 + half,
        "core": lax.rem(part, 2),
    }


def device(where):
    return (
        where["z"] * 4 + where["x"],
        lax.div(where["y"], 2) * 2 + where["core"],
        lax.rem(where["y"], 2),
    )


def moved(here, axis, step):
    there = dict(here)
    if axis == "pair":
        there["y"] = here["y"] + 1 - 2 * lax.rem(here["y"], 2)
    elif axis == "cross":
        there["y"] = 3 - here["y"]
    elif axis == "core":
        there["core"] = 1 - here["core"]
    else:
        there[axis] = lax.rem(here[axis] + step, 4)
    return there


def block_of(y, core):
    return lax.div(y, 2) * 4 + core * 2 + lax.rem(y, 2)


class Group:
    def __init__(self, copies):
        self.copies = copies

    def wait_recv(self):
        for copy in self.copies:
            copy.wait_recv()


class Links:
    def __init__(self, send_sems, recv_sems):
        self.here = place()
        self.send_sems, self.recv_sems = send_sems, recv_sems
        self.started = []

    def meet(self, peers):
        barrier = pltpu.get_barrier_semaphore()
        for axis, step in peers:
            pl.semaphore_signal(
                barrier,
                inc=1,
                device_id=device(moved(self.here, axis, step)),
                device_id_type=MESH,
            )
        pl.semaphore_wait(barrier, len(peers))

    def send(self, src, dst, axis, step=0):
        if isinstance(src, list):
            return Group([self.send(a, b, axis, step) for a, b in zip(src, dst)])
        spot = len(self.started)
        assert spot < self.send_sems.shape[0]
        copy = pltpu.make_async_remote_copy(
            src_ref=src,
            dst_ref=dst,
            send_sem=self.send_sems.at[spot],
            recv_sem=self.recv_sems.at[spot],
            device_id=device(moved(self.here, axis, step)),
            device_id_type=MESH,
        )
        copy.start()
        self.started.append(copy)
        return copy

    def drain(self):
        for copy in self.started:
            copy.wait_send()


class Locals:
    def __init__(self, sems):
        self.sems = sems
        self.count = 0

    def start(self, src, dst):
        assert self.count < self.sems.shape[0]
        copy = pltpu.make_async_copy(src, dst, self.sems.at[self.count])
        self.count += 1
        copy.start()
        return copy


PLANE = [("x", 1), ("x", 2), ("x", 3), ("z", 1), ("z", 2), ("z", 3)]
COLUMN = [("y", 1), ("y", 2), ("y", 3), ("core", 0)]


def step_all(jobs):
    left = []
    for job in jobs:
        try:
            next(job)
            left.append(job)
        except StopIteration:
            pass
    return left


def together(jobs):
    jobs = list(jobs)
    while jobs:
        jobs = step_all(jobs)


def side_by_side(jobs):
    jobs = list(jobs)
    while jobs:
        jobs = step_all(jobs)
        if jobs:
            yield


def each(count, step, body):
    def one(i, carry):
        body(pl.ds(pl.multiple_of(i * step, step), step))
        return carry

    lax.fori_loop(0, count // step, one, 0)


def aligned(start, size):
    return pl.ds(pl.multiple_of(start, size), size)


def add_rows(into, first, second):
    if isinstance(into, list):
        for refs in zip(into, first, second):
            add_rows(*refs)
        return
    lead, rows = into.shape[:-2], into.shape[-2]

    def add(spot):
        def body(window):
            spots = spot + (window,)
            into[spots] = first[spots] + second[spots]

        return body

    if not lead:
        each(rows, 16, add(()))
    else:
        for i in range(lead[0]):
            each(rows, 16, add((i,)))


def gather4(links, axis, own, block, arrived=None):
    me = links.here[axis]
    before, after, far = lax.rem(me + 3, 4), lax.rem(me + 1, 4), lax.rem(me + 2, 4)
    arrived = arrived or (lambda spot, side: None)
    up, down = {}, {}
    up[0] = links.send(own(0), block(me, 0), axis, 1)
    down[1] = links.send(own(1), block(me, 1), axis, 3)
    up[1] = links.send(own(1), block(me, 1), axis, 1)
    down[0] = links.send(own(0), block(me, 0), axis, 3)
    yield
    up[0].wait_recv()
    up_far = links.send(block(before, 0), block(before, 0), axis, 1)
    arrived(before, 0)
    down[1].wait_recv()
    down_far = links.send(block(after, 1), block(after, 1), axis, 3)
    arrived(after, 1)
    yield
    up[1].wait_recv()
    arrived(before, 1)
    down[0].wait_recv()
    arrived(after, 0)
    yield
    up_far.wait_recv()
    arrived(far, 0)
    down_far.wait_recv()
    arrived(far, 1)


def straight4(links, axis, own, block):
    me = links.here[axis]
    copies = [
        links.send(own(h), block(me, h), axis, step) for step in (2, 1, 3) for h in range(2)
    ]
    yield
    for copy in copies:
        copy.wait_recv()


def scatter4(links, axis, mine, near, far):
    me = links.here[axis]
    before, after, beyond = lax.rem(me + 3, 4), lax.rem(me + 1, 4), lax.rem(me + 2, 4)
    up_far = links.send(mine(beyond, 0), far[0], axis, 1)
    down_far = links.send(mine(beyond, 1), far[1], axis, 3)
    up_one = links.send(mine(after, 1), near[0](1), axis, 1)
    down_one = links.send(mine(before, 0), near[1](0), axis, 3)
    yield
    up_far.wait_recv()
    add_rows(far[0], far[0], mine(after, 0))
    up_two = links.send(far[0], near[0](0), axis, 1)
    down_far.wait_recv()
    add_rows(far[1], far[1], mine(before, 1))
    down_two = links.send(far[1], near[1](1), axis, 3)
    yield
    up_one.wait_recv()
    down_one.wait_recv()
    up_two.wait_recv()
    down_two.wait_recv()


def column_gather(links, own_ref, out):
    here = links.here
    rows = out.shape[1] // 2
    shared = []

    def own(h):
        return own_ref.at[pl.ds(h * rows, rows)]

    def block(p, h):
        return out.at[block_of(p, here["core"]), pl.ds(h * rows, rows)]

    def arrived(p, h):
        shared.append(links.send(block(p, h), block(p, h), "core"))

    ring = gather4(links, "y", own, block, arrived)
    next(ring)
    for h in range(2):
        shared.append(links.send(own(h), block(here["y"], h), "core"))
    yield
    for _ in ring:
        yield
    yield
    for copy in shared:
        copy.wait_recv()


def column_fetch(links, own, out, pieces):
    here = links.here
    y, core = here["y"], here["core"]
    y_lo = lax.rem(y, 2)
    rows = out.shape[1] // pieces
    spots = [pl.ds(q * rows, rows) for q in range(pieces)]
    spot, twin = block_of(y, core), block_of(y + 1 - 2 * y_lo, core)
    first, second = block_of(3 - y, core), block_of(2 - y + 2 * y_lo, core)
    across = [links.send(own(y_lo, w), out.at[spot, w], "cross") for w in spots]
    shared = [
        links.send(own(y_lo, pl.ds(0, out.shape[1])), out.at[spot], "core"),
        links.send(own(1 - y_lo, pl.ds(0, out.shape[1])), out.at[twin], "core"),
    ]
    passed = []
    for copy, w in zip(across, spots):
        yield
        copy.wait_recv()
        passed.append(links.send(out.at[first, w], out.at[first, w], "pair"))
        shared.append(links.send(out.at[first, w], out.at[first, w], "core"))
    for copy, w in zip(passed, spots):
        yield
        copy.wait_recv()
        shared.append(links.send(out.at[second, w], out.at[second, w], "core"))
    yield
    for copy in shared:
        copy.wait_recv()


class ColumnSum:
    def __init__(self, links, partial, passed, near, far, done):
        self.links, self.partial, self.done = links, partial, done
        self.passed, self.near, self.far = passed, near, far
        self.copies = {}

    def over(self, y_hi):
        core = self.links.here["core"]
        for y in (2 * y_hi, 2 * y_hi + 1):
            self.copies[y] = self.links.send(
                self.partial.at[block_of(y, 1 - core)], self.passed.at[y], "core"
            )

    def ring(self):
        links, partial, passed, near, far = (
            self.links,
            self.partial,
            self.passed,
            self.near,
            self.far,
        )
        core, me = links.here["core"], links.here["y"]
        before, after, beyond = lax.rem(me + 3, 4), lax.rem(me + 1, 4), lax.rem(me + 2, 4)
        rows = partial.shape[1] // 2

        def mine(p, h):
            return passed.at[p, pl.ds(h * rows, rows)]

        def add(p, h):
            add_rows(mine(p, h), mine(p, h), partial.at[block_of(p, core), pl.ds(h * rows, rows)])

        for y in range(4):
            self.copies[y].wait_recv()
        add(beyond, 0)
        up_far = links.send(mine(beyond, 0), far.at[0], "y", 1)
        add(beyond, 1)
        down_far = links.send(mine(beyond, 1), far.at[1], "y", 3)
        add(after, 1)
        up_one = links.send(mine(after, 1), near.at[0, pl.ds(rows, rows)], "y", 1)
        add(before, 0)
        down_one = links.send(mine(before, 0), near.at[1, pl.ds(0, rows)], "y", 3)
        add(after, 0)
        add(before, 1)
        yield
        up_far.wait_recv()
        add_rows(far.at[0], far.at[0], mine(after, 0))
        up_two = links.send(far.at[0], near.at[0, pl.ds(0, rows)], "y", 1)
        down_far.wait_recv()
        add_rows(far.at[1], far.at[1], mine(before, 1))
        down_two = links.send(far.at[1], near.at[1, pl.ds(rows, rows)], "y", 3)
        for h in range(2):
            add(me, h)
        yield
        up_one.wait_recv()
        down_one.wait_recv()
        up_two.wait_recv()
        down_two.wait_recv()
        total = passed.at[me]

        def body(window):
            self.done(
                window, full(total[window]) + (full(near[0, window]) + full(near[1, window]))
            )

        each(2 * rows, 16, body)


def column_scratch(rows):
    return [
        pltpu.VMEM((4, rows, 2048), LOW),
        pltpu.VMEM((2, rows, 2048), LOW),
        pltpu.VMEM((2, rows // 2, 2048), LOW),
    ]


class ByRows:
    def __init__(self, ref):
        self.ref = ref
        self.sides = [pl.ds(s * ref.shape[3] // 2, ref.shape[3] // 2) for s in range(2)]

    def own(self, own_ref, h, s):
        rows = own_ref.shape[0] // 2
        return [own_ref.at[pl.ds(h * rows, rows), self.sides[s]]]

    def one(self, z, x, h, s):
        rows = self.ref.shape[2] // 2
        return [self.ref.at[z, x, pl.ds(h * rows, rows), self.sides[s]]]

    def of_z(self, z, h, s):
        return [self.ref.at[z, pl.ds(2 * h, 2), :, self.sides[s]]]

    def of_x(self, x, h, s):
        return [self.ref.at[pl.ds(2 * h, 2), x, :, self.sides[s]]]


class ByColumns:
    def __init__(self, ref):
        self.ref = ref
        self.rows = ref.shape[0] // 2

    def own(self, own_ref, h, s):
        rows = self.rows // 2
        return [own_ref.at[pl.ds(s * self.rows + h * rows, rows)]]

    def one(self, z, x, h, s):
        rows = self.rows // 2
        return [self.ref.at[pl.ds(s * self.rows + h * rows, rows), aligned((z * 4 + x) * 128, 128)]]

    def of_z(self, z, h, s):
        return [self.ref.at[pl.ds(s * self.rows, self.rows), aligned(z * 512 + h * 256, 256)]]

    def of_x(self, x, h, s):
        return [
            self.ref.at[pl.ds(s * self.rows, self.rows), aligned((2 * h + k) * 512 + x * 128, 128)]
            for k in range(2)
        ]


def plane_first(links, blocks, own_ref, how):
    z, x = links.here["z"], links.here["x"]
    return side_by_side(
        [
            how(
                links,
                "x",
                lambda h: blocks.own(own_ref, h, 0),
                lambda p, h: blocks.one(z, p, h, 0),
            ),
            how(
                links,
                "z",
                lambda h: blocks.own(own_ref, h, 1),
                lambda p, h: blocks.one(p, x, h, 1),
            ),
        ]
    )


def plane_second(links, blocks, how):
    z, x = links.here["z"], links.here["x"]
    return side_by_side(
        [
            how(
                links, "z", lambda h: blocks.of_z(z, h, 0), lambda p, h: blocks.of_z(p, h, 0)
            ),
            how(
                links, "x", lambda h: blocks.of_x(x, h, 1), lambda p, h: blocks.of_x(p, h, 1)
            ),
        ]
    )


def plane_scratch(rows, width):
    return [
        pltpu.VMEM((2, 2, 4, rows, width), LOW),
        pltpu.VMEM((2, 2, 2, rows, width), LOW),
        pltpu.VMEM((2, 4, rows, width), LOW),
        pltpu.VMEM((2, 2, rows, width), LOW),
        pltpu.VMEM((2, 2, rows // 2, width), LOW),
    ]


def plane_scatter(links, grad, out, near, far, middle, near_two, far_two):
    z, x = links.here["z"], links.here["x"]
    by_rows = len(grad.shape) == 4
    rows, half = middle.shape[2:]

    def block(i, j, s):
        if by_rows:
            return grad.at[i, j, :, pl.ds(s * half, half)]
        return grad.at[pl.ds(s * rows, rows), aligned((i * 4 + j) * 128, 128)]

    def window_of(ref, s):
        if by_rows:
            return ref.at[:, pl.ds(s * half, half)]
        return ref.at[pl.ds(s * rows, rows)]

    def mine(s):
        if s == 0:
            return lambda p, h: [block(2 * h + k, p, 0) for k in range(2)]
        return lambda p, h: [block(p, 2 * h + k, 1) for k in range(2)]

    yield from side_by_side(
        [
            scatter4(
                links,
                axis,
                mine(s),
                [
                    lambda h, s=s, i=i: [near.at[s, i, 2 * h + k] for k in range(2)]
                    for i in range(2)
                ],
                [[far.at[s, i, k] for k in range(2)] for i in range(2)],
            )
            for s, axis in enumerate(("x", "z"))
        ]
    )
    for s in range(2):
        for p in range(4):
            own = block(p, x, 0) if s == 0 else block(z, p, 1)

            def body(window, s=s, p=p, own=own):
                middle[s, p, window] = low(
                    full(own[window])
                    + (full(near[s, 0, p, window]) + full(near[s, 1, p, window]))
                )

            each(rows, 16, body)
    part = rows // 2
    yield from side_by_side(
        [
            scatter4(
                links,
                axis,
                lambda p, h, s=s: middle.at[s, p, pl.ds(h * part, part)],
                [lambda h, s=s, i=i: near_two.at[s, i, pl.ds(h * part, part)] for i in range(2)],
                [far_two.at[s, 0], far_two.at[s, 1]],
            )
            for s, axis in enumerate(("z", "x"))
        ]
    )
    for s, me in enumerate((z, x)):
        into = window_of(out, s)

        def body(window, s=s, me=me, into=into):
            into[window] = low(
                full(middle[s, me, window])
                + (full(near_two[s, 0, window]) + full(near_two[s, 1, window]))
            )

        each(rows, 16, body)


def small_plane(links, own, out):
    z, x = links.here["z"], links.here["x"]
    out[z, x] = own[...]
    copies = [links.send(own, out.at[z, x], "x", step) for step in (1, 2, 3)]
    yield
    for copy in copies:
        copy.wait_recv()
    copies = [links.send(out.at[z], out.at[z], "z", step) for step in (1, 2, 3)]
    yield
    for copy in copies:
        copy.wait_recv()


def small_column(links, own, out):
    core, y = links.here["core"], links.here["y"]
    out[core, y] = own[...]
    copies = [links.send(own, out.at[core, y], "y", step) for step in (1, 2, 3)]
    yield
    for copy in copies:
        copy.wait_recv()
    copy = links.send(out.at[core], out.at[core], "core")
    yield
    copy.wait_recv()


def call(kernel, name, number, copies, kept, outs, out_specs, in_specs, scratch, vmem, operands):
    return pl.pallas_call(
        kernel,
        name=name,
        out_shape=outs,
        in_specs=in_specs,
        out_specs=out_specs,
        scratch_shapes=[
            pltpu.SemaphoreType.DMA((copies,)),
            pltpu.SemaphoreType.DMA((copies,)),
            pltpu.SemaphoreType.DMA((kept,)),
        ]
        + scratch,
        compiler_params=pltpu.CompilerParams(
            collective_id=number, has_side_effects=True, vmem_limit_bytes=vmem * 2**20
        ),
    )(*operands)


def shaped(shape, kind=LOW):
    return jax.ShapeDtypeStruct(shape, kind)


def turn_rows(values, cosine, sine):
    return values * cosine + pltpu.roll(values, HD // 2, 1) * sine


def forward_kernel(
    q_weight,
    k_weight,
    v_weight,
    o_weight,
    gate_weight,
    up_weight,
    down_weight,
    tokens,
    cotangent,
    gain_one,
    gain_two,
    gains,
    seq,
    waves,
    full_qkv_out,
    full_o_out,
    full_gu,
    full_d,
    unit_out,
    two_all,
    dy_all,
    middle,
    attended,
    queries,
    keys,
    values,
    proj,
    table,
    gains_all,
    starts,
    send_sems,
    recv_sems,
    kept,
    raw_qkv,
    own_qkv,
    own_o,
    raw_gu,
    own_gu,
    x_both,
    dy_both,
    down_own,
    full_qkv,
    full_o,
    unit_all,
    seq_all,
    partial,
    two_own,
    *column,
):
    links = Links(send_sems, recv_sems)
    local = Locals(kept)
    here = links.here
    z, x, y, core = here["z"], here["x"], here["y"], here["core"]
    half = lax.rem(y, 2)
    part = lax.div(y, 2) * 2 + core
    spot = block_of(y, core)
    plane = z * 4 + x
    own_rows = x_both.shape[0] // 2
    nq, nkv = own_o.shape[0], keys.shape[1]
    nff = raw_gu.shape[1] // 2

    load_x = local.start(tokens, x_both)
    load_qkv = [
        local.start(q_weight.at[:, aligned(part * nq, nq)], raw_qkv.at[:, pl.ds(0, nq)]),
        local.start(k_weight.at[:, aligned(part * nkv, nkv)], raw_qkv.at[:, pl.ds(nq, nkv)]),
        local.start(v_weight.at[:, aligned(part * nkv, nkv)], raw_qkv.at[:, pl.ds(nq + nkv, nkv)]),
    ]
    load_o = local.start(o_weight.at[aligned(part * nq, nq)], own_o)
    load_gu = [
        local.start(gate_weight.at[:, aligned(part * nff, nff)], raw_gu.at[:, pl.ds(0, nff)]),
        local.start(up_weight.at[:, aligned(part * nff, nff)], raw_gu.at[:, pl.ds(nff, nff)]),
    ]
    load_late = [
        local.start(down_weight.at[aligned(part * nff, nff)], down_own),
        local.start(cotangent, dy_both),
    ]
    links.meet(PLANE + COLUMN)
    load_x.wait()

    base = part * 2

    def norm_one(window):
        rows = pl.ds(pl.multiple_of(half * own_rows + window.start, 16), 16)
        value = full(x_both[rows])
        unit_all[spot, window] = low(value * inverse_of(value))

    each(own_rows, 16, norm_one)
    column_one = column_gather(links, unit_all.at[spot], unit_all)
    small = [small_column(links, seq, seq_all), small_plane(links, gains, gains_all)]
    step_all([column_one] + small)
    for copy in load_qkv:
        copy.wait()

    def scale_qkv(window):
        own_qkv[window] = low(full(raw_qkv[window]) * gain_one[window])
        full_qkv[z, x, window] = own_qkv[window]

    each(own_rows, 16, scale_qkv)
    blocks_qkv, blocks_o = ByRows(full_qkv), ByColumns(full_o)
    blocks_gu, blocks_d = ByRows(full_gu), ByColumns(full_d)
    first_qkv = plane_first(links, blocks_qkv, own_qkv, straight4)
    step_all([first_qkv])
    load_o.wait()
    first_o = plane_first(links, blocks_o, own_o, straight4)
    keep_o = local.start(own_o, full_o.at[:, aligned(plane * 128, 128)])
    for copy in load_gu + load_late:
        copy.wait()

    def scale_gu(window):
        own_gu[window] = low(full(raw_gu[window]) * gain_two[window])

    each(own_rows, 16, scale_gu)
    step_all([first_o])
    first_late = [
        plane_first(links, blocks_gu, own_gu, straight4),
        plane_first(links, blocks_d, down_own, straight4),
    ]
    step_all(first_late)
    keep_gu = local.start(own_gu, full_gu.at[z, x])
    keep_d = local.start(down_own, full_d.at[:, aligned(plane * 128, 128)])
    late = [
        local.start(dy_both.at[pl.ds(i * own_rows, own_rows)], dy_all.at[base + i])
        for i in range(2)
    ]
    together([first_qkv])
    second_qkv = plane_second(links, blocks_qkv, gather4)
    step_all([second_qkv, column_one] + small)
    together(small)

    ids = full(seq_all[...])
    count_0 = jnp.sum((ids < 0.5).astype(WIDE), (0, 1))
    count_01 = jnp.sum((ids < 1.5).astype(WIDE), (0, 1))
    start_1 = jnp.sum(count_0[0:1], 1, keepdims=True)
    start_2 = jnp.sum(count_01[0:1], 1, keepdims=True)
    starts[0:4] = jnp.broadcast_to(start_1, (4, HD))
    starts[4:8] = jnp.broadcast_to(start_2, (4, HD))

    def start_of(index):
        return jnp.where(index < start_1, 0.0, jnp.where(index < start_2, start_1, start_2))

    def tables(i, carry):
        window = aligned(i * 64, 64)
        index = full(lax.broadcasted_iota(jnp.int32, (64, HD), 0) + i * 64)
        angle = (index - start_of(index)) * waves[0:1]
        table[0, window] = jnp.cos(angle)
        table[1, window] = jnp.sin(angle) * waves[1:2]
        return carry

    lax.fori_loop(0, 6, tables, 0)
    step_all([column_one, second_qkv])
    together([first_o])
    keep_o.wait()
    second_o = plane_second(links, blocks_o, gather4)
    step_all([second_o])
    lax.fori_loop(6, 12, tables, 0)
    step_all([column_one, second_qkv])
    lax.fori_loop(12, 16, tables, 0)
    together([second_qkv, column_one])
    step_all([second_o])
    together(first_late)
    keep_gu.wait()
    keep_d.wait()
    second_late = [
        plane_second(links, blocks_gu, gather4),
        plane_second(links, blocks_d, gather4),
    ]
    step_all(second_late)
    column_dy = column_fetch(
        links,
        lambda i, w: dy_both.at[
            pl.ds(pl.multiple_of(i * own_rows + w.start, w.size), w.size)
        ],
        dy_all,
        4,
    )
    step_all([column_dy])
    late += [
        local.start(full_qkv, full_qkv_out),
        local.start(unit_all, unit_out),
    ]

    gain_rows = jnp.sum(gains_all[...], (0, 1))
    q_gain, k_gain = gain_rows[0:1], gain_rows[1:2]

    def project(i, carry):
        window = aligned(i * 256, 256)
        unit = unit_all[pl.ds(2 * i, 2)].reshape(256, unit_all.shape[2])
        weights = full_qkv[...].reshape(16 * own_rows, nq + 2 * nkv)
        out = dot_nn(unit, weights)
        cosine, sine = table[0, window], table[1, window]
        for head in range(3):
            value = out[:, head * HD : (head + 1) * HD]
            proj[head, window] = value
            gain = q_gain if head < 2 else k_gain
            rotated = low(turn_rows(value * inverse_of(value) * gain, cosine, sine))
            if head < 2:
                queries[head, window] = rotated
            else:
                keys[window] = rotated
        values[window] = low(out[:, 3 * HD :])
        return carry

    lax.fori_loop(0, 4, project, 0)
    together([second_o])
    late.append(local.start(full_o, full_o_out))
    step_all([column_dy])

    def turn_done(window, total):
        rows = pl.ds(pl.multiple_of(half * own_rows + window.start, 16), 16)
        value = full(x_both[rows]) + total
        middle[window] = value
        two_own[window] = low(value * inverse_of(value))

    summed = ColumnSum(links, partial, *column, turn_done)
    for i in range(4):
        window = pl.ds(i * 256, 256)
        seen = 256 * (i + 1)
        query = jnp.concatenate([queries[0, window], queries[1, window]], 0)
        scores = dot_nt(query, keys[0:seen]) * SCALE
        row = lax.broadcasted_iota(jnp.int32, (256, 1), 0) + i * 256
        row = full(jnp.concatenate([row, row], 0))
        column_index = full(lax.broadcasted_iota(jnp.int32, (512, seen), 1))
        seen_here = (column_index <= row) & (column_index >= start_of(row))
        scores = jnp.where(seen_here, scores, -jnp.inf)
        power = jnp.exp(scores - jnp.max(scores, -1, keepdims=True))
        probs = power * (1.0 / jnp.sum(power, -1, keepdims=True))
        mixed = low(dot_nn(low(probs), values[0:seen]))
        both = jnp.concatenate([mixed[:256], mixed[256:]], 1)
        attended[window] = both
        partial[2 * i : 2 * i + 2] = low(dot_nn(both, full_o[...])).reshape(
            2, own_rows, partial.shape[2]
        )
        if i % 2:
            summed.over(i // 2)
        if i > 0:
            step_all([column_dy])
    ring = summed.ring()
    step_all([ring])
    step_all([ring])
    step_all(second_late)
    together([ring])
    late.append(local.start(two_own, two_all.at[spot]))
    column_two = column_gather(links, two_own, two_all)
    step_all([column_two])
    step_all([column_two])
    together([column_two, column_dy])
    together(second_late)
    for copy in late:
        copy.wait()
    links.drain()


def middle_kernel(
    full_gu,
    full_d,
    two_all,
    dy_all,
    middle,
    mid_all,
    grad_gu_w,
    grad_mid,
    result,
    sum_d,
    down_part,
    send_sems,
    recv_sems,
    kept,
    gu,
    down,
    two,
    dy,
    product,
    grad_gu,
    partial,
    partial_down,
    grad_d,
    dy_own,
    mid_own,
    *scratch,
):
    column, column_down = scratch[:3], scratch[3:6]
    plane_d = scratch[6:]
    links = Links(send_sems, recv_sems)
    local = Locals(kept)
    here = links.here
    spot = block_of(here["y"], here["core"])
    rows = partial.shape[1] // 2
    width = partial.shape[2]
    nff = product.shape[1]
    windows = [pl.ds(h * rows, rows) for h in range(2)]
    halves = [pl.ds(h * 8 * rows, 8 * rows) for h in range(2)]

    load_gu = local.start(full_gu, gu)
    load_two = [local.start(two_all.at[:, windows[h]], two.at[h]) for h in range(2)]
    load_d = local.start(full_d, down)
    load_dy = [local.start(dy_all.at[:, windows[h]], dy.at[h]) for h in range(2)]
    load_own = local.start(dy_all.at[spot], dy_own)
    links.meet([("x", 1), ("x", 3), ("z", 1), ("z", 3), ("y", 1), ("y", 3), ("core", 0)])

    def loop(first, last, body):
        def one(i, carry):
            body(i)
            return carry

        lax.fori_loop(first, last, one, 0)

    def units(h, first, last):
        def body(j):
            at, after = aligned(j * 256, 256), aligned(nff + j * 256, 256)
            unit = two[h].reshape(8 * rows, width)
            gate = dot_nn(unit, gu[:, :, :, at].reshape(width, 256))
            up = dot_nn(unit, gu[:, :, :, after].reshape(width, 256))
            grad = dot_nt(dy[h].reshape(8 * rows, width), down[at])
            sigmoid = 1.0 / (1.0 + jnp.exp(-gate))
            silu = gate * sigmoid
            product[halves[h], at] = low(silu * up)
            grad_gu[halves[h], at] = low(grad * up * (sigmoid * (1.0 + gate * (1.0 - sigmoid))))
            grad_gu[halves[h], after] = low(grad * silu)

        loop(first, last, body)

    def forward_part(h):
        def body(n):
            at = aligned(n * 512, 512)
            out = low(dot_nn(product[halves[h]], down[:, at]))
            partial_down[:, windows[h], at] = out.reshape(8, rows, 512)

        loop(0, width // 512, body)

    def backward_part(h, first, last):
        def body(n):
            out = low(dot_nt(grad_gu[halves[h]], gu[n].reshape(512, 2 * nff)))
            partial[:, windows[h], aligned(n * 512, 512)] = out.reshape(8, rows, 512)

        loop(first, last, body)

    def here_rows(h, window):
        return pl.ds(pl.multiple_of(h * rows + window.start, 16), 16)

    def done(h):
        def body(window, total):
            at = here_rows(h, window)
            value = middle[at]
            inverse = inverse_of(value)
            value = full(dy_own[at]) + norm_back(total, value * inverse, inverse)
            grad_mid[at] = value
            mid_own[at] = low(value)

        return body

    def done_down(h):
        def body(window, total):
            at = here_rows(h, window)
            result[at] = low(middle[at] + total)

        return body

    def column_sum(source, parts, h, body):
        passed, near, far = parts
        return ColumnSum(
            links,
            source.at[:, windows[h]],
            passed.at[:, windows[h]],
            near.at[:, windows[h]],
            far.at[:, pl.ds(h * rows // 2, rows // 2)],
            body(h),
        )

    sums = [column_sum(partial, column, h, done) for h in range(2)]
    sum_down = column_sum(partial_down, column_down, 0, done_down)
    rings = [one.ring() for one in sums]
    ring_down = sum_down.ring()
    gathers = [
        column_gather(links, mid_own.at[windows[h]], mid_all.at[:, windows[h]]) for h in range(2)
    ]
    load_gu.wait()
    load_two[0].wait()
    load_d.wait()
    load_dy[0].wait()
    load_own.wait()
    def down_grad(i):
        at = aligned(i * 256, 256)
        grad_d[at] = low(dot_tn(product[:, at], dy[...].reshape(16 * rows, width)))

    def gate_up_grad(i):
        acts = two[:, :, :, aligned(i * 512, 512)].reshape(16 * rows, 512)
        gu[i] = low(dot_tn(acts, grad_gu[...])).reshape(4, 128, 2 * nff)

    units(0, 0, nff // 256)
    forward_part(0)
    sum_down.over(0)
    sum_down.over(1)
    backward_part(0, 0, 2)
    step_all([ring_down])
    backward_part(0, 2, 4)
    sums[0].over(0)
    sums[0].over(1)
    load_two[1].wait()
    load_dy[1].wait()
    units(1, 0, 1)
    step_all([rings[0]])
    units(1, 1, nff // 256)
    step_all([ring_down, rings[0]])
    loop(0, nff // 256, down_grad)
    scatter_d = plane_scatter(links, grad_d, sum_d, *plane_d)
    step_all([scatter_d])
    together([rings[0]])
    step_all([gathers[0]])
    step_all([gathers[0]])
    backward_part(1, 0, 4)
    sums[1].over(0)
    sums[1].over(1)
    together([ring_down])
    loop(0, 2, gate_up_grad)
    step_all([rings[1], gathers[0]])
    loop(2, 4, gate_up_grad)
    keep_w = local.start(gu, grad_gu_w)
    step_all([scatter_d, rings[1], gathers[0]])
    forward_part(1)
    keep_down = local.start(partial_down.at[:, windows[1]], down_part)
    step_all([scatter_d])
    together([rings[1]])
    step_all([gathers[1]])
    step_all([gathers[1]])
    step_all([scatter_d])
    keep_mid = local.start(mid_own, mid_all.at[spot])
    step_all([gathers[1], gathers[0], scatter_d])
    together([gathers[1], gathers[0], scatter_d])
    for copy in (keep_w, keep_mid, keep_down):
        copy.wait()
    links.drain()


def end_kernel(
    q_weight,
    k_weight,
    v_weight,
    gate_weight,
    up_weight,
    tokens,
    full_qkv,
    full_o,
    unit_all,
    mid_all,
    grad_gu_w,
    attended,
    queries,
    keys,
    values,
    proj,
    table,
    gains_all,
    starts,
    gain_one,
    gain_two,
    grad_mid,
    middle,
    result,
    sum_d,
    down_part,
    grad_x,
    out_rows,
    all_qkv,
    all_o,
    all_gu,
    all_d,
    sums_out,
    send_sems,
    recv_sems,
    kept,
    weights,
    weight_o,
    unit,
    mid,
    grad_gu,
    grad_o,
    grad_qkv_w,
    raw_qkv,
    raw_gu,
    x_own,
    grad_att,
    dk,
    dv,
    grad_qkv,
    sum_gu,
    sum_qkv,
    own_o,
    own_gu,
    own_qkv,
    small,
    small_all,
    row,
    row_all,
    turned,
    x_pair,
    row_pair,
    part_down,
    *scratch,
):
    column_parts, column_down = scratch[:3], scratch[3:6]
    plane_gu, plane_o, plane_qkv = scratch[6:11], scratch[11:16], scratch[16:]
    links = Links(send_sems, recv_sems)
    local = Locals(kept)
    here = links.here
    y, core = here["y"], here["core"]
    half = lax.rem(y, 2)
    part = lax.div(y, 2) * 2 + core
    part_other = lax.div(lax.rem(y + 2, 4), 2) * 2 + core
    rows, width = x_own.shape
    nq, nkv = own_o.shape[0], keys.shape[1]
    nff = sum_gu.shape[1] // 2

    load_mid = local.start(mid_all, mid)
    load_o = local.start(full_o, weight_o)
    load_gu = local.start(grad_gu_w, grad_gu)
    load_down = local.start(down_part, part_down)
    loads = [
        local.start(full_qkv, weights),
        local.start(unit_all, unit),
        local.start(tokens.at[aligned(half * rows, rows)], x_own),
        local.start(q_weight.at[:, aligned(part * nq, nq)], raw_qkv.at[:, pl.ds(0, nq)]),
        local.start(k_weight.at[:, aligned(part * nkv, nkv)], raw_qkv.at[:, pl.ds(nq, nkv)]),
        local.start(v_weight.at[:, aligned(part * nkv, nkv)], raw_qkv.at[:, pl.ds(nq + nkv, nkv)]),
        local.start(gate_weight.at[:, aligned(part * nff, nff)], raw_gu.at[:, pl.ds(0, nff)]),
        local.start(up_weight.at[:, aligned(part * nff, nff)], raw_gu.at[:, pl.ds(nff, nff)]),
    ]
    links.meet(PLANE + COLUMN)

    def share(own, out):
        across = links.send(own, out.at[part], "y", 2)
        beside = links.send(own, out.at[part], "core")
        keep = local.start(own, out.at[part])
        yield
        across.wait_recv()
        second = links.send(out.at[part_other], out.at[part_other], "core")
        yield
        beside.wait_recv()
        second.wait_recv()
        keep.wait()

    def exchange(own, out):
        copy = links.send(own, out.at[half], "pair")
        keep = local.start(own, out.at[half])
        yield
        copy.wait_recv()
        keep.wait()

    def done_down(window, total):
        late = pl.ds(pl.multiple_of(rows // 2 + window.start, 16), 16)
        row_pair[window] = result[window]
        row_pair[late] = low(middle[late] + total)

    def done_one(window, total):
        value = full(x_own[window])
        inverse = inverse_of(value)
        x_pair[window] = low(grad_mid[window] + norm_back(total, value * inverse, inverse))

    def scale(into, total, raw, gain, spot):
        def body(window):
            into[window] = low(full(total[window]) * gain[window])
            part_sum = jnp.sum(full(total[window]) * full(raw[window]), 1, keepdims=True)
            turned[spot, window] = jnp.broadcast_to(part_sum, (16, HD))

        each(rows, 16, body)

    load_mid.wait()
    load_o.wait()

    def attended_grad(i, carry):
        window = aligned(i * 256, 256)
        out = low(dot_nt(mid[pl.ds(2 * i, 2)].reshape(256, width), weight_o[...]))
        grad_att[0, window] = out[:, :HD]
        grad_att[1, window] = out[:, HD:]
        return carry

    def gu_job():
        yield from plane_scatter(links, grad_gu, sum_gu, *plane_gu)
        scale(own_gu, sum_gu, raw_gu, gain_two, 1)
        yield from share(own_gu, all_gu)

    def o_job():
        yield from plane_scatter(links, grad_o, own_o, *plane_o)
        yield from share(own_o, all_o)

    def qkv_job():
        yield from plane_scatter(links, grad_qkv_w, sum_qkv, *plane_qkv)
        scale(own_qkv, sum_qkv, raw_qkv, gain_one, 0)
        yield from share(own_qkv, all_qkv)

    job_gu, job_o, job_qkv = gu_job(), o_job(), qkv_job()
    sum_down = ColumnSum(links, part_down, *column_down, done_down)
    ring_down = sum_down.ring()
    share_d = share(sum_d, all_d)
    load_gu.wait()
    step_all([job_gu])
    load_down.wait()
    sum_down.over(0)
    sum_down.over(1)
    lax.fori_loop(0, 4, attended_grad, 0)

    gain_rows = jnp.sum(gains_all[...], (0, 1))
    q_gain, k_gain = gain_rows[0:1], gain_rows[1:2]
    start_1, start_2 = starts[0:1, 0:1], starts[4:5, 0:1]
    dk[...] = jnp.zeros_like(dk)
    dv[...] = jnp.zeros_like(dv)
    small[...] = jnp.zeros_like(small)

    def project_back(grad, head, window, gain):
        cosine, sine = table[0, window], table[1, window]
        back = grad * cosine - pltpu.roll(grad, HD // 2, 1) * sine
        value = proj[head, window]
        inverse = inverse_of(value)
        scaled = value * inverse
        spot = 0 if head < 2 else 1
        small[spot : spot + 1] += jnp.sum(back * scaled, 0, keepdims=True)
        return low(norm_back(back * gain, scaled, inverse))

    for i in range(4):
        window = pl.ds(i * 256, 256)
        seen = 256 * (i + 1)
        query = jnp.concatenate([queries[0, window], queries[1, window]], 0)
        grad = jnp.concatenate([grad_att[0, window], grad_att[1, window]], 0)
        key, value = keys[0:seen], values[0:seen]
        scores = dot_nt(key, query) * SCALE
        column = lax.broadcasted_iota(jnp.int32, (1, 256), 1) + i * 256
        column = full(jnp.concatenate([column, column], 1))
        start = jnp.where(
            column < start_1, 0.0, jnp.where(column < start_2, start_1, start_2)
        )
        index = full(lax.broadcasted_iota(jnp.int32, (seen, 512), 0))
        scores = jnp.where((index <= column) & (index >= start), scores, -jnp.inf)
        power = jnp.exp(scores - jnp.max(scores, 0, keepdims=True))
        probs = power * (1.0 / jnp.sum(power, 0, keepdims=True))
        grad_probs = dot_nt(value, grad)
        inner = jnp.sum(probs * grad_probs, 0, keepdims=True)
        grad_scores = low(probs * (grad_probs - inner))
        dv[0:seen] += dot_nn(low(probs), grad)
        dk[0:seen] += dot_nn(grad_scores, query)
        dq = dot_tn(key, grad_scores).T * SCALE
        for head in range(2):
            grad_qkv[window, head * HD : (head + 1) * HD] = project_back(
                dq[head * 256 : (head + 1) * 256], head, window, q_gain
            )
        if i == 0:
            step_all([ring_down])
        if i == 2:
            step_all([ring_down, share_d])

    def keys_back(i, carry):
        window = aligned(i * 256, 256)
        grad_qkv[window, nq : nq + nkv] = project_back(dk[window] * SCALE, 2, window, k_gain)
        grad_qkv[window, nq + nkv :] = low(dv[window])
        return carry

    lax.fori_loop(0, 4, keys_back, 0)
    small_job = small_plane(links, small, small_all)
    step_all([small_job])

    def unit_grad(i, carry):
        out = low(
            dot_nt(
                grad_qkv[aligned(i * 256, 256)], weights[...].reshape(width, nq + 2 * nkv)
            )
        )
        mid[pl.ds(2 * i, 2)] = out.reshape(2, rows, width)
        return carry

    for copy in loads:
        copy.wait()
    sum_one = ColumnSum(links, mid, *column_parts, done_one)
    grad_o[...] = low(dot_tn(attended[...], mid[...].reshape(8 * rows, width)))
    step_all([job_o])
    together([ring_down])
    pair_rows = exchange(row_pair, out_rows)
    step_all([pair_rows])
    lax.fori_loop(0, 2, unit_grad, 0)
    sum_one.over(0)
    lax.fori_loop(2, 4, unit_grad, 0)
    sum_one.over(1)
    step_all([job_gu])
    ring_one = sum_one.ring()
    step_all([ring_one])

    def weight_grad(i, carry):
        at = aligned(i * 512, 512)
        out = dot_tn(unit[:, :, at].reshape(8 * rows, 512), grad_qkv[...])
        grad_qkv_w[i] = low(out).reshape(4, rows, nq + 2 * nkv)
        return carry

    lax.fori_loop(0, 4, weight_grad, 0)
    step_all([job_qkv, job_gu, job_o, small_job])
    step_all([share_d, job_o])
    step_all([ring_one])
    step_all([job_gu, job_qkv, job_o])
    step_all([job_gu, job_qkv, small_job])
    together([ring_one])
    pair_x = exchange(x_pair, grad_x)
    step_all([pair_x, job_gu, job_qkv])
    step_all([job_gu, job_qkv])
    row[0:2] = jnp.sum(small_all[:, :, 0:2], (0, 1))
    row[2:3] = turned[0].T[0:1]
    row[3:4] = turned[1].T[0:1]
    row[4:8] = jnp.zeros((4, HD), WIDE)
    row_job = small_column(links, row, row_all)
    step_all([row_job, job_o, job_gu, job_qkv])
    together([job_o, job_gu, job_qkv, row_job, share_d, pair_rows])
    together([pair_x])
    sums_out[...] = jnp.sum(row_all[...], (0, 1))
    links.drain()


def widen_kernel(
    out_rows,
    grad_x,
    all_qkv,
    all_o,
    all_gu,
    all_d,
    out_final,
    x_final,
    q_final,
    k_final,
    v_final,
    o_final,
    gate_final,
    up_final,
    d_final,
    rows_low,
    x_low,
    qkv_low,
    o_low,
    gu_low,
    d_low,
    x_wide,
    q_wide,
    k_wide,
    v_wide,
    o_wide,
    gate_wide,
    up_wide,
    d_wide,
    kept,
):
    local = Locals(kept)
    halves, rows, _ = x_low.shape
    parts, rows_w = gu_low.shape[:2]
    nff = gu_low.shape[2] // 2
    load_gu = local.start(all_gu, gu_low)
    load_d = local.start(all_d, d_low)
    load_qkv = local.start(all_qkv, qkv_low)
    load_o = local.start(all_o, o_low)
    load_x = local.start(grad_x, x_low)
    load_rows = local.start(out_rows, rows_low)
    nq = q_wide.shape[1] // parts
    nkv = k_wide.shape[1] // parts
    stores = []

    def side_by_side_parts(source, start, size, into, final):
        for c in range(parts):

            def body(window, c=c):
                into[window, c * size : (c + 1) * size] = full(
                    source[c, window, start : start + size]
                )

            each(rows_w, 32, body)
        stores.append(local.start(into, final))

    def stacked(source, into, final, step):
        count, size = source.shape[:2]
        for c in range(count):

            def body(window, c=c):
                into[c, window] = full(source[c, window])

            each(size, step, body)
            stores.append(local.start(into.at[c], final.at[pl.ds(c * size, size)]))

    load_gu.wait()
    side_by_side_parts(gu_low, 0, nff, gate_wide, gate_final)
    side_by_side_parts(gu_low, nff, nff, up_wide, up_final)
    load_d.wait()
    stacked(d_low, d_wide, d_final, 128)
    load_x.wait()
    stacked(x_low, x_wide, x_final, 16)
    load_rows.wait()
    for c in range(halves):
        stores.append(local.start(rows_low.at[c], out_final.at[pl.ds(c * rows, rows)]))
    load_qkv.wait()
    side_by_side_parts(qkv_low, 0, nq, q_wide, q_final)
    side_by_side_parts(qkv_low, nq, nkv, k_wide, k_final)
    side_by_side_parts(qkv_low, nq + nkv, nkv, v_wide, v_final)
    load_o.wait()
    stacked(o_low, o_wide, o_final, 128)
    for copy in stores:
        copy.wait()


def per_device(
    tokens,
    segments,
    attn_gain,
    q_weight,
    k_weight,
    v_weight,
    q_gain,
    k_gain,
    o_weight,
    mlp_gain,
    gate_weight,
    up_weight,
    down_weight,
    cotangent,
):
    parts, halves = lax.axis_size("ctx"), lax.axis_size("tp")
    half = lax.axis_index("tp")
    rows_here, width = tokens.shape
    seq_len = rows_here * parts
    own_rows = rows_here // halves
    blocks = parts * halves

    def own(array):
        return lax.dynamic_slice_in_dim(array, half * own_rows, own_rows, 0)

    attn_gain_f = jnp.broadcast_to(full(attn_gain)[:, None], (attn_gain.shape[0], 1))
    mlp_gain_f = jnp.broadcast_to(full(mlp_gain)[:, None], (mlp_gain.shape[0], 1))
    rows_w = q_weight.shape[0]
    nq, nkv, nff = q_weight.shape[1] // parts, k_weight.shape[1] // parts, gate_weight.shape[1] // parts
    na, nb = nq + 2 * nkv, 2 * nff
    few = q_gain.shape[0]
    gains = lax.dynamic_update_slice(
        jnp.zeros((8, HD), WIDE),
        full(jnp.stack([q_gain, k_gain])),
        (0, lax.axis_index("fsdp") * few),
    )
    seq = jnp.broadcast_to(own(segments)[None, :], (8, own_rows))
    frequency = jnp.power(rope_base, -2.0 * jnp.arange(HD // 2, dtype=WIDE) / HD)
    ones = jnp.ones((HD // 2,), WIDE)
    waves = jnp.zeros((8, HD), WIDE).at[0].set(jnp.tile(frequency, 2))
    waves = waves.at[1].set(jnp.concatenate([-ones, ones]))

    (
        full_qkv,
        full_o,
        full_gu,
        full_d,
        unit_all,
        two_all,
        dy_all,
        middle,
        attended,
        queries,
        keys,
        values,
        proj,
        table,
        gains_all,
        starts,
    ) = call(
        forward_kernel,
        "forward",
        0,
        176,
        24,
        (
            shaped((4, 4, rows_w, na)),
            shaped((nq, width)),
            shaped((4, 4, rows_w, nb)),
            shaped((nff, width)),
            shaped((blocks, own_rows, width)),
            shaped((blocks, own_rows, width)),
            shaped((blocks, own_rows, width)),
            shaped((own_rows, width), WIDE),
            shaped((seq_len, nq)),
            shaped((2, seq_len, HD)),
            shaped((seq_len, HD)),
            shaped((seq_len, HD)),
            shaped((3, seq_len, HD), WIDE),
            shaped((2, seq_len, HD), WIDE),
            shaped((4, 4, 8, HD), WIDE),
            shaped((8, HD), WIDE),
        ),
        [HBM] * 7 + [VMEM] * 9,
        [HBM] * 9 + [VMEM] * 5,
        [
            pltpu.VMEM((rows_w, na), LOW),
            pltpu.VMEM((rows_w, na), LOW),
            pltpu.VMEM((nq, rows_w), LOW),
            pltpu.VMEM((rows_w, nb), LOW),
            pltpu.VMEM((rows_w, nb), LOW),
            pltpu.VMEM((rows_here, width), LOW),
            pltpu.VMEM((rows_here, width), LOW),
            pltpu.VMEM((nff, rows_w), LOW),
            pltpu.VMEM((4, 4, rows_w, na), LOW),
            pltpu.VMEM((nq, width), LOW),
            pltpu.VMEM((blocks, own_rows, width), LOW),
            pltpu.VMEM((2, 4, 8, own_rows), jnp.int32),
            pltpu.VMEM((blocks, own_rows, width), LOW),
            pltpu.VMEM((own_rows, width), LOW),
        ]
        + column_scratch(own_rows),
        58,
        (
            q_weight,
            k_weight,
            v_weight,
            o_weight,
            gate_weight,
            up_weight,
            down_weight,
            tokens,
            cotangent,
            attn_gain_f,
            mlp_gain_f,
            gains,
            seq,
            waves,
        ),
    )

    mid_all, grad_gu_w, grad_mid, result, sum_d, down_part = call(
        middle_kernel,
        "middle",
        1,
        144,
        12,
        (
            shaped((blocks, own_rows, width)),
            shaped((4, 4, rows_w, nb)),
            shaped((own_rows, width), WIDE),
            shaped((own_rows, width)),
            shaped((nff, rows_w)),
            shaped((blocks, own_rows // 2, width)),
        ),
        [HBM] * 2 + [VMEM] * 3 + [HBM],
        [HBM] * 4 + [VMEM],
        [
            pltpu.VMEM((4, 4, rows_w, nb), LOW),
            pltpu.VMEM((nff, width), LOW),
            pltpu.VMEM((2, blocks, own_rows // 2, width), LOW),
            pltpu.VMEM((2, blocks, own_rows // 2, width), LOW),
            pltpu.VMEM((seq_len, nff), LOW),
            pltpu.VMEM((seq_len, nb), LOW),
            pltpu.VMEM((blocks, own_rows, width), LOW),
            pltpu.VMEM((blocks, own_rows, width), LOW),
            pltpu.VMEM((nff, width), LOW),
            pltpu.VMEM((own_rows, width), LOW),
            pltpu.VMEM((own_rows, width), LOW),
        ]
        + column_scratch(own_rows)
        + column_scratch(own_rows // 2)
        + plane_scratch(nff // 2, rows_w),
        62,
        (full_gu, full_d, two_all, dy_all, middle),
    )

    grad_x, out_rows, all_qkv, all_o, all_gu, all_d, sums = call(
        end_kernel,
        "end",
        2,
        160,
        40,
        (
            shaped((halves, own_rows, width)),
            shaped((halves, own_rows, width)),
            shaped((parts, rows_w, na)),
            shaped((parts, nq, rows_w)),
            shaped((parts, rows_w, nb)),
            shaped((parts, nff, rows_w)),
            shaped((8, HD), WIDE),
        ),
        [HBM] * 6 + [VMEM],
        [HBM] * 11 + [VMEM] * 14 + [HBM],
        [
            pltpu.VMEM((4, 4, rows_w, na), LOW),
            pltpu.VMEM((nq, width), LOW),
            pltpu.VMEM((blocks, own_rows, width), LOW),
            pltpu.VMEM((blocks, own_rows, width), LOW),
            pltpu.VMEM((4, 4, rows_w, nb), LOW),
            pltpu.VMEM((nq, width), LOW),
            pltpu.VMEM((4, 4, rows_w, na), LOW),
            pltpu.VMEM((rows_w, na), LOW),
            pltpu.VMEM((rows_w, nb), LOW),
            pltpu.VMEM((own_rows, width), LOW),
            pltpu.VMEM((2, seq_len, HD), LOW),
            pltpu.VMEM((seq_len, HD), WIDE),
            pltpu.VMEM((seq_len, HD), WIDE),
            pltpu.VMEM((seq_len, na), LOW),
            pltpu.VMEM((rows_w, nb), LOW),
            pltpu.VMEM((rows_w, na), LOW),
            pltpu.VMEM((nq, rows_w), LOW),
            pltpu.VMEM((rows_w, nb), LOW),
            pltpu.VMEM((rows_w, na), LOW),
            pltpu.VMEM((8, HD), WIDE),
            pltpu.VMEM((4, 4, 8, HD), WIDE),
            pltpu.VMEM((8, HD), WIDE),
            pltpu.VMEM((2, 4, 8, HD), WIDE),
            pltpu.VMEM((2, rows_w, HD), WIDE),
            pltpu.VMEM((own_rows, width), LOW),
            pltpu.VMEM((own_rows, width), LOW),
            pltpu.VMEM((blocks, own_rows // 2, width), LOW),
        ]
        + column_scratch(own_rows)
        + column_scratch(own_rows // 2)
        + plane_scratch(rows_w, nb // 2)
        + plane_scratch(nq // 2, rows_w)
        + plane_scratch(rows_w, na // 2),
        62,
        (
            q_weight,
            k_weight,
            v_weight,
            gate_weight,
            up_weight,
            tokens,
            full_qkv,
            full_o,
            unit_all,
            mid_all,
            grad_gu_w,
            attended,
            queries,
            keys,
            values,
            proj,
            table,
            gains_all,
            starts,
            attn_gain_f,
            mlp_gain_f,
            grad_mid,
            middle,
            result,
            sum_d,
            down_part,
        ),
    )

    (
        out_final,
        x_final,
        q_final,
        k_final,
        v_final,
        o_final,
        gate_final,
        up_final,
        d_final,
    ) = pl.pallas_call(
        widen_kernel,
        name="widen",
        out_shape=(
            shaped((rows_here, width)),
            shaped((rows_here, width), WIDE),
            shaped(q_weight.shape, WIDE),
            shaped(k_weight.shape, WIDE),
            shaped(v_weight.shape, WIDE),
            shaped(o_weight.shape, WIDE),
            shaped(gate_weight.shape, WIDE),
            shaped(up_weight.shape, WIDE),
            shaped(down_weight.shape, WIDE),
        ),
        in_specs=[HBM] * 6,
        out_specs=[HBM] * 9,
        scratch_shapes=[
            pltpu.VMEM((halves, own_rows, width), LOW),
            pltpu.VMEM((halves, own_rows, width), LOW),
            pltpu.VMEM((parts, rows_w, na), LOW),
            pltpu.VMEM((parts, nq, rows_w), LOW),
            pltpu.VMEM((parts, rows_w, nb), LOW),
            pltpu.VMEM((parts, nff, rows_w), LOW),
            pltpu.VMEM((halves, own_rows, width), WIDE),
            pltpu.VMEM(q_weight.shape, WIDE),
            pltpu.VMEM(k_weight.shape, WIDE),
            pltpu.VMEM(v_weight.shape, WIDE),
            pltpu.VMEM((parts, nq, rows_w), WIDE),
            pltpu.VMEM(gate_weight.shape, WIDE),
            pltpu.VMEM(up_weight.shape, WIDE),
            pltpu.VMEM((parts, nff, rows_w), WIDE),
            pltpu.SemaphoreType.DMA((40,)),
        ],
        compiler_params=pltpu.CompilerParams(vmem_limit_bytes=60 * 2**20),
    )(out_rows, grad_x, all_qkv, all_o, all_gu, all_d)
    sum_qk = lax.dynamic_slice_in_dim(sums[:2], lax.axis_index("fsdp") * few, few, 1)
    return (
        out_final,
        x_final,
        sums[2],
        q_final,
        k_final,
        v_final,
        sum_qk[0],
        sum_qk[1],
        o_final,
        sums[3],
        gate_final,
        up_final,
        d_final,
    )


def solution(mesh):
    weight = P("fsdp", "tp")
    turned = P("tp", "fsdp")
    acts = P(("fsdp", "ctx"), None)
    gain = P("fsdp")
    return jax.shard_map(
        per_device,
        mesh=mesh,
        in_specs=(
            acts,
            P(("fsdp", "ctx")),
            gain,
            weight,
            weight,
            weight,
            gain,
            gain,
            turned,
            gain,
            weight,
            weight,
            turned,
            acts,
        ),
        out_specs=(
            acts,
            acts,
            gain,
            weight,
            weight,
            weight,
            gain,
            gain,
            turned,
            gain,
            weight,
            weight,
            turned,
        ),
        check_vma=False,
    )
```

```python
import jax
import jax.numpy as jnp
import numpy as np
from jax import lax
from jax.experimental import pallas as pl
from jax.experimental.pallas import tpu as pltpu
from jax.sharding import PartitionSpec as P

HD = 128
MESH = pl.DeviceIdType.MESH
HBM = pl.BlockSpec(memory_space=pl.ANY)
VMEM = pl.BlockSpec(memory_space=pltpu.VMEM)
LOW = jnp.bfloat16
WIDE = jnp.float32
SCALE = HD ** (-0.5)


epsilon = 1e-06
rope_base = 1000000.0


def inverse_of(values_in):
    return lax.rsqrt(jnp.mean(values_in * values_in, -1, keepdims=True) + epsilon)


def norm_back(grad_in, unit_in, inverse):
    return inverse * (grad_in - unit_in * jnp.mean(grad_in * unit_in, -1, keepdims=True))


def dot_nn(left, right):
    return jnp.dot(left, right, preferred_element_type=WIDE)


def dot_tn(left, right):
    return lax.dot_general(left, right, (((0,), (0,)), ((), ())), preferred_element_type=WIDE)


def dot_nt(left, right):
    return lax.dot_general(left, right, (((1,), (1,)), ((), ())), preferred_element_type=WIDE)


def low(values_in):
    return values_in.astype(LOW)


def full(values_in):
    return values_in.astype(WIDE)


def place():
    plane = lax.axis_index("fsdp")
    part = lax.axis_index("ctx")
    half = lax.axis_index("tp")
    return {
        "z": lax.div(plane, 4),
        "x": lax.rem(plane, 4),
        "y": lax.div(part, 2) * 2 + half,
        "core": lax.rem(part, 2),
    }


def device(where):
    return (
        where["z"] * 4 + where["x"],
        lax.div(where["y"], 2) * 2 + where["core"],
        lax.rem(where["y"], 2),
    )


def moved(here, axis, step):
    there = dict(here)
    if axis == "pair":
        there["y"] = here["y"] + 1 - 2 * lax.rem(here["y"], 2)
    elif axis == "cross":
        there["y"] = 3 - here["y"]
    elif axis == "core":
        there["core"] = 1 - here["core"]
    else:
        there[axis] = lax.rem(here[axis] + step, 4)
    return there


def block_of(y, core):
    return lax.div(y, 2) * 4 + core * 2 + lax.rem(y, 2)


class Group:
    def __init__(self, copies):
        self.copies = copies

    def wait_recv(self):
        for copy in self.copies:
            copy.wait_recv()


class Links:
    def __init__(self, send_sems, recv_sems):
        self.here = place()
        self.send_sems, self.recv_sems = send_sems, recv_sems
        self.started = []

    def meet(self, peers):
        barrier = pltpu.get_barrier_semaphore()
        for axis, step in peers:
            pl.semaphore_signal(
                barrier,
                inc=1,
                device_id=device(moved(self.here, axis, step)),
                device_id_type=MESH,
            )
        pl.semaphore_wait(barrier, len(peers))

    def send(self, src, dst, axis, step=0):
        if isinstance(src, list):
            return Group([self.send(a, b, axis, step) for a, b in zip(src, dst)])
        spot = len(self.started)
        assert spot < self.send_sems.shape[0]
        copy = pltpu.make_async_remote_copy(
            src_ref=src,
            dst_ref=dst,
            send_sem=self.send_sems.at[spot],
            recv_sem=self.recv_sems.at[spot],
            device_id=device(moved(self.here, axis, step)),
            device_id_type=MESH,
        )
        copy.start()
        self.started.append(copy)
        return copy

    def drain(self):
        for copy in self.started:
            copy.wait_send()


class Locals:
    def __init__(self, sems):
        self.sems = sems
        self.count = 0

    def start(self, src, dst):
        assert self.count < self.sems.shape[0]
        copy = pltpu.make_async_copy(src, dst, self.sems.at[self.count])
        self.count += 1
        copy.start()
        return copy


PLANE = [("x", 1), ("x", 2), ("x", 3), ("z", 1), ("z", 2), ("z", 3)]
COLUMN = [("y", 1), ("y", 2), ("y", 3), ("core", 0)]


def step_all(jobs):
    left = []
    for job in jobs:
        try:
            next(job)
            left.append(job)
        except StopIteration:
            pass
    return left


def together(jobs):
    jobs = list(jobs)
    while jobs:
        jobs = step_all(jobs)


def side_by_side(jobs):
    jobs = list(jobs)
    while jobs:
        jobs = step_all(jobs)
        if jobs:
            yield


def each(count, step, body):
    def one(i, carry):
        body(pl.ds(pl.multiple_of(i * step, step), step))
        return carry

    lax.fori_loop(0, count // step, one, 0)


def aligned(start, size):
    return pl.ds(pl.multiple_of(start, size), size)


def add_rows(into, first, second):
    if isinstance(into, list):
        for refs in zip(into, first, second):
            add_rows(*refs)
        return
    lead, rows = into.shape[:-2], into.shape[-2]

    def add(spot):
        def body(window):
            spots = spot + (window,)
            into[spots] = first[spots] + second[spots]

        return body

    if not lead:
        each(rows, 16, add(()))
    else:
        for i in range(lead[0]):
            each(rows, 16, add((i,)))


def gather4(links, axis, own, block, arrived=None):
    me = links.here[axis]
    before, after, far = lax.rem(me + 3, 4), lax.rem(me + 1, 4), lax.rem(me + 2, 4)
    arrived = arrived or (lambda spot, side: None)
    up, down = {}, {}
    up[0] = links.send(own(0), block(me, 0), axis, 1)
    down[1] = links.send(own(1), block(me, 1), axis, 3)
    up[1] = links.send(own(1), block(me, 1), axis, 1)
    down[0] = links.send(own(0), block(me, 0), axis, 3)
    yield
    up[0].wait_recv()
    up_far = links.send(block(before, 0), block(before, 0), axis, 1)
    arrived(before, 0)
    down[1].wait_recv()
    down_far = links.send(block(after, 1), block(after, 1), axis, 3)
    arrived(after, 1)
    yield
    up[1].wait_recv()
    arrived(before, 1)
    down[0].wait_recv()
    arrived(after, 0)
    yield
    up_far.wait_recv()
    arrived(far, 0)
    down_far.wait_recv()
    arrived(far, 1)


def straight4(links, axis, own, block):
    me = links.here[axis]
    copies = [
        links.send(own(h), block(me, h), axis, step) for step in (2, 1, 3) for h in range(2)
    ]
    yield
    for copy in copies:
        copy.wait_recv()


def scatter4(links, axis, mine, near, far):
    me = links.here[axis]
    before, after, beyond = lax.rem(me + 3, 4), lax.rem(me + 1, 4), lax.rem(me + 2, 4)
    up_far = links.send(mine(beyond, 0), far[0], axis, 1)
    down_far = links.send(mine(beyond, 1), far[1], axis, 3)
    up_one = links.send(mine(after, 1), near[0](1), axis, 1)
    down_one = links.send(mine(before, 0), near[1](0), axis, 3)
    yield
    up_far.wait_recv()
    add_rows(far[0], far[0], mine(after, 0))
    up_two = links.send(far[0], near[0](0), axis, 1)
    down_far.wait_recv()
    add_rows(far[1], far[1], mine(before, 1))
    down_two = links.send(far[1], near[1](1), axis, 3)
    yield
    up_one.wait_recv()
    down_one.wait_recv()
    up_two.wait_recv()
    down_two.wait_recv()


def column_gather(links, own_ref, out):
    here = links.here
    rows = out.shape[1] // 2
    shared = []

    def own(h):
        return own_ref.at[pl.ds(h * rows, rows)]

    def block(p, h):
        return out.at[block_of(p, here["core"]), pl.ds(h * rows, rows)]

    def arrived(p, h):
        shared.append(links.send(block(p, h), block(p, h), "core"))

    ring = gather4(links, "y", own, block, arrived)
    next(ring)
    for h in range(2):
        shared.append(links.send(own(h), block(here["y"], h), "core"))
    yield
    for _ in ring:
        yield
    yield
    for copy in shared:
        copy.wait_recv()


def column_fetch(links, own, out, pieces):
    here = links.here
    y, core = here["y"], here["core"]
    y_lo = lax.rem(y, 2)
    rows = out.shape[1] // pieces
    spots = [pl.ds(q * rows, rows) for q in range(pieces)]
    spot, twin = block_of(y, core), block_of(y + 1 - 2 * y_lo, core)
    first, second = block_of(3 - y, core), block_of(2 - y + 2 * y_lo, core)
    across = [links.send(own(y_lo, w), out.at[spot, w], "cross") for w in spots]
    shared = [
        links.send(own(y_lo, pl.ds(0, out.shape[1])), out.at[spot], "core"),
        links.send(own(1 - y_lo, pl.ds(0, out.shape[1])), out.at[twin], "core"),
    ]
    passed = []
    for copy, w in zip(across, spots):
        yield
        copy.wait_recv()
        passed.append(links.send(out.at[first, w], out.at[first, w], "pair"))
        shared.append(links.send(out.at[first, w], out.at[first, w], "core"))
    for copy, w in zip(passed, spots):
        yield
        copy.wait_recv()
        shared.append(links.send(out.at[second, w], out.at[second, w], "core"))
    yield
    for copy in shared:
        copy.wait_recv()


class ColumnSum:
    def __init__(self, links, partial, passed, near, far, done):
        self.links, self.partial, self.done = links, partial, done
        self.passed, self.near, self.far = passed, near, far
        self.copies = {}

    def over(self, y_hi):
        core = self.links.here["core"]
        for y in (2 * y_hi, 2 * y_hi + 1):
            self.copies[y] = self.links.send(
                self.partial.at[block_of(y, 1 - core)], self.passed.at[y], "core"
            )

    def ring(self):
        links, partial, passed, near, far = (
            self.links,
            self.partial,
            self.passed,
            self.near,
            self.far,
        )
        core, me = links.here["core"], links.here["y"]
        before, after, beyond = lax.rem(me + 3, 4), lax.rem(me + 1, 4), lax.rem(me + 2, 4)
        rows = partial.shape[1] // 2

        def mine(p, h):
            return passed.at[p, pl.ds(h * rows, rows)]

        def add(p, h):
            add_rows(mine(p, h), mine(p, h), partial.at[block_of(p, core), pl.ds(h * rows, rows)])

        for y in range(4):
            self.copies[y].wait_recv()
        add(beyond, 0)
        up_far = links.send(mine(beyond, 0), far.at[0], "y", 1)
        add(beyond, 1)
        down_far = links.send(mine(beyond, 1), far.at[1], "y", 3)
        add(after, 1)
        up_one = links.send(mine(after, 1), near.at[0, pl.ds(rows, rows)], "y", 1)
        add(before, 0)
        down_one = links.send(mine(before, 0), near.at[1, pl.ds(0, rows)], "y", 3)
        add(after, 0)
        add(before, 1)
        yield
        up_far.wait_recv()
        add_rows(far.at[0], far.at[0], mine(after, 0))
        up_two = links.send(far.at[0], near.at[0, pl.ds(0, rows)], "y", 1)
        down_far.wait_recv()
        add_rows(far.at[1], far.at[1], mine(before, 1))
        down_two = links.send(far.at[1], near.at[1, pl.ds(rows, rows)], "y", 3)
        for h in range(2):
            add(me, h)
        yield
        up_one.wait_recv()
        down_one.wait_recv()
        up_two.wait_recv()
        down_two.wait_recv()
        total = passed.at[me]

        def body(window):
            self.done(
                window, full(total[window]) + (full(near[0, window]) + full(near[1, window]))
            )

        each(2 * rows, 16, body)


class PairSum:
    def __init__(self, links, partial, passed, cross, pair, done):
        self.links, self.partial, self.done = links, partial, done
        self.passed, self.cross, self.pair = passed, cross, pair
        self.copies = {}

    def over(self, y_hi):
        core = self.links.here["core"]
        for y in (2 * y_hi, 2 * y_hi + 1):
            self.copies[y] = self.links.send(
                self.partial.at[block_of(y, 1 - core)], self.passed.at[y], "core"
            )

    def ring(self):
        links, partial, passed = self.links, self.partial, self.passed
        core, y_hi = links.here["core"], lax.div(links.here["y"], 2)
        rows = partial.shape[1] // 2
        chunks = [(i, pl.ds(h * rows, rows)) for i in range(2) for h in range(2)]
        theirs, ours = 2 - 2 * y_hi, 2 * y_hi
        for y in range(4):
            self.copies[y].wait_recv()

        def add(first, i, w):
            spot = passed.at[first + i, w]
            add_rows(spot, spot, partial.at[block_of(first + i, core), w])

        across = []
        for i, w in chunks:
            add(theirs, i, w)
            across.append(links.send(passed.at[theirs + i, w], self.cross.at[i, w], "cross"))
        for i, w in chunks:
            add(ours, i, w)
        yield
        beside = []
        for copy, (i, w) in zip(across, chunks):
            copy.wait_recv()
            spot = passed.at[ours + i, w]
            add_rows(spot, spot, self.cross.at[i, w])
            beside.append(links.send(spot, self.pair.at[i, w], "pair"))
            yield
        for n, (copy, (i, w)) in enumerate(zip(beside, chunks)):
            copy.wait_recv()

            def body(window, i=i, start=w.start):
                at = pl.ds(pl.multiple_of(start + window.start, 16), 16)
                self.done(i, at, full(passed[ours + i, at]) + full(self.pair[i, at]))

            each(rows, 16, body)
            if n < 3:
                yield


def column_scratch(rows):
    return [
        pltpu.VMEM((4, rows, 2048), LOW),
        pltpu.VMEM((2, rows, 2048), LOW),
        pltpu.VMEM((2, rows // 2, 2048), LOW),
    ]


class ByRows:
    def __init__(self, ref):
        self.ref = ref
        self.sides = [pl.ds(s * ref.shape[3] // 2, ref.shape[3] // 2) for s in range(2)]

    def own(self, own_ref, h, s):
        rows = own_ref.shape[0] // 2
        return [own_ref.at[pl.ds(h * rows, rows), self.sides[s]]]

    def one(self, z, x, h, s):
        rows = self.ref.shape[2] // 2
        return [self.ref.at[z, x, pl.ds(h * rows, rows), self.sides[s]]]

    def of_z(self, z, h, s):
        return [self.ref.at[z, pl.ds(2 * h, 2), :, self.sides[s]]]

    def of_x(self, x, h, s):
        return [self.ref.at[pl.ds(2 * h, 2), x, :, self.sides[s]]]


class ByColumns:
    def __init__(self, ref):
        self.ref = ref
        self.rows = ref.shape[0] // 2

    def own(self, own_ref, h, s):
        rows = self.rows // 2
        return [own_ref.at[pl.ds(s * self.rows + h * rows, rows)]]

    def one(self, z, x, h, s):
        rows = self.rows // 2
        return [self.ref.at[pl.ds(s * self.rows + h * rows, rows), aligned((z * 4 + x) * 128, 128)]]

    def of_z(self, z, h, s):
        return [self.ref.at[pl.ds(s * self.rows, self.rows), aligned(z * 512 + h * 256, 256)]]

    def of_x(self, x, h, s):
        return [
            self.ref.at[pl.ds(s * self.rows, self.rows), aligned((2 * h + k) * 512 + x * 128, 128)]
            for k in range(2)
        ]


def plane_first(links, blocks, own_ref, how):
    z, x = links.here["z"], links.here["x"]
    return side_by_side(
        [
            how(
                links,
                "x",
                lambda h: blocks.own(own_ref, h, 0),
                lambda p, h: blocks.one(z, p, h, 0),
            ),
            how(
                links,
                "z",
                lambda h: blocks.own(own_ref, h, 1),
                lambda p, h: blocks.one(p, x, h, 1),
            ),
        ]
    )


def plane_second(links, blocks, how):
    z, x = links.here["z"], links.here["x"]
    return side_by_side(
        [
            how(
                links, "z", lambda h: blocks.of_z(z, h, 0), lambda p, h: blocks.of_z(p, h, 0)
            ),
            how(
                links, "x", lambda h: blocks.of_x(x, h, 1), lambda p, h: blocks.of_x(p, h, 1)
            ),
        ]
    )


def plane_scratch(rows, width):
    return [
        pltpu.VMEM((2, 2, 4, rows, width), LOW),
        pltpu.VMEM((2, 2, 2, rows, width), LOW),
        pltpu.VMEM((2, 4, rows, width), LOW),
        pltpu.VMEM((2, 2, rows, width), LOW),
        pltpu.VMEM((2, 2, rows // 2, width), LOW),
    ]


def plane_scatter(links, grad, out, near, far, middle, near_two, far_two):
    z, x = links.here["z"], links.here["x"]
    by_rows = len(grad.shape) == 4
    rows, half = middle.shape[2:]

    def block(i, j, s):
        if by_rows:
            return grad.at[i, j, :, pl.ds(s * half, half)]
        return grad.at[pl.ds(s * rows, rows), aligned((i * 4 + j) * 128, 128)]

    def window_of(ref, s):
        if by_rows:
            return ref.at[:, pl.ds(s * half, half)]
        return ref.at[pl.ds(s * rows, rows)]

    def mine(s):
        if s == 0:
            return lambda p, h: [block(2 * h + k, p, 0) for k in range(2)]
        return lambda p, h: [block(p, 2 * h + k, 1) for k in range(2)]

    yield from side_by_side(
        [
            scatter4(
                links,
                axis,
                mine(s),
                [
                    lambda h, s=s, i=i: [near.at[s, i, 2 * h + k] for k in range(2)]
                    for i in range(2)
                ],
                [[far.at[s, i, k] for k in range(2)] for i in range(2)],
            )
            for s, axis in enumerate(("x", "z"))
        ]
    )
    for s in range(2):
        for p in range(4):
            own = block(p, x, 0) if s == 0 else block(z, p, 1)

            def body(window, s=s, p=p, own=own):
                middle[s, p, window] = low(
                    full(own[window])
                    + (full(near[s, 0, p, window]) + full(near[s, 1, p, window]))
                )

            each(rows, 16, body)
    part = rows // 2
    yield from side_by_side(
        [
            scatter4(
                links,
                axis,
                lambda p, h, s=s: middle.at[s, p, pl.ds(h * part, part)],
                [lambda h, s=s, i=i: near_two.at[s, i, pl.ds(h * part, part)] for i in range(2)],
                [far_two.at[s, 0], far_two.at[s, 1]],
            )
            for s, axis in enumerate(("z", "x"))
        ]
    )
    for s, me in enumerate((z, x)):
        into = window_of(out, s)

        def body(window, s=s, me=me, into=into):
            into[window] = low(
                full(middle[s, me, window])
                + (full(near_two[s, 0, window]) + full(near_two[s, 1, window]))
            )

        each(rows, 16, body)


def small_plane(links, own, out):
    z, x = links.here["z"], links.here["x"]
    out[z, x] = own[...]
    copies = [links.send(own, out.at[z, x], "x", step) for step in (1, 2, 3)]
    yield
    for copy in copies:
        copy.wait_recv()
    copies = [links.send(out.at[z], out.at[z], "z", step) for step in (1, 2, 3)]
    yield
    for copy in copies:
        copy.wait_recv()


def small_column(links, own, out):
    core, y = links.here["core"], links.here["y"]
    out[core, y] = own[...]
    copies = [links.send(own, out.at[core, y], "y", step) for step in (1, 2, 3)]
    yield
    for copy in copies:
        copy.wait_recv()
    copy = links.send(out.at[core], out.at[core], "core")
    yield
    copy.wait_recv()


def call(kernel, name, number, copies, kept, outs, out_specs, in_specs, scratch, vmem, operands):
    return pl.pallas_call(
        kernel,
        name=name,
        out_shape=outs,
        in_specs=in_specs,
        out_specs=out_specs,
        scratch_shapes=[
            pltpu.SemaphoreType.DMA((copies,)),
            pltpu.SemaphoreType.DMA((copies,)),
            pltpu.SemaphoreType.DMA((kept,)),
        ]
        + scratch,
        compiler_params=pltpu.CompilerParams(
            collective_id=number, has_side_effects=True, vmem_limit_bytes=vmem * 2**20
        ),
    )(*operands)


def shaped(shape, kind=LOW):
    return jax.ShapeDtypeStruct(shape, kind)


def turn_rows(values, cosine, sine):
    return values * cosine + pltpu.roll(values, HD // 2, 1) * sine


def gain_columns(gains, columns_of):
    for i in range(2):
        columns_of[i] = jnp.broadcast_to(gains[2 + i : 3 + i], (HD, HD)).T
    return columns_of.at[0], columns_of.at[1]


def forward_kernel(
    q_weight,
    k_weight,
    v_weight,
    o_weight,
    gate_weight,
    up_weight,
    down_weight,
    tokens,
    cotangent,
    gains,
    seq,
    waves,
    full_qkv_out,
    full_o_out,
    full_gu,
    full_d,
    unit_out,
    two_all,
    dy_all,
    middle,
    attended_out,
    queries_out,
    keys_out,
    values_out,
    proj_out,
    table_out,
    gains_all,
    starts,
    send_sems,
    recv_sems,
    kept,
    attended,
    queries,
    keys,
    values,
    proj,
    table,
    raw_qkv,
    own_qkv,
    own_o,
    raw_gu,
    own_gu,
    x_both,
    dy_both,
    down_own,
    full_qkv,
    full_o,
    unit_all,
    seq_all,
    partial,
    two_own,
    columns_of,
    *column,
):
    links = Links(send_sems, recv_sems)
    local = Locals(kept)
    here = links.here
    z, x, y, core = here["z"], here["x"], here["y"], here["core"]
    half = lax.rem(y, 2)
    part = lax.div(y, 2) * 2 + core
    spot = block_of(y, core)
    plane = z * 4 + x
    own_rows = x_both.shape[0] // 2
    nq, nkv = own_o.shape[0], keys.shape[1]
    nff = raw_gu.shape[1] // 2

    load_x = local.start(tokens, x_both)
    load_qkv = [
        local.start(q_weight.at[:, aligned(part * nq, nq)], raw_qkv.at[:, pl.ds(0, nq)]),
        local.start(k_weight.at[:, aligned(part * nkv, nkv)], raw_qkv.at[:, pl.ds(nq, nkv)]),
        local.start(v_weight.at[:, aligned(part * nkv, nkv)], raw_qkv.at[:, pl.ds(nq + nkv, nkv)]),
    ]
    load_o = local.start(o_weight.at[aligned(part * nq, nq)], own_o)
    load_gu = [
        local.start(gate_weight.at[:, aligned(part * nff, nff)], raw_gu.at[:, pl.ds(0, nff)]),
        local.start(up_weight.at[:, aligned(part * nff, nff)], raw_gu.at[:, pl.ds(nff, nff)]),
    ]
    load_late = [
        local.start(down_weight.at[aligned(part * nff, nff)], down_own),
        local.start(cotangent, dy_both),
    ]
    gain_one, gain_two = gain_columns(gains, columns_of)
    links.meet(PLANE + COLUMN)
    load_x.wait()

    base = part * 2

    def norm_one(window):
        rows = pl.ds(pl.multiple_of(half * own_rows + window.start, 16), 16)
        value = full(x_both[rows])
        unit_all[spot, window] = low(value * inverse_of(value))

    each(own_rows, 16, norm_one)
    column_one = column_gather(links, unit_all.at[spot], unit_all)
    small = [small_column(links, seq, seq_all), small_plane(links, gains, gains_all)]
    step_all([column_one] + small)
    for copy in load_qkv:
        copy.wait()

    def scale_qkv(window):
        own_qkv[window] = low(full(raw_qkv[window]) * gain_one[window, 0:1])
        full_qkv[z, x, window] = own_qkv[window]

    each(own_rows, 16, scale_qkv)
    blocks_qkv, blocks_o = ByRows(full_qkv), ByColumns(full_o)
    blocks_gu, blocks_d = ByRows(full_gu), ByColumns(full_d)
    first_qkv = plane_first(links, blocks_qkv, own_qkv, straight4)
    step_all([first_qkv])
    load_o.wait()
    first_o = plane_first(links, blocks_o, own_o, straight4)
    keep_o = local.start(own_o, full_o.at[:, aligned(plane * 128, 128)])
    for copy in load_gu + load_late:
        copy.wait()

    def scale_gu(window):
        own_gu[window] = low(full(raw_gu[window]) * gain_two[window, 0:1])

    each(own_rows, 16, scale_gu)
    step_all([first_o])
    first_late = [
        plane_first(links, blocks_gu, own_gu, straight4),
        plane_first(links, blocks_d, down_own, straight4),
    ]
    step_all(first_late)
    keep_gu = local.start(own_gu, full_gu.at[z, x])
    keep_d = local.start(down_own, full_d.at[:, aligned(plane * 128, 128)])
    late = [
        local.start(dy_both.at[pl.ds(i * own_rows, own_rows)], dy_all.at[base + i])
        for i in range(2)
    ]
    together([first_qkv])
    second_qkv = plane_second(links, blocks_qkv, gather4)
    step_all([second_qkv, column_one] + small)
    together(small)

    ids = full(seq_all[...])
    count_0 = jnp.sum((ids < 0.5).astype(WIDE), (0, 1))
    count_01 = jnp.sum((ids < 1.5).astype(WIDE), (0, 1))
    start_1 = jnp.sum(count_0[0:1], 1, keepdims=True)
    start_2 = jnp.sum(count_01[0:1], 1, keepdims=True)
    starts[0:4] = jnp.broadcast_to(start_1, (4, HD))
    starts[4:8] = jnp.broadcast_to(start_2, (4, HD))

    def start_of(index):
        return jnp.where(index < start_1, 0.0, jnp.where(index < start_2, start_1, start_2))

    def tables(i, carry):
        window = aligned(i * 64, 64)
        index = full(lax.broadcasted_iota(jnp.int32, (64, HD), 0) + i * 64)
        angle = (index - start_of(index)) * waves[0:1]
        table[0, window] = jnp.cos(angle)
        table[1, window] = jnp.sin(angle) * waves[1:2]
        return carry

    lax.fori_loop(0, 6, tables, 0)
    step_all([column_one, second_qkv])
    together([first_o])
    keep_o.wait()
    second_o = plane_second(links, blocks_o, gather4)
    step_all([second_o])
    lax.fori_loop(6, 12, tables, 0)
    step_all([column_one, second_qkv])
    lax.fori_loop(12, 16, tables, 0)
    together([second_qkv, column_one])
    step_all([second_o])
    together(first_late)
    keep_gu.wait()
    keep_d.wait()
    second_late = [
        plane_second(links, blocks_gu, gather4),
        plane_second(links, blocks_d, gather4),
    ]
    step_all(second_late)
    column_dy = column_fetch(
        links,
        lambda i, w: dy_both.at[
            pl.ds(pl.multiple_of(i * own_rows + w.start, w.size), w.size)
        ],
        dy_all,
        4,
    )
    step_all([column_dy])
    late += [
        local.start(full_qkv, full_qkv_out),
        local.start(unit_all, unit_out),
    ]

    gain_rows = jnp.sum(gains_all[...], (0, 1))
    q_gain, k_gain = gain_rows[0:1], gain_rows[1:2]

    def project(i, carry):
        window = aligned(i * 256, 256)
        unit = unit_all[pl.ds(2 * i, 2)].reshape(256, unit_all.shape[2])
        weights = full_qkv[...].reshape(16 * own_rows, nq + 2 * nkv)
        out = dot_nn(unit, weights)
        cosine, sine = table[0, window], table[1, window]
        for head in range(3):
            value = out[:, head * HD : (head + 1) * HD]
            proj[head, window] = value
            gain = q_gain if head < 2 else k_gain
            rotated = low(turn_rows(value * inverse_of(value) * gain, cosine, sine))
            if head < 2:
                queries[head, window] = rotated
            else:
                keys[window] = rotated
        values[window] = low(out[:, 3 * HD :])
        return carry

    lax.fori_loop(0, 4, project, 0)
    together([second_o])
    late.append(local.start(full_o, full_o_out))
    step_all([column_dy])

    def turn_done(window, total):
        rows = pl.ds(pl.multiple_of(half * own_rows + window.start, 16), 16)
        value = full(x_both[rows]) + total
        middle[window] = value
        two_own[window] = low(value * inverse_of(value))

    summed = ColumnSum(links, partial, *column, turn_done)
    for i in range(4):
        window = pl.ds(i * 256, 256)
        seen = 256 * (i + 1)
        query = jnp.concatenate([queries[0, window], queries[1, window]], 0)
        scores = dot_nt(query, keys[0:seen]) * SCALE
        row = lax.broadcasted_iota(jnp.int32, (256, 1), 0) + i * 256
        row = full(jnp.concatenate([row, row], 0))
        column_index = full(lax.broadcasted_iota(jnp.int32, (512, seen), 1))
        seen_here = (column_index <= row) & (column_index >= start_of(row))
        scores = jnp.where(seen_here, scores, -jnp.inf)
        power = jnp.exp(scores - jnp.max(scores, -1, keepdims=True))
        probs = power * (1.0 / jnp.sum(power, -1, keepdims=True))
        mixed = low(dot_nn(low(probs), values[0:seen]))
        both = jnp.concatenate([mixed[:256], mixed[256:]], 1)
        attended[window] = both
        partial[2 * i : 2 * i + 2] = low(dot_nn(both, full_o[...])).reshape(
            2, own_rows, partial.shape[2]
        )
        if i % 2:
            summed.over(i // 2)
        if i > 0:
            step_all([column_dy])
    late += [
        local.start(attended, attended_out),
        local.start(queries, queries_out),
        local.start(keys, keys_out),
        local.start(values, values_out),
        local.start(proj, proj_out),
        local.start(table, table_out),
    ]
    ring = summed.ring()
    step_all([ring])
    step_all(second_late)
    step_all([ring])
    together([ring])
    late.append(local.start(two_own, two_all.at[spot]))
    column_two = column_gather(links, two_own, two_all)
    step_all([column_two])
    step_all([column_two])
    together([column_two, column_dy])
    together(second_late)
    for copy in late:
        copy.wait()
    links.drain()


def middle_kernel(
    full_gu,
    full_d,
    two_all,
    dy_all,
    middle,
    mid_all,
    grad_gu_w,
    result,
    sum_d,
    send_sems,
    recv_sems,
    kept,
    gu,
    down,
    two,
    dy,
    product,
    grad_gu,
    partial,
    partial_down,
    grad_d,
    dy_own,
    mid_own,
    *scratch,
):
    column, column_down = scratch[:3], scratch[3:6]
    plane_d = scratch[6:]
    links = Links(send_sems, recv_sems)
    local = Locals(kept)
    here = links.here
    spot = block_of(here["y"], here["core"])
    rows = partial.shape[1] // 2
    width = partial.shape[2]
    nff = product.shape[1]
    windows = [pl.ds(h * rows, rows) for h in range(2)]
    halves = [pl.ds(h * 8 * rows, 8 * rows) for h in range(2)]

    load_gu = local.start(full_gu, gu)
    load_two = [local.start(two_all.at[:, windows[h]], two.at[h]) for h in range(2)]
    load_d = local.start(full_d, down)
    load_dy = [local.start(dy_all.at[:, windows[h]], dy.at[h]) for h in range(2)]
    load_own = local.start(dy_all.at[spot], dy_own)
    links.meet([("x", 1), ("x", 3), ("z", 1), ("z", 3), ("y", 1), ("y", 3), ("core", 0)])

    def loop(first, last, body):
        def one(i, carry):
            body(i)
            return carry

        lax.fori_loop(first, last, one, 0)

    def units(h, first, last):
        def body(j):
            at, after = aligned(j * 256, 256), aligned(nff + j * 256, 256)
            unit = two[h].reshape(8 * rows, width)
            gate = dot_nn(unit, gu[:, :, :, at].reshape(width, 256))
            up = dot_nn(unit, gu[:, :, :, after].reshape(width, 256))
            grad = dot_nt(dy[h].reshape(8 * rows, width), down[at])
            sigmoid = 1.0 / (1.0 + jnp.exp(-gate))
            silu = gate * sigmoid
            product[halves[h], at] = low(silu * up)
            grad_gu[halves[h], at] = low(grad * up * (sigmoid * (1.0 + gate * (1.0 - sigmoid))))
            grad_gu[halves[h], after] = low(grad * silu)

        loop(first, last, body)

    def forward_part(h):
        def body(n):
            at = aligned(n * 512, 512)
            out = low(dot_nn(product[halves[h]], down[:, at]))
            partial_down[:, windows[h], at] = out.reshape(8, rows, 512)

        loop(0, width // 512, body)

    def backward_part(h, first, last):
        def body(n):
            out = low(dot_nt(grad_gu[halves[h]], gu[n].reshape(512, 2 * nff)))
            partial[:, windows[h], aligned(n * 512, 512)] = out.reshape(8, rows, 512)

        loop(first, last, body)

    def here_rows(h, window):
        return pl.ds(pl.multiple_of(h * rows + window.start, 16), 16)

    def done(h):
        def body(window, total):
            at = here_rows(h, window)
            value = middle[at]
            inverse = inverse_of(value)
            value = full(dy_own[at]) + norm_back(total, value * inverse, inverse)
            mid_own[at] = low(value)

        return body

    def done_down(h):
        def body(window, total):
            at = here_rows(h, window)
            result[at] = low(middle[at] + total)

        return body

    def column_sum(source, parts, h, body):
        passed, near, far = parts
        return ColumnSum(
            links,
            source.at[:, windows[h]],
            passed.at[:, windows[h]],
            near.at[:, windows[h]],
            far.at[:, pl.ds(h * rows // 2, rows // 2)],
            body(h),
        )

    sums = [column_sum(partial, column, h, done) for h in range(2)]
    sums_down = [column_sum(partial_down, column_down, h, done_down) for h in range(2)]
    rings = [one.ring() for one in sums]
    rings_down = [one.ring() for one in sums_down]
    gathers = [
        column_gather(links, mid_own.at[windows[h]], mid_all.at[:, windows[h]]) for h in range(2)
    ]
    load_gu.wait()
    load_two[0].wait()
    load_d.wait()
    load_dy[0].wait()
    load_own.wait()
    def down_grad(i):
        at = aligned(i * 256, 256)
        grad_d[at] = low(dot_tn(product[:, at], dy[...].reshape(16 * rows, width)))

    def gate_up_grad(i):
        acts = two[:, :, :, aligned(i * 512, 512)].reshape(16 * rows, 512)
        gu[i] = low(dot_tn(acts, grad_gu[...])).reshape(4, 128, 2 * nff)

    units(0, 0, nff // 256)
    forward_part(0)
    sums_down[0].over(0)
    sums_down[0].over(1)
    load_two[1].wait()
    load_dy[1].wait()
    units(1, 0, 1)
    step_all([rings_down[0]])
    units(1, 1, nff // 256)
    forward_part(1)
    sums_down[1].over(0)
    sums_down[1].over(1)
    step_all([rings_down[0]])
    backward_part(0, 0, 2)
    step_all([rings_down[1]])
    backward_part(0, 2, 4)
    sums[0].over(0)
    sums[0].over(1)
    backward_part(1, 0, 2)
    step_all([rings[0]])
    backward_part(1, 2, 4)
    sums[1].over(0)
    sums[1].over(1)
    together([rings_down[0]])
    loop(0, 1, down_grad)
    step_all([rings[0], rings[1]])
    loop(1, nff // 256, down_grad)
    scatter_d = plane_scatter(links, grad_d, sum_d, *plane_d)
    step_all([scatter_d])
    together([rings[0]])
    step_all([gathers[0]])
    step_all([gathers[0]])
    loop(0, 2, gate_up_grad)
    step_all([rings[1], rings_down[1]])
    loop(2, 4, gate_up_grad)
    keep_w = local.start(gu, grad_gu_w)
    step_all([gathers[0]])
    together([rings[1]])
    step_all([gathers[1]])
    step_all([gathers[1], scatter_d])
    keep_mid = local.start(mid_own, mid_all.at[spot])
    together([rings_down[1]])
    step_all([gathers[0], scatter_d])
    step_all([gathers[1], scatter_d])
    together([gathers[0], gathers[1], scatter_d])
    for copy in (keep_w, keep_mid):
        copy.wait()
    links.drain()


def end_kernel(
    q_weight,
    k_weight,
    v_weight,
    gate_weight,
    up_weight,
    tokens,
    full_qkv,
    full_o,
    unit_all,
    mid_all,
    grad_gu_w,
    attended_in,
    queries_in,
    keys_in,
    values_in,
    proj_in,
    table_in,
    gains_all,
    starts,
    gains,
    result,
    sum_d,
    grad_x,
    out_rows,
    all_qkv,
    all_o,
    all_gu,
    all_d,
    sums_out,
    send_sems,
    recv_sems,
    kept,
    attended,
    queries,
    keys,
    values,
    proj,
    table,
    columns_of,
    weights,
    weight_o,
    unit,
    mid,
    grad_gu,
    grad_o,
    grad_qkv_w,
    raw_qkv,
    raw_gu,
    x_both,
    mid_both,
    grad_att,
    dk,
    dv,
    grad_qkv,
    sum_gu,
    sum_qkv,
    own_o,
    own_gu,
    own_qkv,
    small,
    small_all,
    row,
    row_all,
    turned,
    x_pair,
    *scratch,
):
    passed, cross, pair = scratch[:3]
    plane_gu, plane_o, plane_qkv = scratch[3:8], scratch[8:13], scratch[13:]
    links = Links(send_sems, recv_sems)
    local = Locals(kept)
    here = links.here
    y, core = here["y"], here["core"]
    half = lax.rem(y, 2)
    part = lax.div(y, 2) * 2 + core
    part_other = lax.div(lax.rem(y + 2, 4), 2) * 2 + core
    _, rows, width = x_both.shape
    nq, nkv = own_o.shape[0], keys.shape[1]
    nff = sum_gu.shape[1] // 2

    load_mid = local.start(mid_all, mid)
    load_o = local.start(full_o, weight_o)
    load_gu = local.start(grad_gu_w, grad_gu)
    load_heads = [
        local.start(queries_in, queries),
        local.start(keys_in, keys),
        local.start(values_in, values),
        local.start(proj_in, proj),
        local.start(table_in, table),
        local.start(attended_in, attended),
    ]
    gain_one, gain_two = gain_columns(gains, columns_of)
    loads = [
        local.start(full_qkv, weights),
        local.start(unit_all, unit),
        local.start(tokens.at[pl.ds(0, rows)], x_both.at[0]),
        local.start(tokens.at[pl.ds(rows, rows)], x_both.at[1]),
        local.start(mid_all.at[pl.ds(pl.multiple_of(2 * part, 2), 2)], mid_both),
        local.start(q_weight.at[:, aligned(part * nq, nq)], raw_qkv.at[:, pl.ds(0, nq)]),
        local.start(k_weight.at[:, aligned(part * nkv, nkv)], raw_qkv.at[:, pl.ds(nq, nkv)]),
        local.start(v_weight.at[:, aligned(part * nkv, nkv)], raw_qkv.at[:, pl.ds(nq + nkv, nkv)]),
        local.start(gate_weight.at[:, aligned(part * nff, nff)], raw_gu.at[:, pl.ds(0, nff)]),
        local.start(up_weight.at[:, aligned(part * nff, nff)], raw_gu.at[:, pl.ds(nff, nff)]),
    ]
    links.meet(PLANE + COLUMN)

    def share(own, out):
        across = links.send(own, out.at[part], "y", 2)
        beside = links.send(own, out.at[part], "core")
        keep = local.start(own, out.at[part])
        yield
        across.wait_recv()
        second = links.send(out.at[part_other], out.at[part_other], "core")
        yield
        beside.wait_recv()
        second.wait_recv()
        keep.wait()

    def exchange(own, out):
        copy = links.send(own, out.at[half], "pair")
        keep = local.start(own, out.at[half])
        yield
        copy.wait_recv()
        keep.wait()

    def done_one(i, window, total):
        value = full(x_both[i, window])
        inverse = inverse_of(value)
        back = norm_back(total, value * inverse, inverse)
        x_pair[i, window] = low(full(mid_both[i, window]) + back)

    def scale(into, total, raw, gain, spot):
        def body(window):
            into[window] = low(full(total[window]) * gain[window, 0:1])
            part_sum = jnp.sum(full(total[window]) * full(raw[window]), 1, keepdims=True)
            turned[spot, window] = jnp.broadcast_to(part_sum, (16, HD))

        each(rows, 16, body)

    def attended_grad(i, carry):
        window = aligned(i * 256, 256)
        out = low(dot_nt(mid[pl.ds(2 * i, 2)].reshape(256, width), weight_o[...]))
        grad_att[0, window] = out[:, :HD]
        grad_att[1, window] = out[:, HD:]
        return carry

    def gu_job():
        yield from plane_scatter(links, grad_gu, sum_gu, *plane_gu)
        scale(own_gu, sum_gu, raw_gu, gain_two, 1)
        yield from share(own_gu, all_gu)

    def o_job():
        yield from plane_scatter(links, grad_o, own_o, *plane_o)
        yield from share(own_o, all_o)

    def qkv_job():
        yield from plane_scatter(links, grad_qkv_w, sum_qkv, *plane_qkv)
        scale(own_qkv, sum_qkv, raw_qkv, gain_one, 0)
        yield from share(own_qkv, all_qkv)

    job_gu, job_o, job_qkv = gu_job(), o_job(), qkv_job()
    share_d = share(sum_d, all_d)
    pair_rows = exchange(result, out_rows)
    step_all([pair_rows, share_d])
    load_gu.wait()
    step_all([job_gu])
    load_mid.wait()
    load_o.wait()
    lax.fori_loop(0, 4, attended_grad, 0)
    for copy in load_heads:
        copy.wait()

    gain_rows = jnp.sum(gains_all[...], (0, 1))
    q_gain, k_gain = gain_rows[0:1], gain_rows[1:2]
    start_1, start_2 = starts[0:1, 0:1], starts[4:5, 0:1]
    dk[...] = jnp.zeros_like(dk)
    dv[...] = jnp.zeros_like(dv)
    small[...] = jnp.zeros_like(small)

    def project_back(grad, head, window, gain):
        cosine, sine = table[0, window], table[1, window]
        back = grad * cosine - pltpu.roll(grad, HD // 2, 1) * sine
        value = proj[head, window]
        inverse = inverse_of(value)
        scaled = value * inverse
        spot = 0 if head < 2 else 1
        small[spot : spot + 1] += jnp.sum(back * scaled, 0, keepdims=True)
        return low(norm_back(back * gain, scaled, inverse))

    for i in range(4):
        window = pl.ds(i * 256, 256)
        seen = 256 * (i + 1)
        query = jnp.concatenate([queries[0, window], queries[1, window]], 0)
        grad = jnp.concatenate([grad_att[0, window], grad_att[1, window]], 0)
        key, value = keys[0:seen], values[0:seen]
        scores = dot_nt(key, query) * SCALE
        column = lax.broadcasted_iota(jnp.int32, (1, 256), 1) + i * 256
        column = full(jnp.concatenate([column, column], 1))
        start = jnp.where(
            column < start_1, 0.0, jnp.where(column < start_2, start_1, start_2)
        )
        index = full(lax.broadcasted_iota(jnp.int32, (seen, 512), 0))
        scores = jnp.where((index <= column) & (index >= start), scores, -jnp.inf)
        power = jnp.exp(scores - jnp.max(scores, 0, keepdims=True))
        probs = power * (1.0 / jnp.sum(power, 0, keepdims=True))
        grad_probs = dot_nt(value, grad)
        inner = jnp.sum(probs * grad_probs, 0, keepdims=True)
        grad_scores = low(probs * (grad_probs - inner))
        dv[0:seen] += dot_nn(low(probs), grad)
        dk[0:seen] += dot_nn(grad_scores, query)
        dq = dot_tn(key, grad_scores).T * SCALE
        for head in range(2):
            grad_qkv[window, head * HD : (head + 1) * HD] = project_back(
                dq[head * 256 : (head + 1) * 256], head, window, q_gain
            )
        if i == 3:
            step_all([share_d])

    def keys_back(i, carry):
        window = aligned(i * 256, 256)
        grad_qkv[window, nq : nq + nkv] = project_back(dk[window] * SCALE, 2, window, k_gain)
        grad_qkv[window, nq + nkv :] = low(dv[window])
        return carry

    lax.fori_loop(0, 4, keys_back, 0)
    small_job = small_plane(links, small, small_all)
    step_all([small_job])

    def unit_grad(i, carry):
        out = low(
            dot_nt(
                grad_qkv[aligned(i * 256, 256)], weights[...].reshape(width, nq + 2 * nkv)
            )
        )
        mid[pl.ds(2 * i, 2)] = out.reshape(2, rows, width)
        return carry

    for copy in loads:
        copy.wait()
    sum_one = PairSum(links, mid, passed, cross, pair, done_one)
    grad_o[...] = low(dot_tn(attended[...], mid[...].reshape(8 * rows, width)))
    step_all([job_o])
    lax.fori_loop(0, 2, unit_grad, 0)
    sum_one.over(0)
    lax.fori_loop(2, 4, unit_grad, 0)
    sum_one.over(1)
    step_all([job_gu])
    ring_one = sum_one.ring()
    step_all([ring_one])

    def weight_grad(i, carry):
        at = aligned(i * 512, 512)
        out = dot_tn(unit[:, :, at].reshape(8 * rows, 512), grad_qkv[...])
        grad_qkv_w[i] = low(out).reshape(4, rows, nq + 2 * nkv)
        return carry

    lax.fori_loop(0, 4, weight_grad, 0)
    step_all([job_qkv])
    step_all([ring_one])
    step_all([job_o, small_job])
    step_all([ring_one])
    step_all([job_gu, job_qkv])
    step_all([ring_one])
    step_all([job_o, job_qkv, share_d])
    step_all([ring_one])
    step_all([job_gu, job_o, job_qkv])
    for _ in range(3):
        step_all([ring_one])
    step_all([job_gu, job_o, job_qkv])
    together([small_job])
    row[0:2] = jnp.sum(small_all[:, :, 0:2], (0, 1))
    row[2:3] = turned[0].T[0:1]
    row[3:4] = turned[1].T[0:1]
    row[4:8] = jnp.zeros((4, HD), WIDE)
    row_job = small_column(links, row, row_all)
    step_all([row_job])
    together([ring_one])
    keep_x = local.start(x_pair, grad_x)
    together([row_job, job_o, job_gu, job_qkv, share_d, pair_rows])
    keep_x.wait()
    sums_out[...] = jnp.sum(row_all[...], (0, 1))
    links.drain()


def widen_kernel(
    out_rows,
    grad_x,
    all_qkv,
    all_o,
    all_gu,
    all_d,
    out_final,
    x_final,
    q_final,
    k_final,
    v_final,
    o_final,
    gate_final,
    up_final,
    d_final,
    rows_low,
    x_low,
    qkv_low,
    o_low,
    gu_low,
    d_low,
    x_wide,
    q_wide,
    k_wide,
    v_wide,
    o_wide,
    gate_wide,
    up_wide,
    d_wide,
    kept,
):
    local = Locals(kept)
    halves, rows, _ = x_low.shape
    parts, rows_w = gu_low.shape[:2]
    nff = gu_low.shape[2] // 2
    load_gu = local.start(all_gu, gu_low)
    load_d = local.start(all_d, d_low)
    load_qkv = local.start(all_qkv, qkv_low)
    load_o = local.start(all_o, o_low)
    load_x = local.start(grad_x, x_low)
    load_rows = local.start(out_rows, rows_low)
    nq = q_wide.shape[1] // parts
    nkv = k_wide.shape[1] // parts
    stores = []

    def side_by_side_parts(source, start, size, into, final):
        for c in range(parts):

            def body(window, c=c):
                into[window, c * size : (c + 1) * size] = full(
                    source[c, window, start : start + size]
                )

            each(rows_w, 32, body)
        stores.append(local.start(into, final))

    def stacked(source, into, final, step):
        count, size = source.shape[:2]
        for c in range(count):

            def body(window, c=c):
                into[c, window] = full(source[c, window])

            each(size, step, body)
            stores.append(local.start(into.at[c], final.at[pl.ds(c * size, size)]))

    load_gu.wait()
    side_by_side_parts(gu_low, 0, nff, gate_wide, gate_final)
    side_by_side_parts(gu_low, nff, nff, up_wide, up_final)
    load_d.wait()
    stacked(d_low, d_wide, d_final, 128)
    load_x.wait()
    stacked(x_low, x_wide, x_final, 16)
    load_rows.wait()
    for c in range(halves):
        stores.append(local.start(rows_low.at[c], out_final.at[pl.ds(c * rows, rows)]))
    load_qkv.wait()
    side_by_side_parts(qkv_low, 0, nq, q_wide, q_final)
    side_by_side_parts(qkv_low, nq, nkv, k_wide, k_final)
    side_by_side_parts(qkv_low, nq + nkv, nkv, v_wide, v_final)
    load_o.wait()
    stacked(o_low, o_wide, o_final, 128)
    for copy in stores:
        copy.wait()


def per_device(
    tokens,
    segments,
    attn_gain,
    q_weight,
    k_weight,
    v_weight,
    q_gain,
    k_gain,
    o_weight,
    mlp_gain,
    gate_weight,
    up_weight,
    down_weight,
    cotangent,
):
    parts, halves = lax.axis_size("ctx"), lax.axis_size("tp")
    half = lax.axis_index("tp")
    rows_here, width = tokens.shape
    seq_len = rows_here * parts
    own_rows = rows_here // halves
    blocks = parts * halves

    def own(array):
        return lax.dynamic_slice_in_dim(array, half * own_rows, own_rows, 0)

    rows_w = q_weight.shape[0]
    nq, nkv, nff = q_weight.shape[1] // parts, k_weight.shape[1] // parts, gate_weight.shape[1] // parts
    na, nb = nq + 2 * nkv, 2 * nff
    few = q_gain.shape[0]
    spread = lax.dynamic_update_slice(
        jnp.zeros((2, HD), WIDE),
        full(jnp.stack([q_gain, k_gain])),
        (0, lax.axis_index("fsdp") * few),
    )
    gains = jnp.concatenate(
        [spread, full(attn_gain)[None], full(mlp_gain)[None], jnp.zeros((4, HD), WIDE)], 0
    )
    seq = jnp.broadcast_to(own(segments)[None, :], (8, own_rows))
    index = np.arange(HD)
    frequency = np.power(rope_base, -2.0 * (index % (HD // 2)) / HD)
    waves = np.zeros((8, HD), np.float32)
    waves[0] = frequency
    waves[1] = np.where(index < HD // 2, -1.0, 1.0)

    (
        full_qkv,
        full_o,
        full_gu,
        full_d,
        unit_all,
        two_all,
        dy_all,
        middle,
        attended,
        queries,
        keys,
        values,
        proj,
        table,
        gains_all,
        starts,
    ) = call(
        forward_kernel,
        "forward",
        0,
        176,
        24,
        (
            shaped((4, 4, rows_w, na)),
            shaped((nq, width)),
            shaped((4, 4, rows_w, nb)),
            shaped((nff, width)),
            shaped((blocks, own_rows, width)),
            shaped((blocks, own_rows, width)),
            shaped((blocks, own_rows, width)),
            shaped((own_rows, width), WIDE),
            shaped((seq_len, nq)),
            shaped((2, seq_len, HD)),
            shaped((seq_len, HD)),
            shaped((seq_len, HD)),
            shaped((3, seq_len, HD), WIDE),
            shaped((2, seq_len, HD), WIDE),
            shaped((4, 4, 8, HD), WIDE),
            shaped((8, HD), WIDE),
        ),
        [HBM] * 7 + [VMEM] + [HBM] * 6 + [VMEM] * 2,
        [HBM] * 9 + [VMEM] * 3,
        [
            pltpu.VMEM((seq_len, nq), LOW),
            pltpu.VMEM((2, seq_len, HD), LOW),
            pltpu.VMEM((seq_len, HD), LOW),
            pltpu.VMEM((seq_len, HD), LOW),
            pltpu.VMEM((3, seq_len, HD), WIDE),
            pltpu.VMEM((2, seq_len, HD), WIDE),
            pltpu.VMEM((rows_w, na), LOW),
            pltpu.VMEM((rows_w, na), LOW),
            pltpu.VMEM((nq, rows_w), LOW),
            pltpu.VMEM((rows_w, nb), LOW),
            pltpu.VMEM((rows_w, nb), LOW),
            pltpu.VMEM((rows_here, width), LOW),
            pltpu.VMEM((rows_here, width), LOW),
            pltpu.VMEM((nff, rows_w), LOW),
            pltpu.VMEM((4, 4, rows_w, na), LOW),
            pltpu.VMEM((nq, width), LOW),
            pltpu.VMEM((blocks, own_rows, width), LOW),
            pltpu.VMEM((2, 4, 8, own_rows), jnp.int32),
            pltpu.VMEM((blocks, own_rows, width), LOW),
            pltpu.VMEM((own_rows, width), LOW),
            pltpu.VMEM((2, HD, HD), WIDE),
        ]
        + column_scratch(own_rows),
        58,
        (
            q_weight,
            k_weight,
            v_weight,
            o_weight,
            gate_weight,
            up_weight,
            down_weight,
            tokens,
            cotangent,
            gains,
            seq,
            jnp.asarray(waves),
        ),
    )

    mid_all, grad_gu_w, result, sum_d = call(
        middle_kernel,
        "middle",
        1,
        144,
        12,
        (
            shaped((blocks, own_rows, width)),
            shaped((4, 4, rows_w, nb)),
            shaped((own_rows, width)),
            shaped((nff, rows_w)),
        ),
        [HBM] * 2 + [VMEM] * 2,
        [HBM] * 4 + [VMEM],
        [
            pltpu.VMEM((4, 4, rows_w, nb), LOW),
            pltpu.VMEM((nff, width), LOW),
            pltpu.VMEM((2, blocks, own_rows // 2, width), LOW),
            pltpu.VMEM((2, blocks, own_rows // 2, width), LOW),
            pltpu.VMEM((seq_len, nff), LOW),
            pltpu.VMEM((seq_len, nb), LOW),
            pltpu.VMEM((blocks, own_rows, width), LOW),
            pltpu.VMEM((blocks, own_rows, width), LOW),
            pltpu.VMEM((nff, width), LOW),
            pltpu.VMEM((own_rows, width), LOW),
            pltpu.VMEM((own_rows, width), LOW),
        ]
        + column_scratch(own_rows)
        + column_scratch(own_rows)
        + plane_scratch(nff // 2, rows_w),
        62,
        (full_gu, full_d, two_all, dy_all, middle),
    )

    grad_x, out_rows, all_qkv, all_o, all_gu, all_d, sums = call(
        end_kernel,
        "end",
        2,
        160,
        40,
        (
            shaped((halves, own_rows, width)),
            shaped((halves, own_rows, width)),
            shaped((parts, rows_w, na)),
            shaped((parts, nq, rows_w)),
            shaped((parts, rows_w, nb)),
            shaped((parts, nff, rows_w)),
            shaped((8, HD), WIDE),
        ),
        [HBM] * 6 + [VMEM],
        [HBM] * 17 + [VMEM] * 5,
        [
            pltpu.VMEM((seq_len, nq), LOW),
            pltpu.VMEM((2, seq_len, HD), LOW),
            pltpu.VMEM((seq_len, HD), LOW),
            pltpu.VMEM((seq_len, HD), LOW),
            pltpu.VMEM((3, seq_len, HD), WIDE),
            pltpu.VMEM((2, seq_len, HD), WIDE),
            pltpu.VMEM((2, HD, HD), WIDE),
            pltpu.VMEM((4, 4, rows_w, na), LOW),
            pltpu.VMEM((nq, width), LOW),
            pltpu.VMEM((blocks, own_rows, width), LOW),
            pltpu.VMEM((blocks, own_rows, width), LOW),
            pltpu.VMEM((4, 4, rows_w, nb), LOW),
            pltpu.VMEM((nq, width), LOW),
            pltpu.VMEM((4, 4, rows_w, na), LOW),
            pltpu.VMEM((rows_w, na), LOW),
            pltpu.VMEM((rows_w, nb), LOW),
            pltpu.VMEM((halves, own_rows, width), LOW),
            pltpu.VMEM((halves, own_rows, width), LOW),
            pltpu.VMEM((2, seq_len, HD), LOW),
            pltpu.VMEM((seq_len, HD), WIDE),
            pltpu.VMEM((seq_len, HD), WIDE),
            pltpu.VMEM((seq_len, na), LOW),
            pltpu.VMEM((rows_w, nb), LOW),
            pltpu.VMEM((rows_w, na), LOW),
            pltpu.VMEM((nq, rows_w), LOW),
            pltpu.VMEM((rows_w, nb), LOW),
            pltpu.VMEM((rows_w, na), LOW),
            pltpu.VMEM((8, HD), WIDE),
            pltpu.VMEM((4, 4, 8, HD), WIDE),
            pltpu.VMEM((8, HD), WIDE),
            pltpu.VMEM((2, 4, 8, HD), WIDE),
            pltpu.VMEM((2, rows_w, HD), WIDE),
            pltpu.VMEM((halves, own_rows, width), LOW),
            pltpu.VMEM((4, own_rows, width), LOW),
            pltpu.VMEM((halves, own_rows, width), LOW),
            pltpu.VMEM((halves, own_rows, width), LOW),
        ]
        + plane_scratch(rows_w, nb // 2)
        + plane_scratch(nq // 2, rows_w)
        + plane_scratch(rows_w, na // 2),
        62,
        (
            q_weight,
            k_weight,
            v_weight,
            gate_weight,
            up_weight,
            tokens,
            full_qkv,
            full_o,
            unit_all,
            mid_all,
            grad_gu_w,
            attended,
            queries,
            keys,
            values,
            proj,
            table,
            gains_all,
            starts,
            gains,
            result,
            sum_d,
        ),
    )

    (
        out_final,
        x_final,
        q_final,
        k_final,
        v_final,
        o_final,
        gate_final,
        up_final,
        d_final,
    ) = pl.pallas_call(
        widen_kernel,
        name="widen",
        out_shape=(
            shaped((rows_here, width)),
            shaped((rows_here, width), WIDE),
            shaped(q_weight.shape, WIDE),
            shaped(k_weight.shape, WIDE),
            shaped(v_weight.shape, WIDE),
            shaped(o_weight.shape, WIDE),
            shaped(gate_weight.shape, WIDE),
            shaped(up_weight.shape, WIDE),
            shaped(down_weight.shape, WIDE),
        ),
        in_specs=[HBM] * 6,
        out_specs=[HBM] * 9,
        scratch_shapes=[
            pltpu.VMEM((halves, own_rows, width), LOW),
            pltpu.VMEM((halves, own_rows, width), LOW),
            pltpu.VMEM((parts, rows_w, na), LOW),
            pltpu.VMEM((parts, nq, rows_w), LOW),
            pltpu.VMEM((parts, rows_w, nb), LOW),
            pltpu.VMEM((parts, nff, rows_w), LOW),
            pltpu.VMEM((halves, own_rows, width), WIDE),
            pltpu.VMEM(q_weight.shape, WIDE),
            pltpu.VMEM(k_weight.shape, WIDE),
            pltpu.VMEM(v_weight.shape, WIDE),
            pltpu.VMEM((parts, nq, rows_w), WIDE),
            pltpu.VMEM(gate_weight.shape, WIDE),
            pltpu.VMEM(up_weight.shape, WIDE),
            pltpu.VMEM((parts, nff, rows_w), WIDE),
            pltpu.SemaphoreType.DMA((40,)),
        ],
        compiler_params=pltpu.CompilerParams(vmem_limit_bytes=60 * 2**20),
    )(out_rows, grad_x, all_qkv, all_o, all_gu, all_d)
    sum_qk = lax.dynamic_slice_in_dim(sums[:2], lax.axis_index("fsdp") * few, few, 1)
    return (
        out_final,
        x_final,
        sums[2],
        q_final,
        k_final,
        v_final,
        sum_qk[0],
        sum_qk[1],
        o_final,
        sums[3],
        gate_final,
        up_final,
        d_final,
    )


def solution(mesh):
    weight = P("fsdp", "tp")
    turned = P("tp", "fsdp")
    acts = P(("fsdp", "ctx"), None)
    gain = P("fsdp")
    return jax.shard_map(
        per_device,
        mesh=mesh,
        in_specs=(
            acts,
            P(("fsdp", "ctx")),
            gain,
            weight,
            weight,
            weight,
            gain,
            gain,
            turned,
            gain,
            weight,
            weight,
            turned,
            acts,
        ),
        out_specs=(
            acts,
            acts,
            gain,
            weight,
            weight,
            weight,
            gain,
            gain,
            turned,
            gain,
            weight,
            weight,
            turned,
        ),
        check_vma=False,
    )
```

```python
import jax
import jax.numpy as jnp
from jax import lax
from jax.experimental import pallas as pl
from jax.experimental.pallas import tpu as pltpu
from jax.sharding import PartitionSpec as P

HD = 128
MESH = pl.DeviceIdType.MESH
HBM = pl.BlockSpec(memory_space=pl.ANY)
VMEM = pl.BlockSpec(memory_space=pltpu.VMEM)
LOW = jnp.bfloat16
WIDE = jnp.float32
SCALE = HD ** (-0.5)


epsilon = 1e-06
rope_base = 1000000.0


def inverse_of(values_in):
    return lax.rsqrt(jnp.mean(values_in * values_in, -1, keepdims=True) + epsilon)


def norm_back(grad_in, unit_in, inverse):
    return inverse * (grad_in - unit_in * jnp.mean(grad_in * unit_in, -1, keepdims=True))


def dot_nn(left, right):
    return jnp.dot(left, right, preferred_element_type=WIDE)


def dot_tn(left, right):
    return lax.dot_general(left, right, (((0,), (0,)), ((), ())), preferred_element_type=WIDE)


def dot_nt(left, right):
    return lax.dot_general(left, right, (((1,), (1,)), ((), ())), preferred_element_type=WIDE)


def low(values_in):
    return values_in.astype(LOW)


def full(values_in):
    return values_in.astype(WIDE)


def place():
    plane = lax.axis_index("fsdp")
    part = lax.axis_index("ctx")
    half = lax.axis_index("tp")
    return {
        "z": lax.div(plane, 4),
        "x": lax.rem(plane, 4),
        "y": lax.div(part, 2) * 2 + half,
        "core": lax.rem(part, 2),
    }


def device(where):
    return (
        where["z"] * 4 + where["x"],
        lax.div(where["y"], 2) * 2 + where["core"],
        lax.rem(where["y"], 2),
    )


def moved(here, axis, step):
    there = dict(here)
    if axis == "pair":
        there["y"] = here["y"] + 1 - 2 * lax.rem(here["y"], 2)
    elif axis == "cross":
        there["y"] = 3 - here["y"]
    elif axis == "core":
        there["core"] = 1 - here["core"]
    else:
        there[axis] = lax.rem(here[axis] + step, 4)
    return there


def block_of(y, core):
    return lax.div(y, 2) * 4 + core * 2 + lax.rem(y, 2)


class Group:
    def __init__(self, copies):
        self.copies = copies

    def wait_recv(self):
        for copy in self.copies:
            copy.wait_recv()


class Links:
    def __init__(self, send_sems, recv_sems):
        self.here = place()
        self.send_sems, self.recv_sems = send_sems, recv_sems
        self.started = []

    def meet(self, peers):
        barrier = pltpu.get_barrier_semaphore()
        for axis, step in peers:
            pl.semaphore_signal(
                barrier,
                inc=1,
                device_id=device(moved(self.here, axis, step)),
                device_id_type=MESH,
            )
        pl.semaphore_wait(barrier, len(peers))

    def send(self, src, dst, axis, step=0):
        if isinstance(src, list):
            return Group([self.send(a, b, axis, step) for a, b in zip(src, dst)])
        spot = len(self.started)
        assert spot < self.send_sems.shape[0]
        copy = pltpu.make_async_remote_copy(
            src_ref=src,
            dst_ref=dst,
            send_sem=self.send_sems.at[spot],
            recv_sem=self.recv_sems.at[spot],
            device_id=device(moved(self.here, axis, step)),
            device_id_type=MESH,
        )
        copy.start()
        self.started.append(copy)
        return copy

    def drain(self):
        for copy in self.started:
            copy.wait_send()


class Locals:
    def __init__(self, sems):
        self.sems = sems
        self.count = 0

    def start(self, src, dst):
        assert self.count < self.sems.shape[0]
        copy = pltpu.make_async_copy(src, dst, self.sems.at[self.count])
        self.count += 1
        copy.start()
        return copy


PLANE = [("x", 1), ("x", 2), ("x", 3), ("z", 1), ("z", 2), ("z", 3)]
COLUMN = [("y", 1), ("y", 2), ("y", 3), ("core", 0)]


def step_all(jobs):
    left = []
    for job in jobs:
        try:
            next(job)
            left.append(job)
        except StopIteration:
            pass
    return left


def together(jobs):
    jobs = list(jobs)
    while jobs:
        jobs = step_all(jobs)


def side_by_side(jobs):
    jobs = list(jobs)
    while jobs:
        jobs = step_all(jobs)
        if jobs:
            yield


def each(count, step, body):
    def one(i, carry):
        body(pl.ds(pl.multiple_of(i * step, step), step))
        return carry

    lax.fori_loop(0, count // step, one, 0)


def aligned(start, size):
    return pl.ds(pl.multiple_of(start, size), size)


def add_rows(into, first, second):
    if isinstance(into, list):
        for refs in zip(into, first, second):
            add_rows(*refs)
        return
    lead, rows = into.shape[:-2], into.shape[-2]

    def add(spot):
        def body(window):
            spots = spot + (window,)
            into[spots] = first[spots] + second[spots]

        return body

    if not lead:
        each(rows, 16, add(()))
    else:
        for i in range(lead[0]):
            each(rows, 16, add((i,)))


def gather4(links, axis, own, block, arrived=None):
    me = links.here[axis]
    before, after, far = lax.rem(me + 3, 4), lax.rem(me + 1, 4), lax.rem(me + 2, 4)
    arrived = arrived or (lambda spot, side: None)
    up, down = {}, {}
    up[0] = links.send(own(0), block(me, 0), axis, 1)
    down[1] = links.send(own(1), block(me, 1), axis, 3)
    up[1] = links.send(own(1), block(me, 1), axis, 1)
    down[0] = links.send(own(0), block(me, 0), axis, 3)
    yield
    up[0].wait_recv()
    up_far = links.send(block(before, 0), block(before, 0), axis, 1)
    arrived(before, 0)
    down[1].wait_recv()
    down_far = links.send(block(after, 1), block(after, 1), axis, 3)
    arrived(after, 1)
    yield
    up[1].wait_recv()
    arrived(before, 1)
    down[0].wait_recv()
    arrived(after, 0)
    yield
    up_far.wait_recv()
    arrived(far, 0)
    down_far.wait_recv()
    arrived(far, 1)


def straight4(links, axis, own, block):
    me = links.here[axis]
    copies = [
        links.send(own(h), block(me, h), axis, step) for step in (2, 1, 3) for h in range(2)
    ]
    yield
    for copy in copies:
        copy.wait_recv()


def scatter4(links, axis, mine, near, far):
    me = links.here[axis]
    before, after, beyond = lax.rem(me + 3, 4), lax.rem(me + 1, 4), lax.rem(me + 2, 4)
    up_far = links.send(mine(beyond, 0), far[0], axis, 1)
    down_far = links.send(mine(beyond, 1), far[1], axis, 3)
    up_one = links.send(mine(after, 1), near[0](1), axis, 1)
    down_one = links.send(mine(before, 0), near[1](0), axis, 3)
    yield
    up_far.wait_recv()
    add_rows(far[0], far[0], mine(after, 0))
    up_two = links.send(far[0], near[0](0), axis, 1)
    down_far.wait_recv()
    add_rows(far[1], far[1], mine(before, 1))
    down_two = links.send(far[1], near[1](1), axis, 3)
    yield
    up_one.wait_recv()
    down_one.wait_recv()
    up_two.wait_recv()
    down_two.wait_recv()


def column_gather(links, own_ref, out):
    here = links.here
    rows = out.shape[1] // 2
    shared = []

    def own(h):
        return own_ref.at[pl.ds(h * rows, rows)]

    def block(p, h):
        return out.at[block_of(p, here["core"]), pl.ds(h * rows, rows)]

    def arrived(p, h):
        shared.append(links.send(block(p, h), block(p, h), "core"))

    ring = gather4(links, "y", own, block, arrived)
    next(ring)
    for h in range(2):
        shared.append(links.send(own(h), block(here["y"], h), "core"))
    yield
    for _ in ring:
        yield
    yield
    for copy in shared:
        copy.wait_recv()


def column_fetch(links, own, out, pieces):
    here = links.here
    y, core = here["y"], here["core"]
    y_lo = lax.rem(y, 2)
    rows = out.shape[1] // pieces
    spots = [pl.ds(q * rows, rows) for q in range(pieces)]
    spot, twin = block_of(y, core), block_of(y + 1 - 2 * y_lo, core)
    first, second = block_of(3 - y, core), block_of(2 - y + 2 * y_lo, core)
    across = [links.send(own(y_lo, w), out.at[spot, w], "cross") for w in spots]
    shared = [
        links.send(own(y_lo, pl.ds(0, out.shape[1])), out.at[spot], "core"),
        links.send(own(1 - y_lo, pl.ds(0, out.shape[1])), out.at[twin], "core"),
    ]
    passed = []
    for copy, w in zip(across, spots):
        yield
        copy.wait_recv()
        passed.append(links.send(out.at[first, w], out.at[first, w], "pair"))
        shared.append(links.send(out.at[first, w], out.at[first, w], "core"))
    for copy, w in zip(passed, spots):
        yield
        copy.wait_recv()
        shared.append(links.send(out.at[second, w], out.at[second, w], "core"))
    yield
    for copy in shared:
        copy.wait_recv()


class ColumnSum:
    def __init__(self, links, partial, passed, near, far, done):
        self.links, self.partial, self.done = links, partial, done
        self.passed, self.near, self.far = passed, near, far
        self.copies = {}

    def over(self, y_hi):
        core = self.links.here["core"]
        for y in (2 * y_hi, 2 * y_hi + 1):
            self.copies[y] = self.links.send(
                self.partial.at[block_of(y, 1 - core)], self.passed.at[y], "core"
            )

    def ring(self):
        links, partial, passed, near, far = (
            self.links,
            self.partial,
            self.passed,
            self.near,
            self.far,
        )
        core, me = links.here["core"], links.here["y"]
        before, after, beyond = lax.rem(me + 3, 4), lax.rem(me + 1, 4), lax.rem(me + 2, 4)
        rows = partial.shape[1] // 2

        def mine(p, h):
            return passed.at[p, pl.ds(h * rows, rows)]

        def add(p, h):
            add_rows(mine(p, h), mine(p, h), partial.at[block_of(p, core), pl.ds(h * rows, rows)])

        for y in range(4):
            self.copies[y].wait_recv()
        add(beyond, 0)
        up_far = links.send(mine(beyond, 0), far.at[0], "y", 1)
        add(beyond, 1)
        down_far = links.send(mine(beyond, 1), far.at[1], "y", 3)
        add(after, 1)
        up_one = links.send(mine(after, 1), near.at[0, pl.ds(rows, rows)], "y", 1)
        add(before, 0)
        down_one = links.send(mine(before, 0), near.at[1, pl.ds(0, rows)], "y", 3)
        add(after, 0)
        add(before, 1)
        yield
        up_far.wait_recv()
        add_rows(far.at[0], far.at[0], mine(after, 0))
        up_two = links.send(far.at[0], near.at[0, pl.ds(0, rows)], "y", 1)
        down_far.wait_recv()
        add_rows(far.at[1], far.at[1], mine(before, 1))
        down_two = links.send(far.at[1], near.at[1, pl.ds(rows, rows)], "y", 3)
        for h in range(2):
            add(me, h)
        yield
        up_one.wait_recv()
        down_one.wait_recv()
        up_two.wait_recv()
        down_two.wait_recv()
        total = passed.at[me]

        def body(window):
            self.done(
                window, full(total[window]) + (full(near[0, window]) + full(near[1, window]))
            )

        each(2 * rows, 16, body)


class PairSum:
    def __init__(self, links, partial, passed, cross, pair, done):
        self.links, self.partial, self.done = links, partial, done
        self.passed, self.cross, self.pair = passed, cross, pair
        self.copies = {}

    def over(self, y_hi):
        core = self.links.here["core"]
        for y in (2 * y_hi, 2 * y_hi + 1):
            self.copies[y] = self.links.send(
                self.partial.at[block_of(y, 1 - core)], self.passed.at[y], "core"
            )

    def ring(self):
        links, partial, passed = self.links, self.partial, self.passed
        core, y_hi = links.here["core"], lax.div(links.here["y"], 2)
        rows = partial.shape[1] // 2
        chunks = [(i, pl.ds(h * rows, rows)) for i in range(2) for h in range(2)]
        theirs, ours = 2 - 2 * y_hi, 2 * y_hi
        for y in range(4):
            self.copies[y].wait_recv()

        def add(first, i, w):
            spot = passed.at[first + i, w]
            add_rows(spot, spot, partial.at[block_of(first + i, core), w])

        across = []
        for i, w in chunks:
            add(theirs, i, w)
            across.append(links.send(passed.at[theirs + i, w], self.cross.at[i, w], "cross"))
        for i, w in chunks:
            add(ours, i, w)
        yield
        beside = []
        for copy, (i, w) in zip(across, chunks):
            copy.wait_recv()
            spot = passed.at[ours + i, w]
            add_rows(spot, spot, self.cross.at[i, w])
            beside.append(links.send(spot, self.pair.at[i, w], "pair"))
            yield
        for n, (copy, (i, w)) in enumerate(zip(beside, chunks)):
            copy.wait_recv()

            def body(window, i=i, start=w.start):
                at = pl.ds(pl.multiple_of(start + window.start, 16), 16)
                self.done(i, at, full(passed[ours + i, at]) + full(self.pair[i, at]))

            each(rows, 16, body)
            if n < 3:
                yield


def column_scratch(rows):
    return [
        pltpu.VMEM((4, rows, 2048), LOW),
        pltpu.VMEM((2, rows, 2048), LOW),
        pltpu.VMEM((2, rows // 2, 2048), LOW),
    ]


class ByRows:
    def __init__(self, ref):
        self.ref = ref
        self.sides = [pl.ds(s * ref.shape[3] // 2, ref.shape[3] // 2) for s in range(2)]

    def own(self, own_ref, h, s):
        rows = own_ref.shape[0] // 2
        return [own_ref.at[pl.ds(h * rows, rows), self.sides[s]]]

    def one(self, z, x, h, s):
        rows = self.ref.shape[2] // 2
        return [self.ref.at[z, x, pl.ds(h * rows, rows), self.sides[s]]]

    def of_z(self, z, h, s):
        return [self.ref.at[z, pl.ds(2 * h, 2), :, self.sides[s]]]

    def of_x(self, x, h, s):
        return [self.ref.at[pl.ds(2 * h, 2), x, :, self.sides[s]]]


class ByColumns:
    def __init__(self, ref):
        self.ref = ref
        self.rows = ref.shape[0] // 2

    def own(self, own_ref, h, s):
        rows = self.rows // 2
        return [own_ref.at[pl.ds(s * self.rows + h * rows, rows)]]

    def one(self, z, x, h, s):
        rows = self.rows // 2
        return [self.ref.at[pl.ds(s * self.rows + h * rows, rows), aligned((z * 4 + x) * 128, 128)]]

    def of_z(self, z, h, s):
        return [self.ref.at[pl.ds(s * self.rows, self.rows), aligned(z * 512 + h * 256, 256)]]

    def of_x(self, x, h, s):
        return [
            self.ref.at[pl.ds(s * self.rows, self.rows), aligned((2 * h + k) * 512 + x * 128, 128)]
            for k in range(2)
        ]


def plane_first(links, blocks, own_ref, how):
    z, x = links.here["z"], links.here["x"]
    return side_by_side(
        [
            how(
                links,
                "x",
                lambda h: blocks.own(own_ref, h, 0),
                lambda p, h: blocks.one(z, p, h, 0),
            ),
            how(
                links,
                "z",
                lambda h: blocks.own(own_ref, h, 1),
                lambda p, h: blocks.one(p, x, h, 1),
            ),
        ]
    )


def plane_second(links, blocks, how):
    z, x = links.here["z"], links.here["x"]
    return side_by_side(
        [
            how(
                links, "z", lambda h: blocks.of_z(z, h, 0), lambda p, h: blocks.of_z(p, h, 0)
            ),
            how(
                links, "x", lambda h: blocks.of_x(x, h, 1), lambda p, h: blocks.of_x(p, h, 1)
            ),
        ]
    )


def plane_scratch(rows, width):
    return [
        pltpu.VMEM((2, 2, 4, rows, width), LOW),
        pltpu.VMEM((2, 2, 2, rows, width), LOW),
        pltpu.VMEM((2, 4, rows, width), LOW),
        pltpu.VMEM((2, 2, rows, width), LOW),
        pltpu.VMEM((2, 2, rows // 2, width), LOW),
    ]


def plane_scatter(links, grad, out, near, far, middle, near_two, far_two):
    z, x = links.here["z"], links.here["x"]
    by_rows = len(grad.shape) == 4
    rows, half = middle.shape[2:]

    def block(i, j, s):
        if by_rows:
            return grad.at[i, j, :, pl.ds(s * half, half)]
        return grad.at[pl.ds(s * rows, rows), aligned((i * 4 + j) * 128, 128)]

    def window_of(ref, s):
        if by_rows:
            return ref.at[:, pl.ds(s * half, half)]
        return ref.at[pl.ds(s * rows, rows)]

    def mine(s):
        if s == 0:
            return lambda p, h: [block(2 * h + k, p, 0) for k in range(2)]
        return lambda p, h: [block(p, 2 * h + k, 1) for k in range(2)]

    yield from side_by_side(
        [
            scatter4(
                links,
                axis,
                mine(s),
                [
                    lambda h, s=s, i=i: [near.at[s, i, 2 * h + k] for k in range(2)]
                    for i in range(2)
                ],
                [[far.at[s, i, k] for k in range(2)] for i in range(2)],
            )
            for s, axis in enumerate(("x", "z"))
        ]
    )
    for s in range(2):
        for p in range(4):
            own = block(p, x, 0) if s == 0 else block(z, p, 1)

            def body(window, s=s, p=p, own=own):
                middle[s, p, window] = low(
                    full(own[window])
                    + (full(near[s, 0, p, window]) + full(near[s, 1, p, window]))
                )

            each(rows, 16, body)
    part = rows // 2
    yield from side_by_side(
        [
            scatter4(
                links,
                axis,
                lambda p, h, s=s: middle.at[s, p, pl.ds(h * part, part)],
                [lambda h, s=s, i=i: near_two.at[s, i, pl.ds(h * part, part)] for i in range(2)],
                [far_two.at[s, 0], far_two.at[s, 1]],
            )
            for s, axis in enumerate(("z", "x"))
        ]
    )
    for s, me in enumerate((z, x)):
        into = window_of(out, s)

        def body(window, s=s, me=me, into=into):
            into[window] = low(
                full(middle[s, me, window])
                + (full(near_two[s, 0, window]) + full(near_two[s, 1, window]))
            )

        each(rows, 16, body)


def small_plane(links, own, out):
    z, x = links.here["z"], links.here["x"]
    out[z, x] = own[...]
    copies = [links.send(own, out.at[z, x], "x", step) for step in (1, 2, 3)]
    yield
    for copy in copies:
        copy.wait_recv()
    copies = [links.send(out.at[z], out.at[z], "z", step) for step in (1, 2, 3)]
    yield
    for copy in copies:
        copy.wait_recv()


def small_column(links, own, out):
    core, y = links.here["core"], links.here["y"]
    out[core, y] = own[...]
    copies = [links.send(own, out.at[core, y], "y", step) for step in (1, 2, 3)]
    yield
    for copy in copies:
        copy.wait_recv()
    copy = links.send(out.at[core], out.at[core], "core")
    yield
    copy.wait_recv()


def call(kernel, name, number, copies, kept, outs, out_specs, in_specs, scratch, vmem, operands):
    return pl.pallas_call(
        kernel,
        name=name,
        out_shape=outs,
        in_specs=in_specs,
        out_specs=out_specs,
        scratch_shapes=[
            pltpu.SemaphoreType.DMA((copies,)),
            pltpu.SemaphoreType.DMA((copies,)),
            pltpu.SemaphoreType.DMA((kept,)),
        ]
        + scratch,
        compiler_params=pltpu.CompilerParams(
            collective_id=number, has_side_effects=True, vmem_limit_bytes=vmem * 2**20
        ),
    )(*operands)


def shaped(shape, kind=LOW):
    return jax.ShapeDtypeStruct(shape, kind)


def turn_rows(values, cosine, sine):
    return values * cosine + pltpu.roll(values, HD // 2, 1) * sine


def gain_columns(gains, columns_of):
    for i in range(2):
        columns_of[i] = jnp.broadcast_to(gains[2 + i : 3 + i], (HD, HD)).T
    return columns_of.at[0], columns_of.at[1]


def forward_kernel(
    q_weight,
    k_weight,
    v_weight,
    o_weight,
    gate_weight,
    up_weight,
    down_weight,
    tokens,
    cotangent,
    gains,
    seq,
    waves,
    full_qkv_out,
    full_o_out,
    full_gu,
    full_d,
    unit_out,
    two_all,
    dy_all,
    middle,
    attended_out,
    queries_out,
    keys_out,
    values_out,
    proj_out,
    table_out,
    gains_all,
    starts,
    send_sems,
    recv_sems,
    kept,
    attended,
    queries,
    keys,
    values,
    proj,
    table,
    raw_qkv,
    own_qkv,
    own_o,
    raw_gu,
    own_gu,
    x_both,
    dy_both,
    down_own,
    full_qkv,
    full_o,
    unit_all,
    seq_all,
    partial,
    two_own,
    columns_of,
    *column,
):
    links = Links(send_sems, recv_sems)
    local = Locals(kept)
    here = links.here
    z, x, y, core = here["z"], here["x"], here["y"], here["core"]
    half = lax.rem(y, 2)
    part = lax.div(y, 2) * 2 + core
    spot = block_of(y, core)
    plane = z * 4 + x
    own_rows = x_both.shape[0] // 2
    nq, nkv = own_o.shape[0], keys.shape[1]
    nff = raw_gu.shape[1] // 2

    load_x = local.start(tokens, x_both)
    load_qkv = [
        local.start(q_weight.at[:, aligned(part * nq, nq)], raw_qkv.at[:, pl.ds(0, nq)]),
        local.start(k_weight.at[:, aligned(part * nkv, nkv)], raw_qkv.at[:, pl.ds(nq, nkv)]),
        local.start(v_weight.at[:, aligned(part * nkv, nkv)], raw_qkv.at[:, pl.ds(nq + nkv, nkv)]),
    ]
    load_o = local.start(o_weight.at[aligned(part * nq, nq)], own_o)
    load_gu = [
        local.start(gate_weight.at[:, aligned(part * nff, nff)], raw_gu.at[:, pl.ds(0, nff)]),
        local.start(up_weight.at[:, aligned(part * nff, nff)], raw_gu.at[:, pl.ds(nff, nff)]),
    ]
    load_late = [
        local.start(down_weight.at[aligned(part * nff, nff)], down_own),
        local.start(cotangent, dy_both),
    ]
    gain_one, gain_two = gain_columns(gains, columns_of)
    links.meet(PLANE + COLUMN)
    load_x.wait()

    base = part * 2

    def norm_one(window):
        rows = pl.ds(pl.multiple_of(half * own_rows + window.start, 16), 16)
        value = full(x_both[rows])
        unit_all[spot, window] = low(value * inverse_of(value))

    each(own_rows, 16, norm_one)
    column_one = column_gather(links, unit_all.at[spot], unit_all)
    small = [small_column(links, seq, seq_all), small_plane(links, gains, gains_all)]
    step_all([column_one] + small)
    for copy in load_qkv:
        copy.wait()

    def scale_qkv(window):
        own_qkv[window] = low(full(raw_qkv[window]) * gain_one[window, 0:1])
        full_qkv[z, x, window] = own_qkv[window]

    each(own_rows, 16, scale_qkv)
    blocks_qkv, blocks_o = ByRows(full_qkv), ByColumns(full_o)
    blocks_gu, blocks_d = ByRows(full_gu), ByColumns(full_d)
    first_qkv = plane_first(links, blocks_qkv, own_qkv, straight4)
    step_all([first_qkv])
    load_o.wait()
    first_o = plane_first(links, blocks_o, own_o, straight4)
    keep_o = local.start(own_o, full_o.at[:, aligned(plane * 128, 128)])
    for copy in load_gu + load_late:
        copy.wait()

    def scale_gu(window):
        own_gu[window] = low(full(raw_gu[window]) * gain_two[window, 0:1])

    each(own_rows, 16, scale_gu)
    step_all([first_o])
    first_late = [
        plane_first(links, blocks_gu, own_gu, straight4),
        plane_first(links, blocks_d, down_own, straight4),
    ]
    step_all(first_late)
    keep_gu = local.start(own_gu, full_gu.at[z, x])
    keep_d = local.start(down_own, full_d.at[:, aligned(plane * 128, 128)])
    late = [
        local.start(dy_both.at[pl.ds(i * own_rows, own_rows)], dy_all.at[base + i])
        for i in range(2)
    ]
    together([first_qkv])
    second_qkv = plane_second(links, blocks_qkv, gather4)
    step_all([second_qkv, column_one] + small)
    together(small)

    ids = full(seq_all[...])
    count_0 = jnp.sum((ids < 0.5).astype(WIDE), (0, 1))
    count_01 = jnp.sum((ids < 1.5).astype(WIDE), (0, 1))
    start_1 = jnp.sum(count_0[0:1], 1, keepdims=True)
    start_2 = jnp.sum(count_01[0:1], 1, keepdims=True)
    starts[0:4] = jnp.broadcast_to(start_1, (4, HD))
    starts[4:8] = jnp.broadcast_to(start_2, (4, HD))

    def start_of(index):
        return jnp.where(index < start_1, 0.0, jnp.where(index < start_2, start_1, start_2))

    def tables(i, carry):
        window = aligned(i * 64, 64)
        index = full(lax.broadcasted_iota(jnp.int32, (64, HD), 0) + i * 64)
        angle = (index - start_of(index)) * waves[0:1]
        table[0, window] = jnp.cos(angle)
        table[1, window] = jnp.sin(angle) * waves[1:2]
        return carry

    lax.fori_loop(0, 6, tables, 0)
    step_all([column_one, second_qkv])
    together([first_o])
    keep_o.wait()
    second_o = plane_second(links, blocks_o, gather4)
    step_all([second_o])
    lax.fori_loop(6, 12, tables, 0)
    step_all([column_one, second_qkv])
    lax.fori_loop(12, 16, tables, 0)
    together([second_qkv, column_one])
    step_all([second_o])
    together(first_late)
    keep_gu.wait()
    keep_d.wait()
    second_late = [
        plane_second(links, blocks_gu, gather4),
        plane_second(links, blocks_d, gather4),
    ]
    step_all(second_late)
    column_dy = column_fetch(
        links,
        lambda i, w: dy_both.at[
            pl.ds(pl.multiple_of(i * own_rows + w.start, w.size), w.size)
        ],
        dy_all,
        4,
    )
    step_all([column_dy])
    late += [
        local.start(full_qkv, full_qkv_out),
        local.start(unit_all, unit_out),
    ]

    gain_rows = jnp.sum(gains_all[...], (0, 1))
    q_gain, k_gain = gain_rows[0:1], gain_rows[1:2]

    def project(i, carry):
        window = aligned(i * 256, 256)
        unit = unit_all[pl.ds(2 * i, 2)].reshape(256, unit_all.shape[2])
        weights = full_qkv[...].reshape(16 * own_rows, nq + 2 * nkv)
        out = dot_nn(unit, weights)
        cosine, sine = table[0, window], table[1, window]
        for head in range(3):
            value = out[:, head * HD : (head + 1) * HD]
            proj[head, window] = value
            gain = q_gain if head < 2 else k_gain
            rotated = low(turn_rows(value * inverse_of(value) * gain, cosine, sine))
            if head < 2:
                queries[head, window] = rotated
            else:
                keys[window] = rotated
        values[window] = low(out[:, 3 * HD :])
        return carry

    lax.fori_loop(0, 4, project, 0)
    together([second_o])
    late.append(local.start(full_o, full_o_out))
    step_all([column_dy])

    def turn_done(window, total):
        rows = pl.ds(pl.multiple_of(half * own_rows + window.start, 16), 16)
        value = full(x_both[rows]) + total
        middle[window] = value
        two_own[window] = low(value * inverse_of(value))

    summed = ColumnSum(links, partial, *column, turn_done)
    for i in range(4):
        window = pl.ds(i * 256, 256)
        seen = 256 * (i + 1)
        query = jnp.concatenate([queries[0, window], queries[1, window]], 0)
        scores = dot_nt(query, keys[0:seen]) * SCALE
        row = lax.broadcasted_iota(jnp.int32, (256, 1), 0) + i * 256
        row = full(jnp.concatenate([row, row], 0))
        column_index = full(lax.broadcasted_iota(jnp.int32, (512, seen), 1))
        seen_here = (column_index <= row) & (column_index >= start_of(row))
        scores = jnp.where(seen_here, scores, -jnp.inf)
        power = jnp.exp(scores - jnp.max(scores, -1, keepdims=True))
        probs = power * (1.0 / jnp.sum(power, -1, keepdims=True))
        mixed = low(dot_nn(low(probs), values[0:seen]))
        both = jnp.concatenate([mixed[:256], mixed[256:]], 1)
        attended[window] = both
        partial[2 * i : 2 * i + 2] = low(dot_nn(both, full_o[...])).reshape(
            2, own_rows, partial.shape[2]
        )
        if i % 2:
            summed.over(i // 2)
        if i > 0:
            step_all([column_dy])
    late += [
        local.start(attended, attended_out),
        local.start(queries, queries_out),
        local.start(keys, keys_out),
        local.start(values, values_out),
        local.start(proj, proj_out),
        local.start(table, table_out),
    ]
    ring = summed.ring()
    step_all([ring])
    step_all(second_late)
    step_all([ring])
    together([ring])
    late.append(local.start(two_own, two_all.at[spot]))
    column_two = column_gather(links, two_own, two_all)
    step_all([column_two])
    step_all([column_two])
    together([column_two, column_dy])
    together(second_late)
    for copy in late:
        copy.wait()
    links.drain()


def middle_kernel(
    full_gu,
    full_d,
    two_all,
    dy_all,
    middle,
    mid_all,
    grad_gu_w,
    result,
    sum_d,
    send_sems,
    recv_sems,
    kept,
    gu,
    down,
    two,
    dy,
    product,
    grad_gu,
    partial,
    partial_down,
    grad_d,
    dy_own,
    mid_own,
    *scratch,
):
    column, column_down = scratch[:3], scratch[3:6]
    plane_d = scratch[6:]
    links = Links(send_sems, recv_sems)
    local = Locals(kept)
    here = links.here
    spot = block_of(here["y"], here["core"])
    rows = partial.shape[1] // 2
    width = partial.shape[2]
    nff = product.shape[1]
    windows = [pl.ds(h * rows, rows) for h in range(2)]
    halves = [pl.ds(h * 8 * rows, 8 * rows) for h in range(2)]

    load_gu = local.start(full_gu, gu)
    load_two = [local.start(two_all.at[:, windows[h]], two.at[h]) for h in range(2)]
    load_d = local.start(full_d, down)
    load_dy = [local.start(dy_all.at[:, windows[h]], dy.at[h]) for h in range(2)]
    load_own = local.start(dy_all.at[spot], dy_own)
    links.meet([("x", 1), ("x", 3), ("z", 1), ("z", 3), ("y", 1), ("y", 3), ("core", 0)])

    def loop(first, last, body):
        def one(i, carry):
            body(i)
            return carry

        lax.fori_loop(first, last, one, 0)

    def units(h, first, last):
        def body(j):
            at, after = aligned(j * 256, 256), aligned(nff + j * 256, 256)
            unit = two[h].reshape(8 * rows, width)
            gate = dot_nn(unit, gu[:, :, :, at].reshape(width, 256))
            up = dot_nn(unit, gu[:, :, :, after].reshape(width, 256))
            grad = dot_nt(dy[h].reshape(8 * rows, width), down[at])
            sigmoid = 1.0 / (1.0 + jnp.exp(-gate))
            silu = gate * sigmoid
            product[halves[h], at] = low(silu * up)
            grad_gu[halves[h], at] = low(grad * up * (sigmoid * (1.0 + gate * (1.0 - sigmoid))))
            grad_gu[halves[h], after] = low(grad * silu)

        loop(first, last, body)

    def forward_part(h):
        def body(n):
            at = aligned(n * 512, 512)
            out = low(dot_nn(product[halves[h]], down[:, at]))
            partial_down[:, windows[h], at] = out.reshape(8, rows, 512)

        loop(0, width // 512, body)

    def backward_part(h, first, last):
        def body(n):
            out = low(dot_nt(grad_gu[halves[h]], gu[n].reshape(512, 2 * nff)))
            partial[:, windows[h], aligned(n * 512, 512)] = out.reshape(8, rows, 512)

        loop(first, last, body)

    def here_rows(h, window):
        return pl.ds(pl.multiple_of(h * rows + window.start, 16), 16)

    def done(h):
        def body(window, total):
            at = here_rows(h, window)
            value = middle[at]
            inverse = inverse_of(value)
            value = full(dy_own[at]) + norm_back(total, value * inverse, inverse)
            mid_own[at] = low(value)

        return body

    def done_down(h):
        def body(window, total):
            at = here_rows(h, window)
            result[at] = low(middle[at] + total)

        return body

    def column_sum(source, parts, h, body):
        passed, near, far = parts
        return ColumnSum(
            links,
            source.at[:, windows[h]],
            passed.at[:, windows[h]],
            near.at[:, windows[h]],
            far.at[:, pl.ds(h * rows // 2, rows // 2)],
            body(h),
        )

    sums = [column_sum(partial, column, h, done) for h in range(2)]
    sums_down = [column_sum(partial_down, column_down, h, done_down) for h in range(2)]
    rings = [one.ring() for one in sums]
    rings_down = [one.ring() for one in sums_down]
    gathers = [
        column_gather(links, mid_own.at[windows[h]], mid_all.at[:, windows[h]]) for h in range(2)
    ]
    load_gu.wait()
    load_two[0].wait()
    load_d.wait()
    load_dy[0].wait()
    load_own.wait()
    def down_grad(i):
        at = aligned(i * 256, 256)
        grad_d[at] = low(dot_tn(product[:, at], dy[...].reshape(16 * rows, width)))

    def gate_up_grad(i):
        acts = two[:, :, :, aligned(i * 512, 512)].reshape(16 * rows, 512)
        gu[i] = low(dot_tn(acts, grad_gu[...])).reshape(4, 128, 2 * nff)

    units(0, 0, nff // 256)
    forward_part(0)
    sums_down[0].over(0)
    sums_down[0].over(1)
    load_two[1].wait()
    load_dy[1].wait()
    units(1, 0, 1)
    step_all([rings_down[0]])
    units(1, 1, nff // 256)
    forward_part(1)
    sums_down[1].over(0)
    sums_down[1].over(1)
    step_all([rings_down[0]])
    backward_part(0, 0, 2)
    step_all([rings_down[1]])
    backward_part(0, 2, 4)
    sums[0].over(0)
    sums[0].over(1)
    backward_part(1, 0, 2)
    step_all([rings[0]])
    backward_part(1, 2, 4)
    sums[1].over(0)
    sums[1].over(1)
    together([rings_down[0]])
    loop(0, 1, down_grad)
    step_all([rings[0], rings[1]])
    loop(1, nff // 256, down_grad)
    scatter_d = plane_scatter(links, grad_d, sum_d, *plane_d)
    step_all([scatter_d])
    together([rings[0]])
    step_all([gathers[0]])
    step_all([gathers[0]])
    loop(0, 2, gate_up_grad)
    step_all([rings[1], rings_down[1]])
    loop(2, 4, gate_up_grad)
    keep_w = local.start(gu, grad_gu_w)
    step_all([gathers[0]])
    together([rings[1]])
    step_all([gathers[1]])
    step_all([gathers[1], scatter_d])
    keep_mid = local.start(mid_own, mid_all.at[spot])
    together([rings_down[1]])
    step_all([gathers[0], scatter_d])
    step_all([gathers[1], scatter_d])
    together([gathers[0], gathers[1], scatter_d])
    for copy in (keep_w, keep_mid):
        copy.wait()
    links.drain()


def end_kernel(
    q_weight,
    k_weight,
    v_weight,
    gate_weight,
    up_weight,
    tokens,
    full_qkv,
    full_o,
    unit_all,
    mid_all,
    grad_gu_w,
    attended_in,
    queries_in,
    keys_in,
    values_in,
    proj_in,
    table_in,
    gains_all,
    starts,
    gains,
    result,
    sum_d,
    grad_x,
    out_rows,
    all_qkv,
    all_o,
    all_gu,
    all_d,
    sums_out,
    send_sems,
    recv_sems,
    kept,
    attended,
    queries,
    keys,
    values,
    proj,
    table,
    columns_of,
    weights,
    weight_o,
    unit,
    mid,
    grad_gu,
    grad_o,
    grad_qkv_w,
    raw_qkv,
    raw_gu,
    x_both,
    mid_both,
    grad_att,
    dk,
    dv,
    grad_qkv,
    sum_gu,
    sum_qkv,
    own_o,
    own_gu,
    own_qkv,
    small,
    small_all,
    row,
    row_all,
    turned,
    x_pair,
    *scratch,
):
    passed, cross, pair = scratch[:3]
    plane_gu, plane_o, plane_qkv = scratch[3:8], scratch[8:13], scratch[13:]
    links = Links(send_sems, recv_sems)
    local = Locals(kept)
    here = links.here
    y, core = here["y"], here["core"]
    half = lax.rem(y, 2)
    part = lax.div(y, 2) * 2 + core
    part_other = lax.div(lax.rem(y + 2, 4), 2) * 2 + core
    _, rows, width = x_both.shape
    nq, nkv = own_o.shape[0], keys.shape[1]
    nff = sum_gu.shape[1] // 2

    load_mid = local.start(mid_all, mid)
    load_o = local.start(full_o, weight_o)
    load_gu = local.start(grad_gu_w, grad_gu)
    load_heads = [
        local.start(queries_in, queries),
        local.start(keys_in, keys),
        local.start(values_in, values),
        local.start(proj_in, proj),
        local.start(table_in, table),
        local.start(attended_in, attended),
    ]
    gain_one, gain_two = gain_columns(gains, columns_of)
    loads = [
        local.start(full_qkv, weights),
        local.start(unit_all, unit),
        local.start(tokens.at[pl.ds(0, rows)], x_both.at[0]),
        local.start(tokens.at[pl.ds(rows, rows)], x_both.at[1]),
        local.start(mid_all.at[pl.ds(pl.multiple_of(2 * part, 2), 2)], mid_both),
        local.start(q_weight.at[:, aligned(part * nq, nq)], raw_qkv.at[:, pl.ds(0, nq)]),
        local.start(k_weight.at[:, aligned(part * nkv, nkv)], raw_qkv.at[:, pl.ds(nq, nkv)]),
        local.start(v_weight.at[:, aligned(part * nkv, nkv)], raw_qkv.at[:, pl.ds(nq + nkv, nkv)]),
        local.start(gate_weight.at[:, aligned(part * nff, nff)], raw_gu.at[:, pl.ds(0, nff)]),
        local.start(up_weight.at[:, aligned(part * nff, nff)], raw_gu.at[:, pl.ds(nff, nff)]),
    ]
    links.meet(PLANE + COLUMN)

    def share(own, out):
        across = links.send(own, out.at[part], "y", 2)
        beside = links.send(own, out.at[part], "core")
        keep = local.start(own, out.at[part])
        yield
        across.wait_recv()
        second = links.send(out.at[part_other], out.at[part_other], "core")
        yield
        beside.wait_recv()
        second.wait_recv()
        keep.wait()

    def exchange(own, out):
        copy = links.send(own, out.at[half], "pair")
        keep = local.start(own, out.at[half])
        yield
        copy.wait_recv()
        keep.wait()

    def done_one(i, window, total):
        value = full(x_both[i, window])
        inverse = inverse_of(value)
        back = norm_back(total, value * inverse, inverse)
        x_pair[i, window] = low(full(mid_both[i, window]) + back)

    def scale(into, total, raw, gain, spot):
        def body(window):
            into[window] = low(full(total[window]) * gain[window, 0:1])
            part_sum = jnp.sum(full(total[window]) * full(raw[window]), 1, keepdims=True)
            turned[spot, window] = jnp.broadcast_to(part_sum, (16, HD))

        each(rows, 16, body)

    def attended_grad(i, carry):
        window = aligned(i * 256, 256)
        out = low(dot_nt(mid[pl.ds(2 * i, 2)].reshape(256, width), weight_o[...]))
        grad_att[0, window] = out[:, :HD]
        grad_att[1, window] = out[:, HD:]
        return carry

    def gu_job():
        yield from plane_scatter(links, grad_gu, sum_gu, *plane_gu)
        scale(own_gu, sum_gu, raw_gu, gain_two, 1)
        yield from share(own_gu, all_gu)

    def o_job():
        yield from plane_scatter(links, grad_o, own_o, *plane_o)
        yield from share(own_o, all_o)

    def qkv_job():
        yield from plane_scatter(links, grad_qkv_w, sum_qkv, *plane_qkv)
        scale(own_qkv, sum_qkv, raw_qkv, gain_one, 0)
        yield from share(own_qkv, all_qkv)

    job_gu, job_o, job_qkv = gu_job(), o_job(), qkv_job()
    share_d = share(sum_d, all_d)
    pair_rows = exchange(result, out_rows)
    step_all([pair_rows, share_d])
    load_gu.wait()
    step_all([job_gu])
    load_mid.wait()
    load_o.wait()
    lax.fori_loop(0, 4, attended_grad, 0)
    for copy in load_heads:
        copy.wait()

    gain_rows = jnp.sum(gains_all[...], (0, 1))
    q_gain, k_gain = gain_rows[0:1], gain_rows[1:2]
    start_1, start_2 = starts[0:1, 0:1], starts[4:5, 0:1]
    dk[...] = jnp.zeros_like(dk)
    dv[...] = jnp.zeros_like(dv)
    small[...] = jnp.zeros_like(small)

    def project_back(grad, head, window, gain):
        cosine, sine = table[0, window], table[1, window]
        back = grad * cosine - pltpu.roll(grad, HD // 2, 1) * sine
        value = proj[head, window]
        inverse = inverse_of(value)
        scaled = value * inverse
        spot = 0 if head < 2 else 1
        small[spot : spot + 1] += jnp.sum(back * scaled, 0, keepdims=True)
        return low(norm_back(back * gain, scaled, inverse))

    for i in range(4):
        window = pl.ds(i * 256, 256)
        seen = 256 * (i + 1)
        query = jnp.concatenate([queries[0, window], queries[1, window]], 0)
        grad = jnp.concatenate([grad_att[0, window], grad_att[1, window]], 0)
        key, value = keys[0:seen], values[0:seen]
        scores = dot_nt(key, query) * SCALE
        column = lax.broadcasted_iota(jnp.int32, (1, 256), 1) + i * 256
        column = full(jnp.concatenate([column, column], 1))
        start = jnp.where(
            column < start_1, 0.0, jnp.where(column < start_2, start_1, start_2)
        )
        index = full(lax.broadcasted_iota(jnp.int32, (seen, 512), 0))
        scores = jnp.where((index <= column) & (index >= start), scores, -jnp.inf)
        power = jnp.exp(scores - jnp.max(scores, 0, keepdims=True))
        probs = power * (1.0 / jnp.sum(power, 0, keepdims=True))
        grad_probs = dot_nt(value, grad)
        inner = jnp.sum(probs * grad_probs, 0, keepdims=True)
        grad_scores = low(probs * (grad_probs - inner))
        dv[0:seen] += dot_nn(low(probs), grad)
        dk[0:seen] += dot_nn(grad_scores, query)
        dq = dot_tn(key, grad_scores).T * SCALE
        for head in range(2):
            grad_qkv[window, head * HD : (head + 1) * HD] = project_back(
                dq[head * 256 : (head + 1) * 256], head, window, q_gain
            )
        if i == 3:
            step_all([share_d])

    def keys_back(i, carry):
        window = aligned(i * 256, 256)
        grad_qkv[window, nq : nq + nkv] = project_back(dk[window] * SCALE, 2, window, k_gain)
        grad_qkv[window, nq + nkv :] = low(dv[window])
        return carry

    lax.fori_loop(0, 4, keys_back, 0)
    small_job = small_plane(links, small, small_all)
    step_all([small_job])

    def unit_grad(i, carry):
        out = low(
            dot_nt(
                grad_qkv[aligned(i * 256, 256)], weights[...].reshape(width, nq + 2 * nkv)
            )
        )
        mid[pl.ds(2 * i, 2)] = out.reshape(2, rows, width)
        return carry

    for copy in loads:
        copy.wait()
    sum_one = PairSum(links, mid, passed, cross, pair, done_one)
    grad_o[...] = low(dot_tn(attended[...], mid[...].reshape(8 * rows, width)))
    step_all([job_o])
    lax.fori_loop(0, 2, unit_grad, 0)
    sum_one.over(0)
    lax.fori_loop(2, 4, unit_grad, 0)
    sum_one.over(1)
    step_all([job_gu])
    ring_one = sum_one.ring()
    step_all([ring_one])

    def weight_grad(i, carry):
        at = aligned(i * 512, 512)
        out = dot_tn(unit[:, :, at].reshape(8 * rows, 512), grad_qkv[...])
        grad_qkv_w[i] = low(out).reshape(4, rows, nq + 2 * nkv)
        return carry

    lax.fori_loop(0, 4, weight_grad, 0)
    step_all([job_qkv])
    step_all([ring_one])
    step_all([job_o, small_job])
    step_all([ring_one])
    step_all([job_gu, job_qkv])
    step_all([ring_one])
    step_all([job_o, job_qkv, share_d])
    step_all([ring_one])
    step_all([job_gu, job_o, job_qkv])
    for _ in range(3):
        step_all([ring_one])
    step_all([job_gu, job_o, job_qkv])
    together([small_job])
    row[0:2] = jnp.sum(small_all[:, :, 0:2], (0, 1))
    row[2:3] = turned[0].T[0:1]
    row[3:4] = turned[1].T[0:1]
    row[4:8] = jnp.zeros((4, HD), WIDE)
    row_job = small_column(links, row, row_all)
    step_all([row_job])
    together([ring_one])
    keep_x = local.start(x_pair, grad_x)
    together([row_job, job_o, job_gu, job_qkv, share_d, pair_rows])
    keep_x.wait()
    sums_out[...] = jnp.sum(row_all[...], (0, 1))
    links.drain()


def widen_kernel(
    out_rows,
    grad_x,
    all_qkv,
    all_o,
    all_gu,
    all_d,
    out_final,
    x_final,
    q_final,
    k_final,
    v_final,
    o_final,
    gate_final,
    up_final,
    d_final,
    rows_low,
    x_low,
    qkv_low,
    o_low,
    gu_low,
    d_low,
    x_wide,
    q_wide,
    k_wide,
    v_wide,
    o_wide,
    gate_wide,
    up_wide,
    d_wide,
    kept,
):
    local = Locals(kept)
    halves, rows, _ = x_low.shape
    parts, rows_w = gu_low.shape[:2]
    nff = gu_low.shape[2] // 2
    load_gu = local.start(all_gu, gu_low)
    load_d = local.start(all_d, d_low)
    load_qkv = local.start(all_qkv, qkv_low)
    load_o = local.start(all_o, o_low)
    load_x = local.start(grad_x, x_low)
    load_rows = local.start(out_rows, rows_low)
    nq = q_wide.shape[1] // parts
    nkv = k_wide.shape[1] // parts
    stores = []

    def side_by_side_parts(source, start, size, into, final):
        for c in range(parts):

            def body(window, c=c):
                into[window, c * size : (c + 1) * size] = full(
                    source[c, window, start : start + size]
                )

            each(rows_w, 32, body)
        stores.append(local.start(into, final))

    def stacked(source, into, final, step):
        count, size = source.shape[:2]
        for c in range(count):

            def body(window, c=c):
                into[c, window] = full(source[c, window])

            each(size, step, body)
            stores.append(local.start(into.at[c], final.at[pl.ds(c * size, size)]))

    load_gu.wait()
    side_by_side_parts(gu_low, 0, nff, gate_wide, gate_final)
    side_by_side_parts(gu_low, nff, nff, up_wide, up_final)
    load_d.wait()
    stacked(d_low, d_wide, d_final, 128)
    load_x.wait()
    stacked(x_low, x_wide, x_final, 16)
    load_rows.wait()
    for c in range(halves):
        stores.append(local.start(rows_low.at[c], out_final.at[pl.ds(c * rows, rows)]))
    load_qkv.wait()
    side_by_side_parts(qkv_low, 0, nq, q_wide, q_final)
    side_by_side_parts(qkv_low, nq, nkv, k_wide, k_final)
    side_by_side_parts(qkv_low, nq + nkv, nkv, v_wide, v_final)
    load_o.wait()
    stacked(o_low, o_wide, o_final, 128)
    for copy in stores:
        copy.wait()


def per_device(
    tokens,
    segments,
    attn_gain,
    q_weight,
    k_weight,
    v_weight,
    q_gain,
    k_gain,
    o_weight,
    mlp_gain,
    gate_weight,
    up_weight,
    down_weight,
    cotangent,
):
    parts, halves = lax.axis_size("ctx"), lax.axis_size("tp")
    half = lax.axis_index("tp")
    rows_here, width = tokens.shape
    seq_len = rows_here * parts
    own_rows = rows_here // halves
    blocks = parts * halves

    def own(array):
        return lax.dynamic_slice_in_dim(array, half * own_rows, own_rows, 0)

    rows_w = q_weight.shape[0]
    nq, nkv, nff = q_weight.shape[1] // parts, k_weight.shape[1] // parts, gate_weight.shape[1] // parts
    na, nb = nq + 2 * nkv, 2 * nff
    few = q_gain.shape[0]
    spread = lax.dynamic_update_slice(
        jnp.zeros((2, HD), WIDE),
        full(jnp.stack([q_gain, k_gain])),
        (0, lax.axis_index("fsdp") * few),
    )
    gains = jnp.concatenate(
        [spread, full(attn_gain)[None], full(mlp_gain)[None], jnp.zeros((4, HD), WIDE)], 0
    )
    seq = jnp.broadcast_to(own(segments)[None, :], (8, own_rows))
    index = lax.broadcasted_iota(WIDE, (8, HD), 1)
    row = lax.broadcasted_iota(WIDE, (8, HD), 0)
    lower = index < HD // 2
    frequency = jnp.power(rope_base, -2.0 * jnp.where(lower, index, index - HD // 2) / HD)
    waves = jnp.where(row == 0, frequency, jnp.where(lower, -1.0, 1.0))

    (
        full_qkv,
        full_o,
        full_gu,
        full_d,
        unit_all,
        two_all,
        dy_all,
        middle,
        attended,
        queries,
        keys,
        values,
        proj,
        table,
        gains_all,
        starts,
    ) = call(
        forward_kernel,
        "forward",
        0,
        176,
        24,
        (
            shaped((4, 4, rows_w, na)),
            shaped((nq, width)),
            shaped((4, 4, rows_w, nb)),
            shaped((nff, width)),
            shaped((blocks, own_rows, width)),
            shaped((blocks, own_rows, width)),
            shaped((blocks, own_rows, width)),
            shaped((own_rows, width), WIDE),
            shaped((seq_len, nq)),
            shaped((2, seq_len, HD)),
            shaped((seq_len, HD)),
            shaped((seq_len, HD)),
            shaped((3, seq_len, HD), WIDE),
            shaped((2, seq_len, HD), WIDE),
            shaped((4, 4, 8, HD), WIDE),
            shaped((8, HD), WIDE),
        ),
        [HBM] * 7 + [VMEM] + [HBM] * 6 + [VMEM] * 2,
        [HBM] * 9 + [VMEM] * 3,
        [
            pltpu.VMEM((seq_len, nq), LOW),
            pltpu.VMEM((2, seq_len, HD), LOW),
            pltpu.VMEM((seq_len, HD), LOW),
            pltpu.VMEM((seq_len, HD), LOW),
            pltpu.VMEM((3, seq_len, HD), WIDE),
            pltpu.VMEM((2, seq_len, HD), WIDE),
            pltpu.VMEM((rows_w, na), LOW),
            pltpu.VMEM((rows_w, na), LOW),
            pltpu.VMEM((nq, rows_w), LOW),
            pltpu.VMEM((rows_w, nb), LOW),
            pltpu.VMEM((rows_w, nb), LOW),
            pltpu.VMEM((rows_here, width), LOW),
            pltpu.VMEM((rows_here, width), LOW),
            pltpu.VMEM((nff, rows_w), LOW),
            pltpu.VMEM((4, 4, rows_w, na), LOW),
            pltpu.VMEM((nq, width), LOW),
            pltpu.VMEM((blocks, own_rows, width), LOW),
            pltpu.VMEM((2, 4, 8, own_rows), jnp.int32),
            pltpu.VMEM((blocks, own_rows, width), LOW),
            pltpu.VMEM((own_rows, width), LOW),
            pltpu.VMEM((2, HD, HD), WIDE),
        ]
        + column_scratch(own_rows),
        58,
        (
            q_weight,
            k_weight,
            v_weight,
            o_weight,
            gate_weight,
            up_weight,
            down_weight,
            tokens,
            cotangent,
            gains,
            seq,
            waves,
        ),
    )

    mid_all, grad_gu_w, result, sum_d = call(
        middle_kernel,
        "middle",
        1,
        144,
        12,
        (
            shaped((blocks, own_rows, width)),
            shaped((4, 4, rows_w, nb)),
            shaped((own_rows, width)),
            shaped((nff, rows_w)),
        ),
        [HBM] * 2 + [VMEM] * 2,
        [HBM] * 4 + [VMEM],
        [
            pltpu.VMEM((4, 4, rows_w, nb), LOW),
            pltpu.VMEM((nff, width), LOW),
            pltpu.VMEM((2, blocks, own_rows // 2, width), LOW),
            pltpu.VMEM((2, blocks, own_rows // 2, width), LOW),
            pltpu.VMEM((seq_len, nff), LOW),
            pltpu.VMEM((seq_len, nb), LOW),
            pltpu.VMEM((blocks, own_rows, width), LOW),
            pltpu.VMEM((blocks, own_rows, width), LOW),
            pltpu.VMEM((nff, width), LOW),
            pltpu.VMEM((own_rows, width), LOW),
            pltpu.VMEM((own_rows, width), LOW),
        ]
        + column_scratch(own_rows)
        + column_scratch(own_rows)
        + plane_scratch(nff // 2, rows_w),
        62,
        (full_gu, full_d, two_all, dy_all, middle),
    )

    grad_x, out_rows, all_qkv, all_o, all_gu, all_d, sums = call(
        end_kernel,
        "end",
        2,
        160,
        40,
        (
            shaped((halves, own_rows, width)),
            shaped((halves, own_rows, width)),
            shaped((parts, rows_w, na)),
            shaped((parts, nq, rows_w)),
            shaped((parts, rows_w, nb)),
            shaped((parts, nff, rows_w)),
            shaped((8, HD), WIDE),
        ),
        [HBM] * 6 + [VMEM],
        [HBM] * 17 + [VMEM] * 5,
        [
            pltpu.VMEM((seq_len, nq), LOW),
            pltpu.VMEM((2, seq_len, HD), LOW),
            pltpu.VMEM((seq_len, HD), LOW),
            pltpu.VMEM((seq_len, HD), LOW),
            pltpu.VMEM((3, seq_len, HD), WIDE),
            pltpu.VMEM((2, seq_len, HD), WIDE),
            pltpu.VMEM((2, HD, HD), WIDE),
            pltpu.VMEM((4, 4, rows_w, na), LOW),
            pltpu.VMEM((nq, width), LOW),
            pltpu.VMEM((blocks, own_rows, width), LOW),
            pltpu.VMEM((blocks, own_rows, width), LOW),
            pltpu.VMEM((4, 4, rows_w, nb), LOW),
            pltpu.VMEM((nq, width), LOW),
            pltpu.VMEM((4, 4, rows_w, na), LOW),
            pltpu.VMEM((rows_w, na), LOW),
            pltpu.VMEM((rows_w, nb), LOW),
            pltpu.VMEM((halves, own_rows, width), LOW),
            pltpu.VMEM((halves, own_rows, width), LOW),
            pltpu.VMEM((2, seq_len, HD), LOW),
            pltpu.VMEM((seq_len, HD), WIDE),
            pltpu.VMEM((seq_len, HD), WIDE),
            pltpu.VMEM((seq_len, na), LOW),
            pltpu.VMEM((rows_w, nb), LOW),
            pltpu.VMEM((rows_w, na), LOW),
            pltpu.VMEM((nq, rows_w), LOW),
            pltpu.VMEM((rows_w, nb), LOW),
            pltpu.VMEM((rows_w, na), LOW),
            pltpu.VMEM((8, HD), WIDE),
            pltpu.VMEM((4, 4, 8, HD), WIDE),
            pltpu.VMEM((8, HD), WIDE),
            pltpu.VMEM((2, 4, 8, HD), WIDE),
            pltpu.VMEM((2, rows_w, HD), WIDE),
            pltpu.VMEM((halves, own_rows, width), LOW),
            pltpu.VMEM((4, own_rows, width), LOW),
            pltpu.VMEM((halves, own_rows, width), LOW),
            pltpu.VMEM((halves, own_rows, width), LOW),
        ]
        + plane_scratch(rows_w, nb // 2)
        + plane_scratch(nq // 2, rows_w)
        + plane_scratch(rows_w, na // 2),
        62,
        (
            q_weight,
            k_weight,
            v_weight,
            gate_weight,
            up_weight,
            tokens,
            full_qkv,
            full_o,
            unit_all,
            mid_all,
            grad_gu_w,
            attended,
            queries,
            keys,
            values,
            proj,
            table,
            gains_all,
            starts,
            gains,
            result,
            sum_d,
        ),
    )

    (
        out_final,
        x_final,
        q_final,
        k_final,
        v_final,
        o_final,
        gate_final,
        up_final,
        d_final,
    ) = pl.pallas_call(
        widen_kernel,
        name="widen",
        out_shape=(
            shaped((rows_here, width)),
            shaped((rows_here, width), WIDE),
            shaped(q_weight.shape, WIDE),
            shaped(k_weight.shape, WIDE),
            shaped(v_weight.shape, WIDE),
            shaped(o_weight.shape, WIDE),
            shaped(gate_weight.shape, WIDE),
            shaped(up_weight.shape, WIDE),
            shaped(down_weight.shape, WIDE),
        ),
        in_specs=[HBM] * 6,
        out_specs=[HBM] * 9,
        scratch_shapes=[
            pltpu.VMEM((halves, own_rows, width), LOW),
            pltpu.VMEM((halves, own_rows, width), LOW),
            pltpu.VMEM((parts, rows_w, na), LOW),
            pltpu.VMEM((parts, nq, rows_w), LOW),
            pltpu.VMEM((parts, rows_w, nb), LOW),
            pltpu.VMEM((parts, nff, rows_w), LOW),
            pltpu.VMEM((halves, own_rows, width), WIDE),
            pltpu.VMEM(q_weight.shape, WIDE),
            pltpu.VMEM(k_weight.shape, WIDE),
            pltpu.VMEM(v_weight.shape, WIDE),
            pltpu.VMEM((parts, nq, rows_w), WIDE),
            pltpu.VMEM(gate_weight.shape, WIDE),
            pltpu.VMEM(up_weight.shape, WIDE),
            pltpu.VMEM((parts, nff, rows_w), WIDE),
            pltpu.SemaphoreType.DMA((40,)),
        ],
        compiler_params=pltpu.CompilerParams(vmem_limit_bytes=60 * 2**20),
    )(out_rows, grad_x, all_qkv, all_o, all_gu, all_d)
    sum_qk = lax.dynamic_slice_in_dim(sums[:2], lax.axis_index("fsdp") * few, few, 1)
    return (
        out_final,
        x_final,
        sums[2],
        q_final,
        k_final,
        v_final,
        sum_qk[0],
        sum_qk[1],
        o_final,
        sums[3],
        gate_final,
        up_final,
        d_final,
    )


def solution(mesh):
    weight = P("fsdp", "tp")
    turned = P("tp", "fsdp")
    acts = P(("fsdp", "ctx"), None)
    gain = P("fsdp")
    return jax.shard_map(
        per_device,
        mesh=mesh,
        in_specs=(
            acts,
            P(("fsdp", "ctx")),
            gain,
            weight,
            weight,
            weight,
            gain,
            gain,
            turned,
            gain,
            weight,
            weight,
            turned,
            acts,
        ),
        out_specs=(
            acts,
            acts,
            gain,
            weight,
            weight,
            weight,
            gain,
            gain,
            turned,
            gain,
            weight,
            weight,
            turned,
        ),
        check_vma=False,
    )
```
